32 devices in a mesh: groups: 2 (over x), ctx: 8 (over z, y), head: 2 (over core).
Axes of the slice: x: 2, y: 2, z: 4, core: 2. Of those that a mesh axis runs over, the one named last changes fastest.
Arguments:
- queries: bfloat16 [1024, 128, 576], P(('groups', 'ctx'), 'head'), parts along dimension 0, may hold values from -10 to 10
- latent_cache: bfloat16 [65536, 576], P(('groups', 'ctx')), parts along dimension 0, may hold values from -8.5 to 8.5
- positions: int32 [1024], P(('groups', 'ctx')), parts along dimension 0, may hold values from 32256 to 32767, as said below
- block_ids: int32 [16, 32], P(('groups', 'ctx')), parts along dimension 0, may hold values from 0 to 511, as said below
Outputs:
- attn_latent: bfloat16 [1024, 128, 512], P(('groups', 'ctx'), 'head'), parts along dimension 0
The draws below stay inside these ranges and needn't reach their ends.
There are 2 independent parts, one for each index of `groups`. The reference program is written for one: setup_inputs(seed, part) draws one part's arguments, and reference() takes and returns one part's arrays. A program takes and returns all parts, laid end to end along the dimension named above; each array names one. Nothing has to cross between parts.
Inputs may be any that keep to these rules, and one draw needn't show every extreme that they name: Rows c*64 to c*64 + 63 hold consecutive positions inside one key block; the 8 query blocks lie in the last 8 key blocks of the cache, one in each. `block_ids`: row c holds 32 different key blocks: the block that holds query block c's positions, which is the only one from its shard of 64 blocks, and otherwise blocks of earlier shards. In each row at most 8 blocks lie in one shard, and exactly 8 in some shard.
All inputs are finite; a program needn't handle non-finite values.
Results may differ from the reference program's by a relative error of at most 0.0034.
Values may be sent and summed in bfloat16 or wider, within the bound.
No kernel may reach another device: no remote copies, remote signals or barrier semaphores. Data moves between devices by JAX's collectives and lax.ppermute only.
A program may use at most 128 MiB of HBM per device.

```python
import jax
import jax.numpy as jnp
from jax import lax

HEADS = 128
KVL = 512
LAT = 576
BLOCK = 64
SEL = 32
Q_DEV = 64
BLK_DEV = 64
QBLOCKS = 8
QROWS = 512
NBLK = 512
CTXLEN = 32768
CAP = 8


def window_layout(key):
    order_key = jax.random.fold_in(key, 101)
    offset_key = jax.random.fold_in(key, 102)
    diag_block = NBLK - QBLOCKS + jax.random.permutation(order_key, QBLOCKS)
    row_offset = jax.random.randint(offset_key, (QBLOCKS,), 0, BLOCK - Q_DEV + 1)
    row_offset = jnp.where(diag_block == NBLK - QBLOCKS, 0, row_offset)
    row_offset = jnp.where(diag_block == NBLK - 1, BLOCK - Q_DEV, row_offset)
    return (diag_block.astype(jnp.int32), row_offset.astype(jnp.int32))


def draw_positions(key, part):
    diag_block, row_offset = window_layout(key)
    starts = diag_block * BLOCK + row_offset
    return (starts[:, None] + jnp.arange(Q_DEV, dtype=jnp.int32)[None, :]).reshape(QROWS).astype(jnp.int32)


def draw_block_ids(key, part):
    diag_block, row_offset = window_layout(key)
    key = jax.random.fold_in(key, 2)
    subkeys = jax.random.split(key, 6)
    full_shards = diag_block // BLK_DEV
    first_pick = jax.random.randint(subkeys[0], (QBLOCKS,), 0, 1 << 20) % full_shards
    second_pick = jax.random.randint(subkeys[1], (QBLOCKS,), 0, 1 << 20) % full_shards
    hot_shard = first_pick * second_pick // full_shards
    stride = BLK_DEV // CAP
    hot_start = jax.random.randint(subkeys[2], (QBLOCKS,), 0, BLK_DEV)
    steps_hot = jnp.arange(CAP, dtype=jnp.int32) * stride
    hot_blocks = hot_shard[:, None] * BLK_DEV + (hot_start[:, None] + steps_hot[None, :]) % BLK_DEV
    entries = jnp.arange(QBLOCKS * CAP, dtype=jnp.int32)
    entry_shard = entries // CAP
    usable = (entry_shard[None, :] < full_shards[:, None]) & (entry_shard[None, :] != hot_shard[:, None])
    ranking = jax.random.randint(subkeys[3], (QBLOCKS, QBLOCKS * CAP), 0, 1 << 16) * (QBLOCKS * CAP) + entries[None, :]
    ranking = jnp.where(usable, ranking, ranking + (1 << 30))
    picked = jnp.argsort(ranking, axis=1, stable=True)[:, :SEL - 1 - CAP].astype(jnp.int32)
    picked_shard = picked // CAP
    picked_rank = picked % CAP
    shard_start = jax.random.randint(subkeys[4], (QBLOCKS, QBLOCKS), 0, BLK_DEV)
    picked_start = jnp.take_along_axis(shard_start, picked_shard, axis=1)
    other_blocks = picked_shard * BLK_DEV + (picked_start + picked_rank * stride) % BLK_DEV
    block_lists = jnp.concatenate([diag_block[:, None], hot_blocks, other_blocks], axis=1).astype(jnp.int32)
    shuffle_keys = jax.random.randint(subkeys[5], (QBLOCKS, SEL), 0, 1 << 16) * SEL + jnp.arange(SEL, dtype=jnp.int32)[None, :]
    shuffle = jnp.argsort(shuffle_keys, axis=1, stable=True)
    return jnp.take_along_axis(block_lists, shuffle, axis=1).astype(jnp.int32)


def draw_latent_cache(key, part):
    key = jax.random.fold_in(key, 3)
    subkeys = jax.random.split(key, 1)
    cache_rows = jnp.clip(jax.random.normal(subkeys[0], (CTXLEN, LAT)), -6.0, 6.0)
    return cache_rows.astype(jnp.bfloat16)


def draw_queries(key, part):
    key = jax.random.fold_in(key, 4)
    subkeys = jax.random.split(key, 1)
    values = 1.25 * jnp.clip(jax.random.normal(subkeys[0], (QROWS, HEADS, LAT)), -6.0, 6.0)
    return values.astype(jnp.bfloat16)


def setup_inputs(seed: int = 0, part: int = 0) -> dict:
    streams_of = jax.random.split(jax.random.key(seed), 5)
    part_splits = jax.random.split(jax.random.fold_in(streams_of[4], part), 5)
    return {
        "queries": draw_queries(jax.random.fold_in(jax.random.fold_in(streams_of[4], part), 71), part),
        "latent_cache": draw_latent_cache(jax.random.fold_in(jax.random.fold_in(streams_of[4], part), 71), part),
        "positions": draw_positions(jax.random.fold_in(jax.random.fold_in(streams_of[4], part), 71), part),
        "block_ids": draw_block_ids(jax.random.fold_in(jax.random.fold_in(streams_of[4], part), 71), part),
    }


softmax_scale = 1.0 / (192.0 ** 0.5)


def attend(query_rows, query_pos, key_rows, key_pos):
    scores = jnp.einsum("qhl,kl->qhk", query_rows.astype(jnp.float32), key_rows.astype(jnp.float32)) * softmax_scale
    visible = key_pos[None, :] <= query_pos[:, None]
    scores = jnp.where(visible[:, None, :], scores, -jnp.inf)
    row_max = jnp.max(scores, axis=-1, keepdims=True)
    weights = jnp.exp(scores - row_max)
    denominator = jnp.sum(weights, axis=-1, keepdims=True)
    rounded = lax.optimization_barrier(weights.astype(jnp.bfloat16))
    combined = jnp.einsum("qhk,kv->qhv", rounded.astype(jnp.float32), key_rows[:, :KVL].astype(jnp.float32))
    return (combined / denominator).astype(jnp.bfloat16)


def reference(queries, latent_cache, positions, block_ids):
    cache_blocks = latent_cache.reshape(NBLK, BLOCK, LAT)
    query_blocks = queries.reshape(QBLOCKS, Q_DEV, HEADS, LAT)
    block_pos = positions.reshape(QBLOCKS, Q_DEV)
    offsets = jnp.arange(BLOCK, dtype=jnp.int32)

    def one_block(block_args):
        query_rows, query_pos, chosen = block_args
        key_rows = cache_blocks[chosen].reshape(SEL * BLOCK, LAT)
        key_pos = (chosen[:, None] * BLOCK + offsets[None, :]).reshape(SEL * BLOCK)
        return attend(query_rows, query_pos, key_rows, key_pos)

    result = lax.map(one_block, (query_blocks, block_pos, block_ids))
    return result.reshape(QROWS, HEADS, KVL)
```

```python
import functools

import jax
import jax.numpy as jnp
from jax import lax
from jax.experimental import pallas as pl
from jax.experimental.pallas import tpu as pltpu
from jax.sharding import PartitionSpec as P

KVL = 512
BLOCK = 64
SEL = 32
PAIR = 2 * BLOCK
TILE = 256
NEG = -1e30
SCALE = 1.4426950408889634 / 192.0**0.5
NT = (((1,), (1,)), ((), ()))
NN = (((1,), (0,)), ((), ()))


def pack_kernel(capacity, ids, cache, *refs):
    chunks = capacity // 2
    outs, (table, rows, sem) = refs[:chunks], refs[chunks:]
    half, tokens = rows.shape
    shard_blocks = tokens // BLOCK
    dests = ids.shape[0]
    head = lax.axis_index("head")
    base = lax.axis_index("ctx") * shard_blocks
    copy = pltpu.make_async_copy(cache.at[pl.ds(pl.multiple_of(head * half, 32), half), :], rows, sem)
    copy.start()

    @pl.loop(0, dests)
    def _(d):
        first = d * (capacity + 1)
        for slot in range(capacity + 1):
            table[first + slot] = 0
        count = jnp.int32(0)
        for j in range(SEL):
            place = ids[d, j] - base
            mine = jnp.logical_and(place >= 0, place < shard_blocks)
            table[first + jnp.minimum(count, capacity)] = jnp.clip(place, 0, shard_blocks - 1)
            count = count + mine.astype(jnp.int32)

    copy.wait()
    left = lax.broadcasted_iota(jnp.int32, (half, PAIR), 1) < BLOCK

    def block_pair(d, chunk):
        first = d * (capacity + 1) + 2 * chunk
        a, b = table[first], table[first + 1]
        xa = rows[:, pl.ds(pl.multiple_of((a // 2) * PAIR, PAIR), PAIR)].astype(jnp.float32)
        xb = rows[:, pl.ds(pl.multiple_of((b // 2) * PAIR, PAIR), PAIR)].astype(jnp.float32)
        xa = pltpu.roll(xa, (a % 2) * BLOCK, 1)
        xb = pltpu.roll(xb, (1 - b % 2) * BLOCK, 1)
        return jnp.where(left, xa, xb).astype(jnp.bfloat16)

    for chunk in range(chunks):
        @pl.loop(0, dests)
        def _(d):
            outs[chunk][d] = block_pair(d, chunk)


def pack(all_ids, cache_t, capacity):
    dests = all_ids.shape[0]
    lat, tokens = cache_t.shape
    half = lat // 2
    chunks = capacity // 2
    return pl.pallas_call(
        functools.partial(pack_kernel, capacity),
        out_shape=[jax.ShapeDtypeStruct((dests, half, PAIR), jnp.bfloat16)] * chunks,
        grid_spec=pltpu.PrefetchScalarGridSpec(
            num_scalar_prefetch=1,
            grid=(1,),
            in_specs=[pl.BlockSpec(memory_space=pl.ANY)],
            out_specs=[pl.BlockSpec((dests, half, PAIR), lambda i, ids: (0, 0, 0))] * chunks,
            scratch_shapes=[
                pltpu.SMEM((dests * (capacity + 1),), jnp.int32),
                pltpu.VMEM((half, tokens), jnp.bfloat16),
                pltpu.SemaphoreType.DMA,
            ],
        ),
        compiler_params=pltpu.CompilerParams(vmem_limit_bytes=40 << 20),
        name="pack",
    )(all_ids, cache_t)


def slot_starts(ids, starts, owners, capacity, shard_blocks):
    for slot in range(owners * capacity):
        starts[slot] = -1
    for o in range(owners):
        starts[owners * capacity + o] = 0
    for j in range(SEL):
        block = ids[j]
        owner = block // shard_blocks
        rank = jnp.minimum(starts[owners * capacity + owner], capacity - 1)
        starts[owner * capacity + rank] = block * BLOCK
        starts[owners * capacity + owner] = rank + 1


def unpack_pair(kt, kr, at, mine, other, head, half, eye):
    kt[pl.ds(pl.multiple_of(head * half, 32), half), pl.ds(at, PAIR)] = mine
    kt[pl.ds(pl.multiple_of((1 - head) * half, 32), half), pl.ds(at, PAIR)] = other
    both = kt[:, pl.ds(at, PAIR)]
    kr[pl.ds(at, PAIR), :] = lax.dot_general(eye, both, NT, preferred_element_type=jnp.float32).astype(jnp.bfloat16)


def identity():
    row = lax.broadcasted_iota(jnp.int32, (PAIR, PAIR), 0)
    col = lax.broadcasted_iota(jnp.int32, (PAIR, PAIR), 1)
    return jnp.where(row == col, 1.0, 0.0).astype(jnp.bfloat16)


def pair_bias(bias, at, start_a, start_b):
    for k, start in enumerate((start_a, start_b)):
        value = jnp.where(start >= 0, 0.0, NEG).astype(jnp.float32)
        bias[pl.ds(at + k * BLOCK, BLOCK), :] = jnp.full((BLOCK, PAIR), value, jnp.float32)


def fold(x, op):
    return op(x.reshape(x.shape[0] // 8, 8, x.shape[1]), axis=0)


def turn(x):
    return jnp.transpose(x, (1, 0))


def first_kernel(capacity, shard_blocks, chunks, final, ids, q, pos, *refs):
    mine, other = refs[:chunks], refs[chunks : 2 * chunks]
    outs = refs[2 * chunks : 2 * chunks + (1 if final else 2)]
    starts, kt, kr, bias, scores, weights = refs[2 * chunks + len(outs) :]
    owners, half, _ = mine[0].shape
    head = lax.axis_index("head")
    keys = owners * chunks * PAIR

    @pl.when(pl.program_id(0) == 0)
    def _():
        slot_starts(ids, starts, owners, capacity, shard_blocks)
        eye = identity()
        for c in range(chunks):
            @pl.loop(0, owners)
            def _(o):
                at = pl.multiple_of((c * owners + o) * PAIR, PAIR)
                unpack_pair(kt, kr, at, mine[c][o], other[c][o], head, half, eye)
                slot = o * capacity + 2 * c
                pair_bias(bias, at, starts[slot], starts[slot + 1])

    scores[...] = lax.dot_general(kr[...], q[...], NT, preferred_element_type=jnp.float32)
    high = jnp.full((8, TILE), NEG, jnp.float32)
    diagonal = (owners - 1) * PAIR
    step = PAIR
    for at in range(0, keys, step):
        part = scores[at : at + step, :] * SCALE
        add = bias[at : at + step, :]
        part = part + jnp.concatenate([add, add], axis=1)
        if at == diagonal:
            key = starts[(owners - 1) * capacity] + lax.broadcasted_iota(jnp.int32, (BLOCK, TILE), 0)
            seen = jnp.where(key <= pos[0:1, :], part[:BLOCK], NEG)
            part = jnp.concatenate([seen, part[BLOCK:]], axis=0)
        scores[at : at + step, :] = part
        high = jnp.maximum(high, fold(part, jnp.max))
    top = jnp.max(high, axis=0, keepdims=True)
    total = jnp.zeros((8, TILE), jnp.float32)
    for at in range(0, keys, step):
        part = jnp.exp2(scores[at : at + step, :] - top)
        total = total + fold(part, jnp.sum)
        weights[at : at + step, :] = part.astype(jnp.bfloat16)
    low = jnp.sum(total, axis=0, keepdims=True)
    summed = lax.dot_general(kt[:KVL, :], weights[...], NN, preferred_element_type=jnp.float32)
    if final:
        outs[0][...] = turn(summed * (1.0 / low)).astype(jnp.bfloat16)
    else:
        outs[0][...] = summed
        outs[1][0:1, :] = top
        outs[1][1:2, :] = low


def rest_kernel(capacity, shard_blocks, chunks, skip, ids, q, carry, stats, *refs):
    mine, other = refs[:chunks], refs[chunks : 2 * chunks]
    out, starts, kt, kr, bias, total, acc, state = refs[2 * chunks :]
    owners, half, _ = mine[0].shape
    head = lax.axis_index("head")
    live = owners * capacity + owners

    @pl.when(pl.program_id(0) == 0)
    def _():
        slot_starts(ids, starts, owners, capacity, shard_blocks)
        eye = identity()
        starts[live] = 0
        for c in range(chunks):
            @pl.loop(0, owners - 1)
            def _(o):
                slot = o * capacity + 2 * (skip + c)
                @pl.when(starts[slot] >= 0)
                def _():
                    count = starts[live]
                    at = pl.multiple_of(count * PAIR, PAIR)
                    unpack_pair(kt, kr, at, mine[c][o], other[c][o], head, half, eye)
                    pair_bias(bias, at, starts[slot], starts[slot + 1])
                    starts[live] = count + 1
        count = starts[live]
        @pl.when(count % 2 == 1)
        def _():
            at = pl.multiple_of(count * PAIR, PAIR)
            kt[:, pl.ds(at, PAIR)] = jnp.zeros((kt.shape[0], PAIR), jnp.bfloat16)
            kr[pl.ds(at, PAIR), :] = jnp.zeros((PAIR, kr.shape[1]), jnp.bfloat16)
            pair_bias(bias, at, -1, -1)

    acc[...] = carry[...]
    state[0:1, :] = stats[0:1, :]
    state[1:2, :] = stats[1:2, :]

    @pl.loop(0, (starts[live] + 1) // 2)
    def _(g):
        at = pl.multiple_of(g * TILE, TILE)
        part = lax.dot_general(kr[pl.ds(at, TILE), :], q[...], NT, preferred_element_type=jnp.float32)
        add = bias[pl.ds(at, TILE), :]
        part = part * SCALE + jnp.concatenate([add, add], axis=1)
        old = state[0:1, :]
        top = jnp.maximum(old, jnp.max(fold(part, jnp.max), axis=0, keepdims=True))
        shrink = jnp.exp2(old - top)
        part = jnp.exp2(part - top)
        state[0:1, :] = top
        state[1:2, :] = state[1:2, :] * shrink + jnp.sum(fold(part, jnp.sum), axis=0, keepdims=True)
        more = lax.dot_general(
            kt[:KVL, pl.ds(at, TILE)], part.astype(jnp.bfloat16), NN, preferred_element_type=jnp.float32
        )
        acc[...] = acc[...] * shrink + more

    out[...] = turn(acc[...] * (1.0 / state[1:2, :])).astype(jnp.bfloat16)


def whole(x):
    return pl.BlockSpec(x.shape, lambda i, ids: (0,) * x.ndim)


def attend_first(ids, q, pos, mine, other, capacity, shard_blocks, final):
    rows, lat = q.shape
    owners = mine[0].shape[0]
    chunks = len(mine)
    keys = owners * chunks * PAIR
    if final:
        out_shape = [jax.ShapeDtypeStruct((rows, KVL), jnp.bfloat16)]
        out_specs = [pl.BlockSpec((TILE, KVL), lambda i, ids: (i, 0))]
    else:
        out_shape = [jax.ShapeDtypeStruct((KVL, rows), jnp.float32), jax.ShapeDtypeStruct((8, rows), jnp.float32)]
        out_specs = [
            pl.BlockSpec((KVL, TILE), lambda i, ids: (0, i)),
            pl.BlockSpec((8, TILE), lambda i, ids: (0, i)),
        ]
    return pl.pallas_call(
        functools.partial(first_kernel, capacity, shard_blocks, chunks, final),
        out_shape=out_shape,
        grid_spec=pltpu.PrefetchScalarGridSpec(
            num_scalar_prefetch=1,
            grid=(rows // TILE,),
            in_specs=[
                pl.BlockSpec((TILE, lat), lambda i, ids: (i, 0)),
                pl.BlockSpec((8, TILE), lambda i, ids: (0, i)),
            ]
            + [whole(x) for x in (*mine, *other)],
            out_specs=out_specs,
            scratch_shapes=[
                pltpu.SMEM((owners * capacity + owners,), jnp.int32),
                pltpu.VMEM((lat, keys), jnp.bfloat16),
                pltpu.VMEM((keys, lat), jnp.bfloat16),
                pltpu.VMEM((keys, PAIR), jnp.float32),
                pltpu.VMEM((keys, TILE), jnp.float32),
                pltpu.VMEM((keys, TILE), jnp.bfloat16),
            ],
        ),
        compiler_params=pltpu.CompilerParams(vmem_limit_bytes=48 << 20),
        cost_estimate=pl.CostEstimate(
            flops=2 * rows * keys * (lat + KVL), bytes_accessed=rows * (lat + 2 * KVL) * 2, transcendentals=rows * keys
        ),
        name="attend_first",
    )(ids, q, pos, *mine, *other)


def attend_rest(ids, q, carry, stats, mine, other, capacity, shard_blocks, skip):
    rows, lat = q.shape
    owners = mine[0].shape[0]
    chunks = len(mine)
    keys = owners * chunks * PAIR
    return pl.pallas_call(
        functools.partial(rest_kernel, capacity, shard_blocks, chunks, skip),
        out_shape=jax.ShapeDtypeStruct((rows, KVL), jnp.bfloat16),
        grid_spec=pltpu.PrefetchScalarGridSpec(
            num_scalar_prefetch=1,
            grid=(rows // TILE,),
            in_specs=[
                pl.BlockSpec((TILE, lat), lambda i, ids: (i, 0)),
                pl.BlockSpec((KVL, TILE), lambda i, ids: (0, i)),
                pl.BlockSpec((8, TILE), lambda i, ids: (0, i)),
            ]
            + [whole(x) for x in (*mine, *other)],
            out_specs=pl.BlockSpec((TILE, KVL), lambda i, ids: (i, 0)),
            scratch_shapes=[
                pltpu.SMEM((owners * capacity + owners + 1,), jnp.int32),
                pltpu.VMEM((lat, keys), jnp.bfloat16),
                pltpu.VMEM((keys, lat), jnp.bfloat16),
                pltpu.VMEM((keys, PAIR), jnp.float32),
                pltpu.VMEM((keys, TILE), jnp.float32),
                pltpu.VMEM((KVL, TILE), jnp.float32),
                pltpu.VMEM((8, TILE), jnp.float32),
            ],
        ),
        compiler_params=pltpu.CompilerParams(vmem_limit_bytes=48 << 20),
        cost_estimate=pl.CostEstimate(
            flops=rows * keys * (lat + KVL), bytes_accessed=rows * (lat + 3 * KVL) * 2, transcendentals=rows * keys // 2
        ),
        name="attend_rest",
    )(ids, q, carry, stats, *mine, *other)


def local(queries, latent_cache, positions, block_ids):
    owners = lax.axis_size("ctx")
    capacity = max(2, 2 * SEL // owners)
    shard_blocks = latent_cache.shape[0] // BLOCK
    q_rows, heads, lat = queries.shape
    rows = q_rows * heads
    cache_t = latent_cache.T
    all_ids = lax.all_to_all(
        jnp.broadcast_to(block_ids, (owners, SEL)), "ctx", split_axis=0, concat_axis=0, tiled=True
    )
    packed = pack(all_ids, cache_t, capacity)
    mine, other = [], []
    for part in packed:
        got = lax.all_to_all(part, "ctx", split_axis=0, concat_axis=0, tiled=True)
        mine.append(got)
        other.append(lax.ppermute(got, "head", [(0, 1), (1, 0)]))
    q = queries.reshape(rows, lat)
    pos = jnp.broadcast_to(jnp.repeat(positions, heads)[None, :], (8, rows))
    ids = block_ids[0]
    cut = (len(packed) + 1) // 2
    final = cut == len(packed)
    first = attend_first(ids, q, pos, mine[:cut], other[:cut], capacity, shard_blocks, final)
    if final:
        out = first[0]
    else:
        out = attend_rest(ids, q, *first, mine[cut:], other[cut:], capacity, shard_blocks, cut)
    return out.reshape(q_rows, heads, KVL)


def solution(mesh):
    return jax.shard_map(
        local,
        mesh=mesh,
        in_specs=(
            P(("groups", "ctx"), "head", None),
            P(("groups", "ctx"), None),
            P(("groups", "ctx")),
            P(("groups", "ctx"), None),
        ),
        out_specs=P(("groups", "ctx"), "head", None),
        check_vma=False,
    )
```

```python
import functools

import jax
import jax.numpy as jnp
from jax import lax
from jax.experimental import pallas as pl
from jax.experimental.pallas import tpu as pltpu
from jax.sharding import PartitionSpec as P

KVL = 512
BLOCK = 64
SEL = 32
PAIR = 2 * BLOCK
GROUP = 2 * PAIR
SUB = 512
STEP = 2 * SUB
NEG = -1e30
SCALE = 1.4426950408889634 / 192.0**0.5
NT = (((1,), (1,)), ((), ()))
NN = (((1,), (0,)), ((), ()))


def log2(n):
    shift = n.bit_length() - 1
    assert 1 << shift == n
    return shift


def pack_kernel(capacity, phases, ids, cache, *refs):
    dests = ids.shape[0]
    count_out = len(phases) * (dests + 1)
    outs = [refs[p * (dests + 1) : (p + 1) * (dests + 1)] for p in range(len(phases))]
    table, rows, sems = refs[count_out:]
    _, half, tokens = rows.shape
    shift = log2(tokens // BLOCK)
    head = lax.axis_index("head")
    me = lax.axis_index("ctx")
    copies = []
    for i, start in enumerate((head, 1 - head)):
        from_rows = pl.ds(pl.multiple_of(start * half, 32), half)
        copies.append(pltpu.make_async_copy(cache.at[from_rows, :], rows.at[i], sems.at[i]))
        copies[i].start()

    @pl.loop(0, dests)
    def _(d):
        first = d * (capacity + 1)
        for slot in range(capacity + 1):
            table[first + slot] = 0
        at = first
        for j in range(SEL):
            block = ids[d, j]
            table[at] = block & ((1 << shift) - 1)
            at = at + (block >> shift == me).astype(jnp.int32)
        table[at] = 0

    left = lax.broadcasted_iota(jnp.int32, (half, PAIR), 1) < BLOCK

    def block_pair(part, d, chunk):
        first = d * (capacity + 1) + 2 * chunk
        a, b = table[first], table[first + 1]
        xa = rows[part, :, pl.ds(pl.multiple_of((a >> 1) * PAIR, PAIR), PAIR)].astype(jnp.float32)
        xb = rows[part, :, pl.ds(pl.multiple_of((b >> 1) * PAIR, PAIR), PAIR)].astype(jnp.float32)
        xa = pltpu.roll(xa, (a & 1) * BLOCK, 1)
        xb = pltpu.roll(xb, (1 - (b & 1)) * BLOCK, 1)
        return jnp.where(left, xa, xb).astype(jnp.bfloat16)

    copies[0].wait()
    for p, chunks in enumerate(phases):
        for c, chunk in enumerate(chunks):
            for k in range(dests):
                outs[p][k][c] = block_pair(0, me ^ k, chunk)
    copies[1].wait()
    for p, chunks in enumerate(phases):
        for c, chunk in enumerate(chunks):
            outs[p][dests][c] = block_pair(1, me, chunk)


def pack(all_ids, cache_t, capacity, phases):
    dests = all_ids.shape[0]
    lat, tokens = cache_t.shape
    half = lat // 2
    shapes = [(len(chunks), half, PAIR) for chunks in phases for _ in range(dests + 1)]
    return pl.pallas_call(
        functools.partial(pack_kernel, capacity, phases),
        out_shape=[jax.ShapeDtypeStruct(s, jnp.bfloat16) for s in shapes],
        grid_spec=pltpu.PrefetchScalarGridSpec(
            num_scalar_prefetch=1,
            grid=(1,),
            in_specs=[pl.BlockSpec(memory_space=pltpu.HBM)],
            out_specs=[pl.BlockSpec(s, lambda i, ids: (0, 0, 0)) for s in shapes],
            scratch_shapes=[
                pltpu.SMEM((dests * (capacity + 1),), jnp.int32),
                pltpu.VMEM((2, half, tokens), jnp.bfloat16),
                pltpu.SemaphoreType.DMA((2,)),
            ],
        ),
        compiler_params=pltpu.CompilerParams(vmem_limit_bytes=40 << 20),
        name="pack",
    )(all_ids, cache_t)


def slot_starts(ids, starts, owners, capacity, shift):
    for slot in range(owners * capacity):
        starts[slot] = -1
    for o in range(owners):
        starts[owners * capacity + o] = 0
    for j in range(SEL):
        block = ids[j]
        owner = block >> shift
        rank = starts[owners * capacity + owner]
        starts[owner * capacity + rank] = block * BLOCK
        starts[owners * capacity + owner] = rank + 1


def pair_copies(source, kt, at, head, half, sems):
    return [
        pltpu.make_async_copy(
            source[i], kt.at[pl.ds(pl.multiple_of(part * half, 32), half), pl.ds(at, PAIR)], sems.at[i]
        )
        for i, part in enumerate((head, 1 - head))
    ]


def pair_bias(bias, at, start_a, start_b):
    lane = lax.broadcasted_iota(jnp.int32, (8, PAIR), 1)
    start = jnp.where(lane < BLOCK, start_a, start_b)
    bias[:, pl.ds(at, PAIR)] = jnp.where(start >= 0, 0.0, NEG).astype(jnp.float32)


class Half:
    def __init__(self, base, q, kt, bias, scores, weights, keys, diagonal=None):
        self.base, self.q, self.kt, self.bias = base, q, kt, bias
        self.scores, self.weights, self.keys, self.diagonal = scores, weights, keys, diagonal

    def score(self, group):
        at = group * GROUP
        rows = pl.ds(self.base, SUB)
        part = lax.dot_general(
            self.q[rows, :], self.kt[:, at : at + GROUP], NN, preferred_element_type=jnp.float32
        )
        self.scores[:, at : at + GROUP] = part + self.bias[0:1, at : at + GROUP]
        if self.diagonal is not None:
            where, key, pos, first = self.diagonal
            if at <= where < at + GROUP:
                for s in range(SUB // BLOCK):
                    slab = pl.ds(s * BLOCK, BLOCK)
                    seen = key <= pos[first + (self.base // BLOCK) + s]
                    self.scores[slab, where : where + PAIR] = jnp.where(
                        seen, self.scores[slab, where : where + PAIR], NEG
                    )

    def weigh(self, slab, old=None):
        rows = pl.ds(slab * BLOCK, BLOCK)
        high = self.scores[rows, 0:PAIR]
        for at in range(PAIR, self.keys, PAIR):
            high = jnp.maximum(high, self.scores[rows, at : at + PAIR])
        top = jnp.max(high, axis=1, keepdims=True) * SCALE
        if old is not None:
            top = jnp.maximum(top, old)
        spread = jnp.broadcast_to(top, (BLOCK, PAIR))
        total = jnp.zeros((BLOCK, PAIR), jnp.float32)
        for at in range(0, self.keys, PAIR):
            part = jnp.exp2(self.scores[rows, at : at + PAIR] * SCALE - spread)
            total = total + part
            self.weights[rows, at : at + PAIR] = part.astype(jnp.bfloat16)
        return top, jnp.sum(total, axis=1, keepdims=True)

    def combine(self, column):
        return lax.dot_general(
            self.weights[:, 0 : self.keys],
            self.kt[column : column + GROUP, 0 : self.keys],
            NT,
            preferred_element_type=jnp.float32,
        )


def first_kernel(capacity, shift, chunks, final, ids, pos, q, *refs):
    owners = len(refs_pairs := refs[: len(refs) - (1 if final else 2) - 8]) // 2
    mine, other = refs_pairs[:owners], refs_pairs[owners:]
    outs = refs[2 * owners : len(refs) - 8]
    starts, kt, bias, scores_a, scores_b, weights_a, weights_b, sems = refs[len(refs) - 8 :]
    half = mine[0].shape[1]
    head = lax.axis_index("head")
    me = lax.axis_index("ctx")
    keys = owners * chunks * PAIR
    step = pl.program_id(0)

    @pl.when(step == 0)
    def _():
        copies = []
        for c in range(chunks):
            for k in range(owners):
                at = pl.multiple_of((c * owners + (me ^ k)) * PAIR, PAIR)
                copies += pair_copies((mine[k].at[c], other[k].at[c]), kt, at, head, half, sems.at[c * owners + k])
        for copy in copies:
            copy.start()
        slot_starts(ids, starts, owners, capacity, shift)
        for c in range(chunks):
            for o in range(owners):
                slot = o * capacity + 2 * c
                pair_bias(bias, (c * owners + o) * PAIR, starts[slot], starts[slot + 1])
        for copy in copies:
            copy.wait()

    key = starts[(owners - 1) * capacity] + lax.broadcasted_iota(jnp.int32, (1, PAIR), 1)
    diagonal = ((owners - 1) * PAIR, key, pos, step * (STEP // BLOCK))
    a = Half(0, q, kt, bias, scores_a, weights_a, keys, diagonal)
    b = Half(SUB, q, kt, bias, scores_b, weights_b, keys, diagonal)
    lane = lax.broadcasted_iota(jnp.int32, (BLOCK, PAIR), 1)
    groups, slabs = keys // GROUP, SUB // BLOCK
    sums = {}

    def weigh(part, slab):
        top, low = part.weigh(slab)
        sums[part.base, slab] = low
        if not final:
            outs[1][pl.ds(part.base + slab * BLOCK, BLOCK), :] = jnp.where(lane < BLOCK, top, low)

    def combine(part, column):
        summed = part.combine(column)
        if final:
            inverse = jnp.concatenate([1.0 / sums[part.base, s] for s in range(slabs)], axis=0)
            summed = (summed * inverse).astype(jnp.bfloat16)
        outs[0][pl.ds(part.base, SUB), column : column + GROUP] = summed

    for g in range(groups):
        a.score(g)
    for i in range(max(groups, slabs)):
        if i < groups:
            b.score(i)
        if i < slabs:
            weigh(a, i)
    for i, column in enumerate(range(0, KVL, GROUP)):
        combine(a, column)
        for s in range(i * slabs // 2, (i + 1) * slabs // 2):
            weigh(b, s)
    for column in range(0, KVL, GROUP):
        combine(b, column)


def rest_kernel(capacity, shift, chunks, skip, levels, ids, q, carry, stats, *refs):
    owners = (len(refs) - 9) // 2
    mine, other = refs[:owners], refs[owners : 2 * owners]
    out, starts, kt, bias, scores_a, scores_b, weights_a, weights_b, sems = refs[2 * owners :]
    half = mine[0].shape[1]
    head = lax.axis_index("head")
    me = lax.axis_index("ctx")
    live = owners * capacity + owners

    @pl.when(pl.program_id(0) == 0)
    def _():
        slot_starts(ids, starts, owners, capacity, shift)
        kt[...] = jnp.zeros(kt.shape, kt.dtype)
        bias[...] = jnp.full(bias.shape, NEG, bias.dtype)
        pairs = [(c, k) for c in range(chunks) for k in range(owners)]

        def each(act):
            starts[live] = 0
            for c, k in pairs:
                slot = (me ^ k) * capacity + 2 * (skip + c)
                @pl.when(starts[slot] >= 0)
                def _():
                    count = starts[live]
                    starts[live] = count + 1
                    at = pl.multiple_of(count * PAIR, PAIR)
                    source = (mine[k].at[c], other[k].at[c])
                    act(pair_copies(source, kt, at, head, half, sems.at[c * owners + k]), at, slot)

        def begin(copies, at, slot):
            for copy in copies:
                copy.start()
            pair_bias(bias, at, starts[slot], starts[slot + 1])

        def end(copies, at, slot):
            for copy in copies:
                copy.wait()

        each(begin)
        each(end)

    slabs = SUB // BLOCK

    def attend(groups):
        keys = groups * GROUP
        a = Half(0, q, kt, bias, scores_a, weights_a, keys)
        b = Half(SUB, q, kt, bias, scores_b, weights_b, keys)
        factors = {}

        def weigh(part, slab):
            rows = pl.ds(part.base + slab * BLOCK, BLOCK)
            old, low = stats[rows, 0:1], stats[rows, BLOCK : BLOCK + 1]
            top, more = part.weigh(slab, old)
            shrink = jnp.exp2(old - top)
            inverse = 1.0 / (low * shrink + more)
            factors[part.base, slab] = (shrink * inverse, inverse)

        def combine(part, column):
            rows = pl.ds(part.base, SUB)
            cols = slice(column, column + GROUP)
            summed = part.combine(column)
            for s in range(slabs):
                slab = pl.ds(part.base + s * BLOCK, BLOCK)
                before, now = factors[part.base, s]
                result = carry[slab, cols] * before + summed[s * BLOCK : (s + 1) * BLOCK] * now
                out[slab, cols] = result.astype(jnp.bfloat16)

        for g in range(groups):
            a.score(g)
        for i in range(max(groups, slabs)):
            if i < groups:
                b.score(i)
            if i < slabs:
                weigh(a, i)
        for i, column in enumerate(range(0, KVL, GROUP)):
            combine(a, column)
            for s in range(i * slabs // 2, (i + 1) * slabs // 2):
                weigh(b, s)
        for column in range(0, KVL, GROUP):
            combine(b, column)

    needed = (starts[live] + 1) // 2
    below = -1
    for level in levels:
        @pl.when(jnp.logical_and(needed > below, needed <= level))
        def _():
            attend(level)
        below = level


def anywhere(count):
    return [pl.BlockSpec(memory_space=pl.ANY)] * count


def scratch(owners, capacity, chunks, lat, keys):
    return [
        pltpu.SMEM((owners * capacity + owners + 1,), jnp.int32),
        pltpu.VMEM((lat, keys), jnp.bfloat16),
        pltpu.VMEM((8, keys), jnp.float32),
        pltpu.VMEM((SUB, keys), jnp.float32),
        pltpu.VMEM((SUB, keys), jnp.float32),
        pltpu.VMEM((SUB, keys), jnp.bfloat16),
        pltpu.VMEM((SUB, keys), jnp.bfloat16),
        pltpu.SemaphoreType.DMA((chunks * owners, 2)),
    ]


def attend_first(ids, pos, q, mine, other, capacity, shift, final):
    rows, lat = q.shape
    owners, chunks = len(mine), mine[0].shape[0]
    keys = owners * chunks * PAIR
    if final:
        out_shape = [jax.ShapeDtypeStruct((rows, KVL), jnp.bfloat16)]
    else:
        out_shape = [jax.ShapeDtypeStruct((rows, KVL), jnp.float32), jax.ShapeDtypeStruct((rows, PAIR), jnp.float32)]
    return pl.pallas_call(
        functools.partial(first_kernel, capacity, shift, chunks, final),
        out_shape=out_shape,
        grid_spec=pltpu.PrefetchScalarGridSpec(
            num_scalar_prefetch=2,
            grid=(rows // STEP,),
            in_specs=[pl.BlockSpec((STEP, lat), lambda i, *_: (i, 0))] + anywhere(2 * owners),
            out_specs=[pl.BlockSpec((STEP, s.shape[1]), lambda i, *_: (i, 0)) for s in out_shape],
            scratch_shapes=scratch(owners, capacity, chunks, lat, keys),
        ),
        compiler_params=pltpu.CompilerParams(vmem_limit_bytes=56 << 20),
        cost_estimate=pl.CostEstimate(
            flops=2 * rows * keys * (lat + KVL), bytes_accessed=rows * (lat + 2 * KVL) * 2, transcendentals=rows * keys
        ),
        name="attend_first",
    )(ids, pos, q, *mine, *other)


def attend_rest(ids, q, carry, stats, mine, other, capacity, shift, skip):
    rows, lat = q.shape
    owners, chunks = len(mine), mine[0].shape[0]
    keys = owners * chunks * PAIR
    most = keys // GROUP
    levels = [n for n in (2, 3, 4) if n < most] + [most]
    return pl.pallas_call(
        functools.partial(rest_kernel, capacity, shift, chunks, skip, levels),
        out_shape=jax.ShapeDtypeStruct((rows, KVL), jnp.bfloat16),
        grid_spec=pltpu.PrefetchScalarGridSpec(
            num_scalar_prefetch=1,
            grid=(rows // STEP,),
            in_specs=[
                pl.BlockSpec((STEP, lat), lambda i, *_: (i, 0)),
                pl.BlockSpec((STEP, KVL), lambda i, *_: (i, 0)),
                pl.BlockSpec((STEP, PAIR), lambda i, *_: (i, 0)),
            ]
            + anywhere(2 * owners),
            out_specs=pl.BlockSpec((STEP, KVL), lambda i, *_: (i, 0)),
            scratch_shapes=scratch(owners, capacity, chunks, lat, keys),
        ),
        compiler_params=pltpu.CompilerParams(vmem_limit_bytes=56 << 20),
        cost_estimate=pl.CostEstimate(
            flops=rows * keys * (lat + KVL), bytes_accessed=rows * (lat + 3 * KVL) * 2, transcendentals=rows * keys // 2
        ),
        name="attend_rest",
    )(ids, q, carry, stats, *mine, *other)


def local(queries, latent_cache, positions, block_ids):
    owners = lax.axis_size("ctx")
    capacity = max(2, 2 * SEL // owners)
    shift = log2(latent_cache.shape[0] // BLOCK)
    q_rows, heads, lat = queries.shape
    rows = q_rows * heads
    all_ids = lax.all_to_all(
        jnp.broadcast_to(block_ids, (owners, SEL)), "ctx", split_axis=0, concat_axis=0, tiled=True
    )
    chunks = list(range(capacity // 2))
    cut = (len(chunks) + 1) // 2
    phases = [part for part in (chunks[:cut], chunks[cut:]) if part]
    packed = pack(all_ids, latent_cache.T, capacity, phases)
    near_first = sorted(range(1, owners), reverse=True)
    mine, other = [], []
    for p in range(len(phases)):
        own = packed[p * (owners + 1) : (p + 1) * (owners + 1)]
        got, swapped = [own[0]] + [None] * (owners - 1), [own[owners]] + [None] * (owners - 1)
        for k in near_first:
            got[k] = lax.ppermute(own[k], "ctx", [(c, c ^ k) for c in range(owners)])
        for k in near_first:
            swapped[k] = lax.ppermute(got[k], "head", [(0, 1), (1, 0)])
        mine.append(got)
        other.append(swapped)
    q = queries.reshape(rows, lat)
    ids = block_ids[0]
    final = len(phases) == 1
    out = attend_first(ids, positions, q, mine[0], other[0], capacity, shift, final)
    if final:
        out = out[0]
    else:
        out = attend_rest(ids, q, *out, mine[1], other[1], capacity, shift, cut)
    return out.reshape(q_rows, heads, KVL)


def solution(mesh):
    return jax.shard_map(
        local,
        mesh=mesh,
        in_specs=(
            P(("groups", "ctx"), "head", None),
            P(("groups", "ctx"), None),
            P(("groups", "ctx")),
            P(("groups", "ctx"), None),
        ),
        out_specs=P(("groups", "ctx"), "head", None),
        check_vma=False,
    )
```

```python
import functools

import jax
import jax.numpy as jnp
from jax import lax
from jax.experimental import pallas as pl
from jax.experimental.pallas import tpu as pltpu
from jax.sharding import PartitionSpec as P

KVL = 512
BLOCK = 64
SEL = 32
PAIR = 2 * BLOCK
GROUP = 2 * PAIR
SUB = 512
STEP = 2 * SUB
VMEM = 60 << 20
NEG = -1e30
SCALE = 1.4426950408889634 / 192.0**0.5
NT = (((1,), (1,)), ((), ()))
NN = (((1,), (0,)), ((), ()))


def log2(n):
    shift = n.bit_length() - 1
    assert 1 << shift == n
    return shift


def partners(owners):
    count = (owners - 2) // 2
    low, high = range(1, count + 1), range(count + 1, 2 * count + 1)
    return [(a, b) if i % 2 == 0 else (b, a) for i, (a, b) in enumerate(zip(low, high))]


def pack_kernel(capacity, phases, ids, cache, *refs):
    dests = ids.shape[0]
    pairs = partners(dests)
    each = len(pairs) + 2
    outs = [refs[p * each : (p + 1) * each] for p in range(len(phases))]
    table, rows, sem = refs[len(phases) * each :]
    lat, tokens = rows.shape
    half = lat // 2
    shift = log2(tokens // BLOCK)
    head = lax.axis_index("head")
    me = lax.axis_index("ctx")
    copy = pltpu.make_async_copy(cache, rows, sem)
    copy.start()

    @pl.loop(0, dests)
    def _(d):
        first = d * (capacity + 1)
        for slot in range(capacity + 1):
            table[first + slot] = 0
        at = first
        for j in range(SEL):
            block = ids[d, j]
            table[at] = block & ((1 << shift) - 1)
            at = at + (block >> shift == me).astype(jnp.int32)
        table[at] = 0

    def block_pair(d, chunk, start, size):
        first = d * (capacity + 1) + 2 * chunk
        a, b = table[first], table[first + 1]
        left = lax.broadcasted_iota(jnp.int32, (size, PAIR), 1) < BLOCK
        xa = rows[pl.ds(start, size), pl.ds(pl.multiple_of((a >> 1) * PAIR, PAIR), PAIR)].astype(jnp.float32)
        xb = rows[pl.ds(start, size), pl.ds(pl.multiple_of((b >> 1) * PAIR, PAIR), PAIR)].astype(jnp.float32)
        xa = pltpu.roll(xa, (a & 1) * BLOCK, 1)
        xb = pltpu.roll(xb, (1 - (b & 1)) * BLOCK, 1)
        return jnp.where(left, xa, xb).astype(jnp.bfloat16)

    copy.wait()
    for p, chunks in enumerate(phases):
        for c, chunk in enumerate(chunks):
            for j, (a, b) in enumerate(pairs):
                d = me ^ jnp.where(head == 0, a, b)
                outs[p][j][c] = block_pair(d, chunk, 0, lat)
            shared = pl.multiple_of(head * half, 32)
            outs[p][-2][c] = block_pair(me ^ (dests - 1), chunk, shared, half)
    for p, chunks in enumerate(phases):
        for c, chunk in enumerate(chunks):
            outs[p][-1][c] = block_pair(me, chunk, 0, lat)


def pack(all_ids, cache_t, capacity, phases):
    dests = all_ids.shape[0]
    lat, tokens = cache_t.shape
    sizes = [lat] * len(partners(dests)) + [lat // 2, lat]
    shapes = [(len(chunks), size, PAIR) for chunks in phases for size in sizes]
    packed = pl.pallas_call(
        functools.partial(pack_kernel, capacity, phases),
        out_shape=[jax.ShapeDtypeStruct(s, jnp.bfloat16) for s in shapes],
        grid_spec=pltpu.PrefetchScalarGridSpec(
            num_scalar_prefetch=1,
            grid=(1,),
            in_specs=[pl.BlockSpec(memory_space=pl.ANY)],
            out_specs=[pl.BlockSpec(s, lambda i, ids: (0, 0, 0)) for s in shapes],
            scratch_shapes=[
                pltpu.SMEM((dests * (capacity + 1),), jnp.int32),
                pltpu.VMEM((lat, tokens), jnp.bfloat16),
                pltpu.SemaphoreType.DMA,
            ],
        ),
        compiler_params=pltpu.CompilerParams(vmem_limit_bytes=VMEM),
        name="pack",
    )(all_ids, cache_t)
    return [packed[p * len(sizes) : (p + 1) * len(sizes)] for p in range(len(phases))]


def slot_starts(ids, starts, owners, capacity, shift):
    for slot in range(owners * capacity):
        starts[slot] = -1
    for o in range(owners):
        starts[owners * capacity + o] = 0
    for j in range(SEL):
        block = ids[j]
        owner = block >> shift
        rank = starts[owners * capacity + owner]
        starts[owner * capacity + rank] = block * BLOCK
        starts[owners * capacity + owner] = rank + 1


class Arrived:
    def __init__(self, owners, arrays, sems):
        pairs = partners(owners)
        count = len(pairs)
        head, me = lax.axis_index("head"), lax.axis_index("ctx")
        got, shared, own = arrays[:count], arrays[count], arrays[count + 1]
        swapped, shared_other = arrays[count + 2 : 2 * count + 2], arrays[2 * count + 2]
        self.chunks, lat, _ = own.shape
        half = lat // 2
        self.sems = sems
        self.parts = [(me, [(own, 0, lat)])]
        for (a, b), x, y in zip(pairs, got, swapped):
            self.parts.append((me ^ jnp.where(head == 0, a, b), [(x, 0, lat)]))
            self.parts.append((me ^ jnp.where(head == 0, b, a), [(y, 0, lat)]))
        split = [(x, pl.multiple_of(h * half, 32), half) for x, h in ((shared, head), (shared_other, 1 - head))]
        self.parts.append((me ^ (owners - 1), split))

    def owners(self):
        return [owner for owner, _ in self.parts]

    def copies(self, place, chunk, kt, at):
        sources = self.parts[place][1]
        return [
            pltpu.make_async_copy(
                x.at[chunk], kt.at[pl.ds(start, size), pl.ds(at, PAIR)], self.sems.at[chunk * len(self.parts) + place, i]
            )
            for i, (x, start, size) in enumerate(sources)
        ]


def pair_bias(bias, at, start_a, start_b):
    lane = lax.broadcasted_iota(jnp.int32, (8, PAIR), 1)
    start = jnp.where(lane < BLOCK, start_a, start_b)
    bias[:, pl.ds(at, PAIR)] = jnp.where(start >= 0, 0.0, NEG).astype(jnp.float32)


class Half:
    def __init__(self, base, q, kt, bias, scores, weights, tops, sums, keys, diagonal=None):
        self.base, self.q, self.kt, self.bias = base, q, kt, bias
        self.scores, self.weights, self.tops, self.sums = scores, weights, tops, sums
        self.keys, self.diagonal = keys, diagonal
        self.groups = -(-keys // GROUP)

    def score(self, group):
        at = group * GROUP
        end = min(at + GROUP, self.keys)
        part = lax.dot_general(
            self.q[pl.ds(self.base, SUB), :], self.kt[:, at:end], NN, preferred_element_type=jnp.float32
        )
        part = part + self.bias[0:1, at:end]
        columns = [part[:, c : c + PAIR] for c in range(0, end - at, PAIR)]
        if self.diagonal is not None:
            where, key, pos, first = self.diagonal
            if at <= where < end:
                seen = jnp.concatenate(
                    [
                        jnp.broadcast_to(key, (BLOCK, PAIR)) <= pos[first + self.base // BLOCK + s]
                        for s in range(SUB // BLOCK)
                    ],
                    axis=0,
                )
                index = (where - at) // PAIR
                columns[index] = jnp.where(seen, columns[index], NEG)
        high = columns[0]
        for i, column in enumerate(columns):
            self.scores[:, at + i * PAIR : at + (i + 1) * PAIR] = column
            high = jnp.maximum(high, column) if i else high
        self.tops[...] = high if group == 0 else jnp.maximum(self.tops[...], high)

    def settle(self, old=None):
        top = jnp.max(self.tops[...], axis=1, keepdims=True) * SCALE
        top = jnp.broadcast_to(top, (SUB, PAIR))
        self.tops[...] = top if old is None else jnp.maximum(top, old)

    def weigh(self, slab):
        rows = pl.ds(slab * BLOCK, BLOCK)
        top = self.tops[rows, :]
        total = jnp.zeros((BLOCK, PAIR), jnp.float32)
        for at in range(0, self.keys, PAIR):
            part = jnp.exp2(self.scores[rows, at : at + PAIR] * SCALE - top)
            total = total + part
            self.weights[rows, at : at + PAIR] = part.astype(jnp.bfloat16)
        self.sums[rows, :] = total

    def total(self):
        return jnp.broadcast_to(jnp.sum(self.sums[...], axis=1, keepdims=True), (SUB, PAIR))

    def combine(self, column):
        return lax.dot_general(
            self.weights[:, 0 : self.keys],
            self.kt[column : column + GROUP, 0 : self.keys],
            NT,
            preferred_element_type=jnp.float32,
        )


def run_halves(a, b, before, after, combine):
    slabs = SUB // BLOCK
    for g in range(a.groups):
        a.score(g)
    before(a)
    for i in range(max(a.groups, slabs)):
        if i < b.groups:
            b.score(i)
        if i < slabs:
            a.weigh(i)
    before(b)
    after(a)
    for i, column in enumerate(range(0, KVL, GROUP)):
        combine(a, column)
        for s in range(i * slabs // 2, (i + 1) * slabs // 2):
            b.weigh(s)
    after(b)
    for column in range(0, KVL, GROUP):
        combine(b, column)


SCRATCH = 12


def first_kernel(capacity, shift, owners, final, ids, pos, q, *refs):
    count = len(refs) - SCRATCH - (1 if final else 2)
    outs = refs[count : len(refs) - SCRATCH]
    starts, kt, bias, *work, sems = refs[len(refs) - SCRATCH :]
    arrived = Arrived(owners, refs[:count], sems)
    chunks = arrived.chunks
    keys = owners * chunks * PAIR
    step = pl.program_id(0)

    @pl.when(step == 0)
    def _():
        copies = []
        for c in range(chunks):
            for place, owner in enumerate(arrived.owners()):
                copies += arrived.copies(place, c, kt, pl.multiple_of((c * owners + owner) * PAIR, PAIR))
        for copy in copies:
            copy.start()
        slot_starts(ids, starts, owners, capacity, shift)
        for c in range(chunks):
            for o in range(owners):
                slot = o * capacity + 2 * c
                pair_bias(bias, (c * owners + o) * PAIR, starts[slot], starts[slot + 1])
        for copy in copies:
            copy.wait()

    key = starts[(owners - 1) * capacity] + lax.broadcasted_iota(jnp.int32, (1, PAIR), 1)
    diagonal = ((owners - 1) * PAIR, key, pos, step * (STEP // BLOCK))
    a = Half(0, q, kt, bias, *work[0::2], keys, diagonal)
    b = Half(SUB, q, kt, bias, *work[1::2], keys, diagonal)

    def after(part):
        total = part.total()
        part.sums[...] = 1.0 / total
        if not final:
            outs[1][pl.ds(part.base, SUB), :] = part.tops[...] + jnp.log2(total)

    def combine(part, column):
        summed = part.combine(column)
        for at in range(0, GROUP, PAIR):
            result = summed[:, at : at + PAIR] * part.sums[...]
            outs[0][pl.ds(part.base, SUB), column + at : column + at + PAIR] = result.astype(jnp.bfloat16)

    run_halves(a, b, lambda part: part.settle(), after, combine)


def rest_kernel(capacity, shift, owners, skip, levels, ids, q, carry, logs, *refs):
    count = len(refs) - SCRATCH - 1
    out = refs[count]
    starts, kt, bias, *work, sems = refs[len(refs) - SCRATCH :]
    arrived = Arrived(owners, refs[:count], sems)
    live = owners * capacity + owners

    @pl.when(pl.program_id(0) == 0)
    def _():
        slot_starts(ids, starts, owners, capacity, shift)
        kt[...] = jnp.zeros(kt.shape, kt.dtype)
        bias[...] = jnp.full(bias.shape, NEG, bias.dtype)

        def each(act):
            starts[live] = 0
            for c in range(arrived.chunks):
                for place, owner in enumerate(arrived.owners()):
                    slot = owner * capacity + 2 * (skip + c)
                    @pl.when(starts[slot] >= 0)
                    def _():
                        at = starts[live]
                        starts[live] = at + 1
                        at = pl.multiple_of(at * PAIR, PAIR)
                        act(arrived.copies(place, c, kt, at), at, slot)

        def begin(copies, at, slot):
            for copy in copies:
                copy.start()
            pair_bias(bias, at, starts[slot], starts[slot + 1])

        def end(copies, at, slot):
            for copy in copies:
                copy.wait()

        each(begin)
        each(end)

    def attend(keys):
        a = Half(0, q, kt, bias, *work[0::2], keys)
        b = Half(SUB, q, kt, bias, *work[1::2], keys)

        def before(part):
            part.settle(logs[pl.ds(part.base, SUB), :])

        def after(part):
            kept = jnp.exp2(logs[pl.ds(part.base, SUB), :] - part.tops[...])
            inverse = 1.0 / (kept + part.total())
            part.sums[...] = inverse
            part.tops[...] = kept * inverse

        def combine(part, column):
            summed = part.combine(column)
            rows = pl.ds(part.base, SUB)
            for at in range(0, GROUP, PAIR):
                cols = slice(column + at, column + at + PAIR)
                result = summed[:, at : at + PAIR] * part.sums[...]
                result = result + carry[rows, cols].astype(jnp.float32) * part.tops[...]
                out[rows, cols] = result.astype(jnp.bfloat16)

        run_halves(a, b, before, after, combine)

    needed = starts[live]
    below = -1
    for level in levels:
        @pl.when(jnp.logical_and(needed > below, needed <= level))
        def _():
            attend(level * PAIR)
        below = level


def anywhere(count):
    return [pl.BlockSpec(memory_space=pl.ANY)] * count


def scratch(owners, capacity, chunks, lat, keys):
    return [
        pltpu.SMEM((owners * capacity + owners + 1,), jnp.int32),
        pltpu.VMEM((lat, keys), jnp.bfloat16),
        pltpu.VMEM((8, keys), jnp.float32),
        *[pltpu.VMEM((SUB, keys), jnp.float32)] * 2,
        *[pltpu.VMEM((SUB, keys), jnp.bfloat16)] * 2,
        *[pltpu.VMEM((SUB, PAIR), jnp.float32)] * 4,
        pltpu.SemaphoreType.DMA((chunks * owners, 2)),
    ]


def attend_first(ids, pos, q, arrays, owners, capacity, shift, chunks, final):
    rows, lat = q.shape
    keys = owners * chunks * PAIR
    out_shape = [jax.ShapeDtypeStruct((rows, KVL), jnp.bfloat16), jax.ShapeDtypeStruct((rows, PAIR), jnp.float32)]
    if final:
        out_shape = out_shape[:1]
    return pl.pallas_call(
        functools.partial(first_kernel, capacity, shift, owners, final),
        out_shape=out_shape,
        grid_spec=pltpu.PrefetchScalarGridSpec(
            num_scalar_prefetch=2,
            grid=(rows // STEP,),
            in_specs=[pl.BlockSpec((STEP, lat), lambda i, *_: (i, 0))] + anywhere(len(arrays)),
            out_specs=[pl.BlockSpec((STEP, s.shape[1]), lambda i, *_: (i, 0)) for s in out_shape],
            scratch_shapes=scratch(owners, capacity, chunks, lat, keys),
        ),
        compiler_params=pltpu.CompilerParams(vmem_limit_bytes=VMEM),
        cost_estimate=pl.CostEstimate(
            flops=2 * rows * keys * (lat + KVL), bytes_accessed=rows * (lat + KVL) * 2, transcendentals=rows * keys
        ),
        name="attend_first",
    )(ids, pos, q, *arrays)


def attend_rest(ids, q, carry, logs, arrays, owners, capacity, shift, chunks, skip):
    rows, lat = q.shape
    keys = owners * chunks * PAIR
    most = owners * chunks
    levels = [n for n in (4, 5, 6, 8) if n < most] + [most]
    return pl.pallas_call(
        functools.partial(rest_kernel, capacity, shift, owners, skip, levels),
        out_shape=jax.ShapeDtypeStruct((rows, KVL), jnp.bfloat16),
        grid_spec=pltpu.PrefetchScalarGridSpec(
            num_scalar_prefetch=1,
            grid=(rows // STEP,),
            in_specs=[
                pl.BlockSpec((STEP, lat), lambda i, *_: (i, 0)),
                pl.BlockSpec((STEP, KVL), lambda i, *_: (i, 0)),
                pl.BlockSpec((STEP, PAIR), lambda i, *_: (i, 0)),
            ]
            + anywhere(len(arrays)),
            out_specs=pl.BlockSpec((STEP, KVL), lambda i, *_: (i, 0)),
            scratch_shapes=scratch(owners, capacity, chunks, lat, keys),
        ),
        compiler_params=pltpu.CompilerParams(vmem_limit_bytes=VMEM),
        cost_estimate=pl.CostEstimate(
            flops=rows * keys * (lat + KVL), bytes_accessed=rows * (lat + 2 * KVL) * 2, transcendentals=rows * keys // 2
        ),
        name="attend_rest",
    )(ids, q, carry, logs, *arrays)


def local(queries, latent_cache, positions, block_ids):
    owners = lax.axis_size("ctx")
    capacity = max(2, 2 * SEL // owners)
    shift = log2(latent_cache.shape[0] // BLOCK)
    q_rows, heads, lat = queries.shape
    rows = q_rows * heads
    all_ids = lax.all_to_all(
        jnp.broadcast_to(block_ids, (owners, SEL)), "ctx", split_axis=0, concat_axis=0, tiled=True
    )
    chunks = list(range(capacity // 2))
    cut = (len(chunks) + 1) // 2
    phases = [part for part in (chunks[:cut], chunks[cut:]) if part]
    packed = pack(all_ids, latent_cache.T, capacity, phases)
    steps = partners(owners) + [(owners - 1, owners - 1)]

    def send(own):
        got = []
        for x, ks in zip(own, steps):
            moves = [(2 * c + h, 2 * (c ^ k) + h) for c in range(owners) for h, k in enumerate(ks)]
            got.append(lax.ppermute(x, ("ctx", "head"), moves))
        return got

    def swap(got):
        return [lax.ppermute(x, "head", [(0, 1), (1, 0)]) for x in got]

    q = queries.reshape(rows, lat)
    ids = block_ids[0]
    final = len(phases) == 1
    got = [send(own) for own in packed]
    arrays = [*got[0], packed[0][-1], *swap(got[0])]
    out = attend_first(ids, positions, q, arrays, owners, capacity, shift, len(phases[0]), final)
    if final:
        out = out[0]
    else:
        carry, logs = out
        *late, logs = lax.optimization_barrier((*got[1], logs))
        arrays = [*late, packed[1][-1], *swap(late)]
        out = attend_rest(ids, q, carry, logs, arrays, owners, capacity, shift, len(phases[1]), cut)
    return out.reshape(q_rows, heads, KVL)


def solution(mesh):
    return jax.shard_map(
        local,
        mesh=mesh,
        in_specs=(
            P(("groups", "ctx"), "head", None),
            P(("groups", "ctx"), None),
            P(("groups", "ctx")),
            P(("groups", "ctx"), None),
        ),
        out_specs=P(("groups", "ctx"), "head", None),
        check_vma=False,
    )
```

```python
import functools

import jax
import jax.numpy as jnp
from jax import lax
from jax.experimental import pallas as pl
from jax.experimental.pallas import tpu as pltpu
from jax.sharding import PartitionSpec as P

KVL = 512
BLOCK = 64
SEL = 32
PAIR = 2 * BLOCK
GROUP = 2 * PAIR
SUB = 512
STEP = 2 * SUB
VMEM = 60 << 20
NEG = -1e30
SCALE = 1.4426950408889634 / 192.0**0.5
NT = (((1,), (1,)), ((), ()))
NN = (((1,), (0,)), ((), ()))


def log2(n):
    shift = n.bit_length() - 1
    assert 1 << shift == n
    return shift


def partners(owners):
    count = (owners - 2) // 2
    low, high = range(1, count + 1), range(count + 1, 2 * count + 1)
    return [(a, b) if i % 2 == 0 else (b, a) for i, (a, b) in enumerate(zip(low, high))]


def pack_kernel(capacity, chunks, ids, cache, *refs):
    dests = ids.shape[0]
    pairs = partners(dests)
    outs = refs[: len(pairs) + 2]
    table, rows, sem = refs[len(pairs) + 2 :]
    lat, tokens = rows.shape
    half = lat // 2
    shift = log2(tokens // BLOCK)
    head = lax.axis_index("head")
    me = lax.axis_index("ctx")
    copy = pltpu.make_async_copy(cache, rows, sem)
    copy.start()

    @pl.loop(0, dests)
    def _(d):
        first = d * (capacity + 1)
        for slot in range(capacity + 1):
            table[first + slot] = 0
        at = first
        for j in range(SEL):
            block = ids[d, j]
            table[at] = block & ((1 << shift) - 1)
            at = at + (block >> shift == me).astype(jnp.int32)
        table[at] = 0

    def block_pair(d, chunk, start, size):
        first = d * (capacity + 1) + 2 * chunk
        a, b = table[first], table[first + 1]
        left = lax.broadcasted_iota(jnp.int32, (size, PAIR), 1) < BLOCK
        xa = rows[pl.ds(start, size), pl.ds(pl.multiple_of((a >> 1) * PAIR, PAIR), PAIR)].astype(jnp.float32)
        xb = rows[pl.ds(start, size), pl.ds(pl.multiple_of((b >> 1) * PAIR, PAIR), PAIR)].astype(jnp.float32)
        xa = pltpu.roll(xa, (a & 1) * BLOCK, 1)
        xb = pltpu.roll(xb, (1 - (b & 1)) * BLOCK, 1)
        return jnp.where(left, xa, xb).astype(jnp.bfloat16)

    copy.wait()
    for c, chunk in enumerate(chunks):
        for j, (a, b) in enumerate(pairs):
            d = me ^ jnp.where(head == 0, a, b)
            outs[j][c] = block_pair(d, chunk, 0, lat)
        shared = pl.multiple_of(head * half, 32)
        outs[-2][c] = block_pair(me ^ (dests - 1), chunk, shared, half)
        outs[-1][c] = block_pair(me, chunk, 0, lat)


def pack(all_ids, cache_t, capacity, phases):
    dests = all_ids.shape[0]
    lat, tokens = cache_t.shape
    chunks = [chunk for phase in phases for chunk in phase]
    sizes = [lat] * len(partners(dests)) + [lat // 2, lat]
    shapes = [(len(phase), size, PAIR) for phase in phases for size in sizes]

    def kernel(ids, cache, *refs):
        scratch = refs[len(shapes) :]
        joined = []
        for j in range(len(sizes)):
            views = [refs[p * len(sizes) + j].at[i] for p, phase in enumerate(phases) for i in range(len(phase))]
            joined.append(Views(views))
        pack_kernel(capacity, chunks, ids, cache, *joined, *scratch)

    packed = pl.pallas_call(
        kernel,
        out_shape=[jax.ShapeDtypeStruct(s, jnp.bfloat16) for s in shapes],
        grid_spec=pltpu.PrefetchScalarGridSpec(
            num_scalar_prefetch=1,
            grid=(1,),
            in_specs=[pl.BlockSpec(memory_space=pl.ANY)],
            out_specs=[pl.BlockSpec(s, lambda i, ids: (0, 0, 0)) for s in shapes],
            scratch_shapes=[
                pltpu.SMEM((dests * (capacity + 1),), jnp.int32),
                pltpu.VMEM((lat, tokens), jnp.bfloat16),
                pltpu.SemaphoreType.DMA,
            ],
        ),
        compiler_params=pltpu.CompilerParams(vmem_limit_bytes=VMEM),
        cost_estimate=pl.CostEstimate(flops=0, bytes_accessed=8 * lat * tokens, transcendentals=0),
        name="pack",
    )(all_ids, cache_t)
    return [list(packed[p * len(sizes) : (p + 1) * len(sizes)]) for p in range(len(phases))]


class Views:
    def __init__(self, refs):
        self.refs = refs

    def __setitem__(self, i, value):
        self.refs[i][...] = value


def pair_bias(bias, at, start_a, start_b):
    lane = lax.broadcasted_iota(jnp.int32, (8, PAIR), 1)
    start = jnp.where(lane < BLOCK, start_a, start_b)
    bias[:, pl.ds(at, PAIR)] = jnp.where(start >= 0, 0.0, NEG).astype(jnp.float32)


def plan_kernel(owners, capacity, shift, phases, ids, table, *rest):
    biases, count = rest[:-1], rest[-1]
    for slot in range(owners * capacity):
        table[slot] = -1
    for o in range(owners):
        count[o] = 0
    for j in range(SEL):
        block = ids[j]
        owner = block >> shift
        rank = count[owner]
        table[owner * capacity + rank] = block * BLOCK
        count[owner] = rank + 1
    for p, (bias, phase) in enumerate(zip(biases, phases)):
        last = p > 0 and p == len(phases) - 1
        if last:
            bias[...] = jnp.full(bias.shape, NEG, bias.dtype)
            live = jnp.int32(0)
        for c, chunk in enumerate(phase):
            for o in range(owners if p == 0 else owners - 1):
                slot = o * capacity + 2 * chunk
                a, b = table[slot], table[slot + 1]
                if last:
                    used = a >= 0
                    table[owners * capacity + c * owners + o] = jnp.where(used, live, -1)
                    pair_bias(bias, pl.multiple_of(live * PAIR, PAIR), a, b)
                    live = live + used.astype(jnp.int32)
                else:
                    pair_bias(bias, (c * (owners if p == 0 else owners - 1) + o) * PAIR, a, b)
            if last:
                table[owners * capacity + c * owners + owners - 1] = -1
        if last:
            table[owners * capacity + len(phase) * owners] = live


def plan(ids, owners, capacity, shift, phases):
    shapes = [(8, len(phase) * (owners if p == 0 else owners - 1) * PAIR) for p, phase in enumerate(phases)]
    if len(phases) > 1:
        shapes[-1] = (8, shapes[-1][1] + PAIR)
    entries = owners * capacity + len(phases[-1]) * owners + 1
    return pl.pallas_call(
        functools.partial(plan_kernel, owners, capacity, shift, phases),
        out_shape=[jax.ShapeDtypeStruct((entries,), jnp.int32)]
        + [jax.ShapeDtypeStruct(s, jnp.float32) for s in shapes],
        grid_spec=pltpu.PrefetchScalarGridSpec(
            num_scalar_prefetch=1,
            grid=(1,),
            in_specs=[],
            out_specs=[pl.BlockSpec(memory_space=pltpu.SMEM)] + [pl.BlockSpec(s, lambda i, ids: (0, 0)) for s in shapes],
            scratch_shapes=[pltpu.SMEM((owners,), jnp.int32)],
        ),
        cost_estimate=pl.CostEstimate(flops=0, bytes_accessed=1 << 20, transcendentals=0),
        name="plan",
    )(ids)


class Arrived:
    def __init__(self, owners, arrays):
        pairs = partners(owners)
        count = len(pairs)
        head, me = lax.axis_index("head"), lax.axis_index("ctx")
        got, shared, own = arrays[:count], arrays[count], arrays[count + 1]
        swapped, shared_other = arrays[count + 2 : 2 * count + 2], arrays[2 * count + 2]
        self.chunks, lat, _ = own.shape
        half = lat // 2
        self.parts = [(me, [(own, 0, lat)])]
        for (a, b), x, y in zip(pairs, got, swapped):
            self.parts.append((me ^ jnp.where(head == 0, a, b), [(x, 0, lat)]))
            self.parts.append((me ^ jnp.where(head == 0, b, a), [(y, 0, lat)]))
        split = [(x, pl.multiple_of(h * half, 32), half) for x, h in ((shared, head), (shared_other, 1 - head))]
        self.parts.append((me ^ (owners - 1), split))

    def place(self, chunk, part, kt, at):
        for x, start, size in self.parts[part][1]:
            kt[pl.ds(start, size), pl.ds(pl.multiple_of(at, PAIR), PAIR)] = x[chunk]


class Half:
    def __init__(self, base, q, kt, bias, scores, weights, tops, sums, keys, diagonal=None):
        self.base, self.q, self.kt, self.bias = base, q, kt, bias
        self.scores, self.weights, self.tops, self.sums = scores, weights, tops, sums
        self.keys, self.diagonal = keys, diagonal
        self.groups = -(-keys // GROUP)

    def score(self, group):
        at = group * GROUP
        end = min(at + GROUP, self.keys)
        part = lax.dot_general(
            self.q[pl.ds(self.base, SUB), :], self.kt[:, at:end], NN, preferred_element_type=jnp.float32
        )
        part = part + self.bias[0:1, at:end]
        columns = [part[:, c : c + PAIR] for c in range(0, end - at, PAIR)]
        if self.diagonal is not None:
            where, key, pos, first = self.diagonal
            if at <= where < end:
                seen = jnp.concatenate(
                    [
                        jnp.broadcast_to(key, (BLOCK, PAIR)) <= pos[first + self.base // BLOCK + s]
                        for s in range(SUB // BLOCK)
                    ],
                    axis=0,
                )
                index = (where - at) // PAIR
                columns[index] = jnp.where(seen, columns[index], NEG)
        high = columns[0]
        for i, column in enumerate(columns):
            self.scores[:, at + i * PAIR : at + (i + 1) * PAIR] = column
            high = jnp.maximum(high, column) if i else high
        self.tops[...] = high if group == 0 else jnp.maximum(self.tops[...], high)

    def settle(self, old=None):
        top = jnp.max(self.tops[...], axis=1, keepdims=True) * SCALE
        top = jnp.broadcast_to(top, (SUB, PAIR))
        self.tops[...] = top if old is None else jnp.maximum(top, old)

    def weigh(self, slab):
        rows = pl.ds(slab * BLOCK, BLOCK)
        top = self.tops[rows, :]
        total = jnp.zeros((BLOCK, PAIR), jnp.float32)
        for at in range(0, self.keys, PAIR):
            part = jnp.exp2(self.scores[rows, at : at + PAIR] * SCALE - top)
            total = total + part
            self.weights[rows, at : at + PAIR] = part.astype(jnp.bfloat16)
        self.sums[rows, :] = total

    def total(self):
        return jnp.broadcast_to(jnp.sum(self.sums[...], axis=1, keepdims=True), (SUB, PAIR))

    def combine(self, column):
        return lax.dot_general(
            self.weights[:, 0 : self.keys],
            self.kt[column : column + GROUP, 0 : self.keys],
            NT,
            preferred_element_type=jnp.float32,
        )


def run_halves(a, b, before, after, combine):
    slabs = SUB // BLOCK
    for g in range(a.groups):
        a.score(g)
    before(a)
    for i in range(max(a.groups, slabs)):
        if i < b.groups:
            b.score(i)
        if i < slabs:
            a.weigh(i)
    before(b)
    after(a)
    for i, column in enumerate(range(0, KVL, GROUP)):
        combine(a, column)
        for s in range(i * slabs // 2, (i + 1) * slabs // 2):
            b.weigh(s)
    after(b)
    for column in range(0, KVL, GROUP):
        combine(b, column)


SCRATCH = 9


def attend_kernel(owners, capacity, kind, levels, table, pos, q, bias, *refs):
    start, end = kind in ("first", "only"), kind in ("last", "only")
    if not start:
        carry, logs, *refs = refs
    outs = refs[len(refs) - SCRATCH - (1 if end else 2) : len(refs) - SCRATCH]
    kt, *work = refs[len(refs) - SCRATCH :]
    arrived = Arrived(owners, refs[: len(refs) - SCRATCH - len(outs)])
    chunks = arrived.chunks
    step = pl.program_id(0)
    index = owners * capacity
    needed = table[index + chunks * owners] if kind == "last" else None

    @pl.when(step == 0)
    def _():
        for c in range(chunks):
            for part, (owner, _) in enumerate(arrived.parts):
                if kind == "last":
                    at = table[index + c * owners + owner]
                    pl.when(at >= 0)(functools.partial(arrived.place, c, part, kt, at * PAIR))
                elif start:
                    arrived.place(c, part, kt, (c * owners + owner) * PAIR)
                else:
                    at = (c * (owners - 1) + owner) * PAIR
                    pl.when(owner < owners - 1)(functools.partial(arrived.place, c, part, kt, at))
        if kind == "last":
            fill = jnp.int32(levels[-1])
            for level in reversed(levels[:-1]):
                fill = jnp.where(needed <= level, level, fill)

            @pl.loop(needed, fill)
            def _(i):
                kt[:, pl.ds(pl.multiple_of(i * PAIR, PAIR), PAIR)] = jnp.zeros((kt.shape[0], PAIR), kt.dtype)

    def attend(keys):
        diagonal = None
        if start:
            key = table[(owners - 1) * capacity] + lax.broadcasted_iota(jnp.int32, (1, PAIR), 1)
            diagonal = ((owners - 1) * PAIR, key, pos, step * (STEP // BLOCK))
        a = Half(0, q, kt, bias, *work[0::2], keys, diagonal)
        b = Half(SUB, q, kt, bias, *work[1::2], keys, diagonal)

        def before(part):
            part.settle(None if start else logs[pl.ds(part.base, SUB), :])

        def after(part):
            rows = pl.ds(part.base, SUB)
            total = part.total()
            if not start:
                kept = jnp.exp2(logs[rows, :] - part.tops[...])
                total = total + kept
            inverse = 1.0 / total
            part.sums[...] = inverse
            if not end:
                outs[1][rows, :] = part.tops[...] + jnp.log2(total)
            if not start:
                part.tops[...] = kept * inverse

        def combine(part, column):
            summed = part.combine(column)
            rows = pl.ds(part.base, SUB)
            for at in range(0, GROUP, PAIR):
                cols = slice(column + at, column + at + PAIR)
                result = summed[:, at : at + PAIR] * part.sums[...]
                if not start:
                    result = result + carry[rows, cols] * part.tops[...]
                outs[0][rows, cols] = result.astype(outs[0].dtype)

        run_halves(a, b, before, after, combine)

    if kind != "last":
        attend(kt.shape[1])
        return
    below = -1
    for level in levels:
        pl.when(jnp.logical_and(needed > below, needed <= level))(functools.partial(attend, level * PAIR))
        below = level


def attend(table, pos, q, bias, state, arrays, owners, capacity, kind, chunks):
    rows, lat = q.shape
    pairs = chunks * (owners if kind in ("first", "only") else owners - 1)
    keys = pairs * PAIR
    levels = [n for n in (4, 5, 6, 8) if n < pairs] + [pairs]
    out_shape = [jax.ShapeDtypeStruct((rows, KVL), jnp.float32), jax.ShapeDtypeStruct((rows, PAIR), jnp.float32)]
    if kind in ("last", "only"):
        out_shape = [jax.ShapeDtypeStruct((rows, KVL), jnp.bfloat16)]

    def whole(x):
        return pl.BlockSpec(x.shape, lambda i, *_: (0,) * x.ndim)

    def row_block(x):
        return pl.BlockSpec((STEP, x.shape[1]), lambda i, *_: (i, 0))

    return pl.pallas_call(
        functools.partial(attend_kernel, owners, capacity, kind, levels),
        out_shape=out_shape,
        grid_spec=pltpu.PrefetchScalarGridSpec(
            num_scalar_prefetch=2,
            grid=(rows // STEP,),
            in_specs=[row_block(q), whole(bias)] + [row_block(x) for x in state] + [whole(x) for x in arrays],
            out_specs=[row_block(x) for x in out_shape],
            scratch_shapes=[
                pltpu.VMEM((lat, keys), jnp.bfloat16),
                *[pltpu.VMEM((SUB, keys), jnp.float32)] * 2,
                *[pltpu.VMEM((SUB, keys), jnp.bfloat16)] * 2,
                *[pltpu.VMEM((SUB, PAIR), jnp.float32)] * 4,
            ],
        ),
        compiler_params=pltpu.CompilerParams(vmem_limit_bytes=VMEM),
        cost_estimate=pl.CostEstimate(
            flops=2 * rows * keys * (lat + KVL), bytes_accessed=rows * (lat + 2 * KVL) * 2, transcendentals=rows * keys
        ),
        name="attend_" + kind,
    )(table, pos, q, bias, *state, *arrays)


def split_phases(chunks):
    if chunks < 3:
        return [[c] for c in range(chunks)]
    return [[0], [1], list(range(2, chunks))]


def local(queries, latent_cache, positions, block_ids):
    owners = lax.axis_size("ctx")
    capacity = max(2, 2 * SEL // owners)
    shift = log2(latent_cache.shape[0] // BLOCK)
    q_rows, heads, lat = queries.shape
    rows = q_rows * heads
    all_ids = lax.all_to_all(
        jnp.broadcast_to(block_ids, (owners, SEL)), "ctx", split_axis=0, concat_axis=0, tiled=True
    )
    phases = split_phases(capacity // 2)
    packed = pack(all_ids, latent_cache.T, capacity, phases[:1])
    if len(phases) > 1:
        packed += pack(all_ids, latent_cache.T, capacity, phases[1:])
    table, *biases = plan(block_ids[0], owners, capacity, shift, phases)
    steps = partners(owners) + [(owners - 1, owners - 1)]

    def send(own):
        got = []
        for x, ks in zip(own, steps):
            moves = [(2 * c + h, 2 * (c ^ k) + h) for c in range(owners) for h, k in enumerate(ks)]
            got.append(lax.ppermute(x, ("ctx", "head"), moves))
        return got

    def swap(got):
        return [lax.ppermute(x, "head", [(0, 1), (1, 0)]) for x in got]

    q = queries.reshape(rows, lat)
    got = [send(own) for own in packed]
    if len(phases) > 1:
        *got[0], packed[1][-1], table = lax.optimization_barrier((*got[0], packed[1][-1], table))
    state = []
    for p, phase in enumerate(phases):
        late = got[p]
        if state:
            *late, logs = lax.optimization_barrier((*late, state[1]))
            state = [state[0], logs]
        arrays = [*late, packed[p][-1], *swap(late)]
        kind = "only" if len(phases) == 1 else "first" if p == 0 else "last" if p == len(phases) - 1 else "middle"
        state = attend(table, positions, q, biases[p], state, arrays, owners, capacity, kind, len(phase))
    return state[0].reshape(q_rows, heads, KVL)


def solution(mesh):
    return jax.shard_map(
        local,
        mesh=mesh,
        in_specs=(
            P(("groups", "ctx"), "head", None),
            P(("groups", "ctx"), None),
            P(("groups", "ctx")),
            P(("groups", "ctx"), None),
        ),
        out_specs=P(("groups", "ctx"), "head", None),
        check_vma=False,
    )
```

```python
import functools

import jax
import jax.numpy as jnp
from jax import lax
from jax.experimental import pallas as pl
from jax.experimental.pallas import tpu as pltpu
from jax.sharding import PartitionSpec as P

KVL = 512
BLOCK = 64
SEL = 32
PAIR = 2 * BLOCK
GROUP = 2 * PAIR
SUB = 512
STEP = 2 * SUB
VMEM = 60 << 20
NEG = -1e30
SCALE = 1.4426950408889634 / 192.0**0.5
NT = (((1,), (1,)), ((), ()))
NN = (((1,), (0,)), ((), ()))


def log2(n):
    shift = n.bit_length() - 1
    assert 1 << shift == n
    return shift


def partners(owners):
    count = (owners - 2) // 2
    low, high = range(1, count + 1), range(count + 1, 2 * count + 1)
    return [(a, b) if i % 2 == 0 else (b, a) for i, (a, b) in enumerate(zip(low, high))]


def pack_kernel(capacity, chunks, ids, cache, *refs):
    dests = len(ids)
    pairs = partners(dests)
    outs = refs[: len(pairs) + 2]
    table, rows, sem = refs[len(pairs) + 2 :]
    lat, tokens = rows.shape
    half = lat // 2
    shift = log2(tokens // BLOCK)
    head = lax.axis_index("head")
    me = lax.axis_index("ctx")
    copy = pltpu.make_async_copy(cache, rows, sem)
    copy.start()
    for k in range(dests):
        at = jnp.int32(k * (capacity + 1))
        for slot in range(capacity + 1):
            table[k * (capacity + 1) + slot] = 0
        for j in range(SEL):
            block = ids[k][0, j]
            table[at] = block & ((1 << shift) - 1)
            at = at + (block >> shift == me).astype(jnp.int32)
        table[at] = 0

    def block_pair(k, chunk, start, size):
        first = k * (capacity + 1) + 2 * chunk
        a, b = table[first], table[first + 1]
        left = lax.broadcasted_iota(jnp.int32, (size, PAIR), 1) < BLOCK
        xa = rows[pl.ds(start, size), pl.ds(pl.multiple_of((a >> 1) * PAIR, PAIR), PAIR)].astype(jnp.float32)
        xb = rows[pl.ds(start, size), pl.ds(pl.multiple_of((b >> 1) * PAIR, PAIR), PAIR)].astype(jnp.float32)
        xa = pltpu.roll(xa, (a & 1) * BLOCK, 1)
        xb = pltpu.roll(xb, (1 - (b & 1)) * BLOCK, 1)
        return jnp.where(left, xa, xb).astype(jnp.bfloat16)

    copy.wait()
    for c, chunk in enumerate(chunks):
        for j, (a, b) in enumerate(pairs):
            outs[j][c] = block_pair(jnp.where(head == 0, a, b), chunk, 0, lat)
        outs[-2][c] = block_pair(dests - 1, chunk, pl.multiple_of(head * half, 32), half)
        outs[-1][c] = block_pair(0, chunk, 0, lat)


def pack(ids, cache_t, capacity, chunks):
    dests = len(ids)
    lat, tokens = cache_t.shape
    sizes = [lat] * len(partners(dests)) + [lat // 2, lat]
    shapes = [(len(chunks), size, PAIR) for size in sizes]

    def kernel(*refs):
        pack_kernel(capacity, chunks, refs[:dests], *refs[dests:])

    packed = pl.pallas_call(
        kernel,
        out_shape=[jax.ShapeDtypeStruct(s, jnp.bfloat16) for s in shapes],
        grid_spec=pltpu.PrefetchScalarGridSpec(
            num_scalar_prefetch=dests,
            grid=(1,),
            in_specs=[pl.BlockSpec(memory_space=pl.ANY)],
            out_specs=[pl.BlockSpec(s, lambda i, *_: (0, 0, 0)) for s in shapes],
            scratch_shapes=[
                pltpu.SMEM((dests * (capacity + 1),), jnp.int32),
                pltpu.VMEM((lat, tokens), jnp.bfloat16),
                pltpu.SemaphoreType.DMA,
            ],
        ),
        compiler_params=pltpu.CompilerParams(vmem_limit_bytes=VMEM),
        cost_estimate=pl.CostEstimate(flops=0, bytes_accessed=8 * lat * tokens, transcendentals=0),
        name="pack",
    )(*ids, cache_t)
    return list(packed)


def pair_bias(bias, at, start_a, start_b):
    lane = lax.broadcasted_iota(jnp.int32, (8, PAIR), 1)
    start = jnp.where(lane < BLOCK, start_a, start_b)
    bias[:, pl.ds(at, PAIR)] = jnp.where(start >= 0, 0.0, NEG).astype(jnp.float32)


def pair_places(owners, phase, first):
    return {
        (c, o): i
        for i, (c, o) in enumerate((c, o) for c in range(phase) for o in range(owners) if o < owners - 1 or first and c == 0)
    }


def plan_kernel(owners, capacity, shift, phases, ids, table, *rest):
    biases, count = rest[:-1], rest[-1]
    for slot in range(owners * capacity):
        table[slot] = -1
    for o in range(owners):
        count[o] = 0
    for j in range(SEL):
        block = ids[j]
        owner = block >> shift
        rank = count[owner]
        table[owner * capacity + rank] = block * BLOCK
        count[owner] = rank + 1
    for p, (bias, phase) in enumerate(zip(biases, phases)):
        last = p > 0 and p == len(phases) - 1
        if last:
            bias[...] = jnp.full(bias.shape, NEG, bias.dtype)
            live = jnp.int32(0)
        for (c, o), i in pair_places(owners, len(phase), p == 0).items():
            slot = o * capacity + 2 * phase[c]
            a, b = table[slot], table[slot + 1]
            if last:
                used = a >= 0
                table[owners * capacity + c * owners + o] = jnp.where(used, live, -1)
                pair_bias(bias, pl.multiple_of(live * PAIR, PAIR), a, b)
                live = live + used.astype(jnp.int32)
            else:
                pair_bias(bias, i * PAIR, a, b)
        if last:
            for c in range(len(phase)):
                table[owners * capacity + c * owners + owners - 1] = -1
            table[owners * capacity + len(phase) * owners] = live


def plan(ids, owners, capacity, shift, phases):
    shapes = [(8, len(pair_places(owners, len(phase), p == 0)) * PAIR) for p, phase in enumerate(phases)]
    if len(phases) > 1:
        shapes[-1] = (8, shapes[-1][1] + PAIR)
    entries = owners * capacity + len(phases[-1]) * owners + 1
    return pl.pallas_call(
        functools.partial(plan_kernel, owners, capacity, shift, phases),
        out_shape=[jax.ShapeDtypeStruct((entries,), jnp.int32)]
        + [jax.ShapeDtypeStruct(s, jnp.float32) for s in shapes],
        grid_spec=pltpu.PrefetchScalarGridSpec(
            num_scalar_prefetch=1,
            grid=(1,),
            in_specs=[],
            out_specs=[pl.BlockSpec(memory_space=pltpu.SMEM)] + [pl.BlockSpec(s, lambda i, ids: (0, 0)) for s in shapes],
            scratch_shapes=[pltpu.SMEM((owners,), jnp.int32)],
        ),
        cost_estimate=pl.CostEstimate(flops=0, bytes_accessed=1 << 20, transcendentals=0),
        name="plan",
    )(ids)


class Arrived:
    def __init__(self, owners, arrays):
        pairs = partners(owners)
        count = len(pairs)
        head, me = lax.axis_index("head"), lax.axis_index("ctx")
        got, shared, own = arrays[:count], arrays[count], arrays[count + 1]
        swapped, shared_other = arrays[count + 2 : 2 * count + 2], arrays[2 * count + 2]
        self.chunks, lat, _ = own.shape
        half = lat // 2
        self.parts = [(me, [(own, 0, lat)])]
        for (a, b), x, y in zip(pairs, got, swapped):
            self.parts.append((me ^ jnp.where(head == 0, a, b), [(x, 0, lat)]))
            self.parts.append((me ^ jnp.where(head == 0, b, a), [(y, 0, lat)]))
        split = [(x, pl.multiple_of(h * half, 32), half) for x, h in ((shared, head), (shared_other, 1 - head))]
        self.parts.append((me ^ (owners - 1), split))

    def place(self, chunk, part, kt, at):
        for x, start, size in self.parts[part][1]:
            kt[pl.ds(start, size), pl.ds(pl.multiple_of(at, PAIR), PAIR)] = x[chunk]


class Half:
    def __init__(self, base, q, kt, bias, scores, weights, tops, sums, keys, diagonal=None):
        self.base, self.q, self.kt, self.bias = base, q, kt, bias
        self.scores, self.weights, self.tops, self.sums = scores, weights, tops, sums
        self.keys, self.diagonal = keys, diagonal
        self.groups = -(-keys // GROUP)

    def score(self, group):
        at = group * GROUP
        end = min(at + GROUP, self.keys)
        part = lax.dot_general(
            self.q[pl.ds(self.base, SUB), :], self.kt[:, at:end], NN, preferred_element_type=jnp.float32
        )
        part = part + self.bias[0:1, at:end]
        columns = [part[:, c : c + PAIR] for c in range(0, end - at, PAIR)]
        if self.diagonal is not None:
            where, key, pos, first = self.diagonal
            if at <= where < end:
                seen = jnp.concatenate(
                    [
                        jnp.broadcast_to(key, (BLOCK, PAIR)) <= pos[first + self.base // BLOCK + s]
                        for s in range(SUB // BLOCK)
                    ],
                    axis=0,
                )
                index = (where - at) // PAIR
                columns[index] = jnp.where(seen, columns[index], NEG)
        high = columns[0]
        for i, column in enumerate(columns):
            self.scores[:, at + i * PAIR : at + (i + 1) * PAIR] = column
            high = jnp.maximum(high, column) if i else high
        self.tops[...] = high if group == 0 else jnp.maximum(self.tops[...], high)

    def settle(self, old=None):
        top = jnp.max(self.tops[...], axis=1, keepdims=True) * SCALE
        top = jnp.broadcast_to(top, (SUB, PAIR))
        self.tops[...] = top if old is None else jnp.maximum(top, old)

    def weigh(self, slab):
        rows = pl.ds(slab * BLOCK, BLOCK)
        top = self.tops[rows, :]
        total = jnp.zeros((BLOCK, PAIR), jnp.float32)
        for at in range(0, self.keys, PAIR):
            part = jnp.exp2(self.scores[rows, at : at + PAIR] * SCALE - top)
            total = total + part
            self.weights[rows, at : at + PAIR] = part.astype(jnp.bfloat16)
        self.sums[rows, :] = total

    def total(self):
        return jnp.broadcast_to(jnp.sum(self.sums[...], axis=1, keepdims=True), (SUB, PAIR))

    def combine(self, column):
        return lax.dot_general(
            self.weights[:, 0 : self.keys],
            self.kt[column : column + GROUP, 0 : self.keys],
            NT,
            preferred_element_type=jnp.float32,
        )


def run_halves(a, b, before, after, combine):
    slabs = SUB // BLOCK
    for g in range(a.groups):
        a.score(g)
    before(a)
    for i in range(max(a.groups, slabs)):
        if i < b.groups:
            b.score(i)
        if i < slabs:
            a.weigh(i)
    before(b)
    after(a)
    for i, column in enumerate(range(0, KVL, GROUP)):
        combine(a, column)
        for s in range(i * slabs // 2, (i + 1) * slabs // 2):
            b.weigh(s)
    after(b)
    for column in range(0, KVL, GROUP):
        combine(b, column)


SCRATCH = 9


def attend_kernel(owners, capacity, kind, levels, table, pos, q, bias, *refs):
    start, end = kind in ("first", "only"), kind in ("last", "only")
    if not start:
        carry, logs, *refs = refs
    outs = refs[len(refs) - SCRATCH - (1 if end else 2) : len(refs) - SCRATCH]
    kt, *work = refs[len(refs) - SCRATCH :]
    arrived = Arrived(owners, refs[: len(refs) - SCRATCH - len(outs)])
    chunks = arrived.chunks
    step = pl.program_id(0)
    index = owners * capacity
    needed = table[index + chunks * owners] if kind == "last" else None

    @pl.when(step == 0)
    def _():
        for c in range(chunks):
            for part, (owner, _) in enumerate(arrived.parts):
                if kind == "last":
                    at = table[index + c * owners + owner]
                    pl.when(at >= 0)(functools.partial(arrived.place, c, part, kt, at * PAIR))
                elif start and c == 0:
                    arrived.place(c, part, kt, owner * PAIR)
                else:
                    at = (c * (owners - 1) + owner + int(start)) * PAIR
                    pl.when(owner < owners - 1)(functools.partial(arrived.place, c, part, kt, at))
        if kind == "last":
            fill = jnp.int32(levels[-1])
            for level in reversed(levels[:-1]):
                fill = jnp.where(needed <= level, level, fill)

            @pl.loop(needed, fill)
            def _(i):
                kt[:, pl.ds(pl.multiple_of(i * PAIR, PAIR), PAIR)] = jnp.zeros((kt.shape[0], PAIR), kt.dtype)

    def attend(keys):
        diagonal = None
        if start:
            key = table[(owners - 1) * capacity] + lax.broadcasted_iota(jnp.int32, (1, PAIR), 1)
            diagonal = ((owners - 1) * PAIR, key, pos, step * (STEP // BLOCK))
        a = Half(0, q, kt, bias, *work[0::2], keys, diagonal)
        b = Half(SUB, q, kt, bias, *work[1::2], keys, diagonal)

        def before(part):
            part.settle(None if start else logs[pl.ds(part.base, SUB), :])

        def after(part):
            rows = pl.ds(part.base, SUB)
            total = part.total()
            if not start:
                kept = jnp.exp2(logs[rows, :] - part.tops[...])
                total = total + kept
            inverse = 1.0 / total
            part.sums[...] = inverse
            if not end:
                outs[1][rows, :] = part.tops[...] + jnp.log2(total)
            if not start:
                part.tops[...] = kept * inverse

        def combine(part, column):
            summed = part.combine(column)
            rows = pl.ds(part.base, SUB)
            for at in range(0, GROUP, PAIR):
                cols = slice(column + at, column + at + PAIR)
                result = summed[:, at : at + PAIR] * part.sums[...]
                if not start:
                    result = result + carry[rows, cols] * part.tops[...]
                outs[0][rows, cols] = result.astype(outs[0].dtype)

        run_halves(a, b, before, after, combine)

    if kind != "last":
        attend(kt.shape[1])
        return
    below = -1
    for level in levels:
        pl.when(jnp.logical_and(needed > below, needed <= level))(functools.partial(attend, level * PAIR))
        below = level


def attend(table, pos, q, bias, state, arrays, owners, capacity, kind, chunks):
    rows, lat = q.shape
    pairs = len(pair_places(owners, chunks, kind in ("first", "only")))
    keys = pairs * PAIR
    levels = [n for n in (4, 5, 6, 8) if n < pairs] + [pairs]
    out_shape = [jax.ShapeDtypeStruct((rows, KVL), jnp.float32), jax.ShapeDtypeStruct((rows, PAIR), jnp.float32)]
    if kind in ("last", "only"):
        out_shape = [jax.ShapeDtypeStruct((rows, KVL), jnp.bfloat16)]

    def whole(x):
        return pl.BlockSpec(x.shape, lambda i, *_: (0,) * x.ndim)

    def row_block(x):
        return pl.BlockSpec((STEP, x.shape[1]), lambda i, *_: (i, 0))

    return pl.pallas_call(
        functools.partial(attend_kernel, owners, capacity, kind, levels),
        out_shape=out_shape,
        grid_spec=pltpu.PrefetchScalarGridSpec(
            num_scalar_prefetch=2,
            grid=(rows // STEP,),
            in_specs=[row_block(q), whole(bias)] + [row_block(x) for x in state] + [whole(x) for x in arrays],
            out_specs=[row_block(x) for x in out_shape],
            scratch_shapes=[
                pltpu.VMEM((lat, keys), jnp.bfloat16),
                *[pltpu.VMEM((SUB, keys), jnp.float32)] * 2,
                *[pltpu.VMEM((SUB, keys), jnp.bfloat16)] * 2,
                *[pltpu.VMEM((SUB, PAIR), jnp.float32)] * 4,
            ],
        ),
        compiler_params=pltpu.CompilerParams(vmem_limit_bytes=VMEM),
        cost_estimate=pl.CostEstimate(
            flops=2 * rows * keys * (lat + KVL), bytes_accessed=rows * (lat + 2 * KVL) * 2, transcendentals=rows * keys
        ),
        name="attend_" + kind,
    )(table, pos, q, bias, *state, *arrays)


def split_phases(chunks):
    cut = (chunks + 1) // 2
    return [phase for phase in (list(range(cut)), list(range(cut, chunks))) if phase]


def local(queries, latent_cache, positions, block_ids):
    owners = lax.axis_size("ctx")
    capacity = max(2, 2 * SEL // owners)
    shift = log2(latent_cache.shape[0] // BLOCK)
    q_rows, heads, lat = queries.shape
    rows = q_rows * heads
    lists = [block_ids] + [
        lax.ppermute(block_ids, "ctx", [(c, c ^ k) for c in range(owners)]) for k in range(1, owners)
    ]
    phases = split_phases(capacity // 2)
    packed = [pack(lists, latent_cache.T, capacity, phase) for phase in phases]
    table, *biases = plan(block_ids[0], owners, capacity, shift, phases)
    steps = partners(owners) + [(owners - 1, owners - 1)]

    def send(own):
        got = []
        for x, ks in zip(own, steps):
            moves = [(2 * c + h, 2 * (c ^ k) + h) for c in range(owners) for h, k in enumerate(ks)]
            got.append(lax.ppermute(x, ("ctx", "head"), moves))
        return got

    def swap(got):
        return [lax.ppermute(x, "head", [(0, 1), (1, 0)]) for x in got]

    q = queries.reshape(rows, lat)
    got = [send(packed[0])]
    for own in packed[1:]:
        both = lax.optimization_barrier((*got[-1], *own[:-1], table))
        got[-1], own[:-1], table = list(both[: len(got[-1])]), both[len(got[-1]) : -1], both[-1]
        got.append(send(own))
    state = []
    for p, phase in enumerate(phases):
        late = got[p]
        if state:
            *late, logs = lax.optimization_barrier((*late, state[1]))
            state = [state[0], logs]
        arrays = [*late, packed[p][-1], *swap(late)]
        kind = "only" if len(phases) == 1 else "first" if p == 0 else "last" if p == len(phases) - 1 else "middle"
        state = attend(table, positions, q, biases[p], state, arrays, owners, capacity, kind, len(phase))
    return state[0].reshape(q_rows, heads, KVL)


def solution(mesh):
    return jax.shard_map(
        local,
        mesh=mesh,
        in_specs=(
            P(("groups", "ctx"), "head", None),
            P(("groups", "ctx"), None),
            P(("groups", "ctx")),
            P(("groups", "ctx"), None),
        ),
        out_specs=P(("groups", "ctx"), "head", None),
        check_vma=False,
    )
```

```python
import functools

import jax
import jax.numpy as jnp
from jax import lax
from jax.experimental import pallas as pl
from jax.experimental.pallas import tpu as pltpu
from jax.sharding import PartitionSpec as P

KVL = 512
BLOCK = 64
SEL = 32
PAIR = 2 * BLOCK
GROUP = 2 * PAIR
VMEM = 60 << 20
NEG = -1e30
SCALE = 1.4426950408889634 / 192.0**0.5
NT = (((1,), (1,)), ((), ()))
NN = (((1,), (0,)), ((), ()))


def log2(n):
    shift = n.bit_length() - 1
    assert 1 << shift == n
    return shift


def partners(owners):
    count = (owners - 2) // 2
    low, high = range(1, count + 1), range(count + 1, 2 * count + 1)
    return [(a, b) if i % 2 == 0 else (b, a) for i, (a, b) in enumerate(zip(low, high))]


def pack_kernel(capacity, chunks, ids, cache, *refs):
    dests = ids.shape[0]
    pairs = partners(dests)
    outs = refs[: len(pairs) + 2]
    table, rows, sem = refs[len(pairs) + 2 :]
    lat, tokens = rows.shape
    half = lat // 2
    shift = log2(tokens // BLOCK)
    head = lax.axis_index("head")
    me = lax.axis_index("ctx")
    copy = pltpu.make_async_copy(cache, rows, sem)
    copy.start()
    for k in range(dests):
        at = jnp.int32(k * (capacity + 1))
        for slot in range(capacity + 1):
            table[k * (capacity + 1) + slot] = 0
        for j in range(SEL):
            block = ids[me ^ k, j]
            table[at] = block & ((1 << shift) - 1)
            at = at + (block >> shift == me).astype(jnp.int32)
        table[at] = 0

    def block_pair(k, chunk, start, size):
        first = k * (capacity + 1) + 2 * chunk
        a, b = table[first], table[first + 1]
        left = lax.broadcasted_iota(jnp.int32, (size, PAIR), 1) < BLOCK
        xa = rows[pl.ds(start, size), pl.ds(pl.multiple_of((a >> 1) * PAIR, PAIR), PAIR)].astype(jnp.float32)
        xb = rows[pl.ds(start, size), pl.ds(pl.multiple_of((b >> 1) * PAIR, PAIR), PAIR)].astype(jnp.float32)
        xa = pltpu.roll(xa, (a & 1) * BLOCK, 1)
        xb = pltpu.roll(xb, (1 - (b & 1)) * BLOCK, 1)
        return jnp.where(left, xa, xb).astype(jnp.bfloat16)

    copy.wait()
    for c, chunk in enumerate(chunks):
        for j, (a, b) in enumerate(pairs):
            outs[j][c] = block_pair(jnp.where(head == 0, a, b), chunk, 0, lat)
        outs[-2][c] = block_pair(dests - 1, chunk, pl.multiple_of(head * half, 32), half)
        outs[-1][c] = block_pair(0, chunk, 0, lat)


def pack(ids, cache_t, capacity, chunks):
    dests = ids.shape[0]
    lat, tokens = cache_t.shape
    sizes = [lat] * len(partners(dests)) + [lat // 2, lat]
    shapes = [(len(chunks), size, PAIR) for size in sizes]

    packed = pl.pallas_call(
        functools.partial(pack_kernel, capacity, chunks),
        out_shape=[jax.ShapeDtypeStruct(s, jnp.bfloat16) for s in shapes],
        grid_spec=pltpu.PrefetchScalarGridSpec(
            num_scalar_prefetch=1,
            grid=(1,),
            in_specs=[pl.BlockSpec(memory_space=pl.ANY)],
            out_specs=[pl.BlockSpec(s, lambda i, *_: (0, 0, 0)) for s in shapes],
            scratch_shapes=[
                pltpu.SMEM((dests * (capacity + 1),), jnp.int32),
                pltpu.VMEM((lat, tokens), jnp.bfloat16),
                pltpu.SemaphoreType.DMA,
            ],
        ),
        compiler_params=pltpu.CompilerParams(vmem_limit_bytes=VMEM),
        cost_estimate=pl.CostEstimate(flops=0, bytes_accessed=8 * lat * tokens, transcendentals=0),
        name="pack",
    )(ids, cache_t)
    return list(packed)


def pair_bias(bias, at, start_a, start_b):
    lane = lax.broadcasted_iota(jnp.int32, (8, PAIR), 1)
    start = jnp.where(lane < BLOCK, start_a, start_b)
    bias[:, pl.ds(at, PAIR)] = jnp.where(start >= 0, 0.0, NEG).astype(jnp.float32)


def pair_places(owners, phase, first):
    return {
        (c, o): i
        for i, (c, o) in enumerate((c, o) for c in range(phase) for o in range(owners) if o < owners - 1 or first and c == 0)
    }


def plan_kernel(owners, capacity, shift, phases, ids, table, *rest):
    biases, count = rest[:-1], rest[-1]
    for slot in range(owners * capacity):
        table[slot] = -1
    for o in range(owners):
        count[o] = 0
    for j in range(SEL):
        block = ids[j]
        owner = block >> shift
        rank = count[owner]
        table[owner * capacity + rank] = block * BLOCK
        count[owner] = rank + 1
    for p, (bias, phase) in enumerate(zip(biases, phases)):
        last = p > 0 and p == len(phases) - 1
        if last:
            bias[...] = jnp.full(bias.shape, NEG, bias.dtype)
            live = jnp.int32(0)
        for (c, o), i in pair_places(owners, len(phase), p == 0).items():
            slot = o * capacity + 2 * phase[c]
            a, b = table[slot], table[slot + 1]
            if last:
                used = a >= 0
                table[owners * capacity + c * owners + o] = jnp.where(used, live, -1)
                pair_bias(bias, pl.multiple_of(live * PAIR, PAIR), a, b)
                live = live + used.astype(jnp.int32)
            else:
                pair_bias(bias, i * PAIR, a, b)
        if last:
            for c in range(len(phase)):
                table[owners * capacity + c * owners + owners - 1] = -1
            table[owners * capacity + len(phase) * owners] = live


def plan(ids, owners, capacity, shift, phases):
    shapes = [(8, len(pair_places(owners, len(phase), p == 0)) * PAIR) for p, phase in enumerate(phases)]
    if len(phases) > 1:
        shapes[-1] = (8, shapes[-1][1] + PAIR)
    entries = owners * capacity + len(phases[-1]) * owners + 1
    return pl.pallas_call(
        functools.partial(plan_kernel, owners, capacity, shift, phases),
        out_shape=[jax.ShapeDtypeStruct((entries,), jnp.int32)]
        + [jax.ShapeDtypeStruct(s, jnp.float32) for s in shapes],
        grid_spec=pltpu.PrefetchScalarGridSpec(
            num_scalar_prefetch=1,
            grid=(1,),
            in_specs=[],
            out_specs=[pl.BlockSpec(memory_space=pltpu.SMEM)] + [pl.BlockSpec(s, lambda i, ids: (0, 0)) for s in shapes],
            scratch_shapes=[pltpu.SMEM((owners,), jnp.int32)],
        ),
        cost_estimate=pl.CostEstimate(flops=0, bytes_accessed=1 << 20, transcendentals=0),
        name="plan",
    )(ids)


class Arrived:
    def __init__(self, owners, arrays):
        pairs = partners(owners)
        count = len(pairs)
        head, me = lax.axis_index("head"), lax.axis_index("ctx")
        got, shared, own = arrays[:count], arrays[count], arrays[count + 1]
        swapped, shared_other = arrays[count + 2 : 2 * count + 2], arrays[2 * count + 2]
        self.chunks, lat, _ = own.shape
        half = lat // 2
        self.parts = [(me, [(own, 0, lat)])]
        for (a, b), x, y in zip(pairs, got, swapped):
            self.parts.append((me ^ jnp.where(head == 0, a, b), [(x, 0, lat)]))
            self.parts.append((me ^ jnp.where(head == 0, b, a), [(y, 0, lat)]))
        split = [(x, pl.multiple_of(h * half, 32), half) for x, h in ((shared, head), (shared_other, 1 - head))]
        self.parts.append((me ^ (owners - 1), split))

    def place(self, chunk, part, kt, at):
        for x, start, size in self.parts[part][1]:
            kt[pl.ds(start, size), pl.ds(pl.multiple_of(at, PAIR), PAIR)] = x[chunk]


class Half:
    def __init__(self, base, q, kt, bias, scores, weights, tops, sums, keys, diagonal=None):
        self.base, self.q, self.kt, self.bias = base, q, kt, bias
        self.scores, self.weights, self.tops, self.sums = scores, weights, tops, sums
        self.keys, self.diagonal = keys, diagonal
        self.groups = -(-keys // GROUP)
        self.size = scores.shape[0]

    def score(self, group):
        at = group * GROUP
        end = min(at + GROUP, self.keys)
        part = lax.dot_general(
            self.q[pl.ds(self.base, self.size), :], self.kt[:, at:end], NN, preferred_element_type=jnp.float32
        )
        part = part + self.bias[0:1, at:end]
        columns = [part[:, c : c + PAIR] for c in range(0, end - at, PAIR)]
        if self.diagonal is not None:
            where, key, pos, first = self.diagonal
            if at <= where < end:
                seen = jnp.concatenate(
                    [
                        jnp.broadcast_to(key, (BLOCK, PAIR)) <= pos[first + self.base // BLOCK + s]
                        for s in range(self.size // BLOCK)
                    ],
                    axis=0,
                )
                index = (where - at) // PAIR
                columns[index] = jnp.where(seen, columns[index], NEG)
        high = columns[0]
        for i, column in enumerate(columns):
            self.scores[:, at + i * PAIR : at + (i + 1) * PAIR] = column
            high = jnp.maximum(high, column) if i else high
        self.tops[...] = high if group == 0 else jnp.maximum(self.tops[...], high)

    def settle(self, old=None):
        top = jnp.max(self.tops[...], axis=1, keepdims=True) * SCALE
        top = jnp.broadcast_to(top, (self.size, PAIR))
        self.tops[...] = top if old is None else jnp.maximum(top, old)

    def weigh(self, slab):
        rows = pl.ds(slab * BLOCK, BLOCK)
        top = self.tops[rows, :]
        total = jnp.zeros((BLOCK, PAIR), jnp.float32)
        for at in range(0, self.keys, PAIR):
            part = jnp.exp2(self.scores[rows, at : at + PAIR] * SCALE - top)
            total = total + part
            self.weights[rows, at : at + PAIR] = part.astype(jnp.bfloat16)
        self.sums[rows, :] = total

    def total(self):
        return jnp.broadcast_to(jnp.sum(self.sums[...], axis=1, keepdims=True), (self.size, PAIR))

    def combine(self, column):
        return lax.dot_general(
            self.weights[:, 0 : self.keys],
            self.kt[column : column + GROUP, 0 : self.keys],
            NT,
            preferred_element_type=jnp.float32,
        )


def run_halves(a, b, before, after, combine):
    slabs = a.size // BLOCK
    for g in range(a.groups):
        a.score(g)
    before(a)
    for i in range(max(a.groups, slabs)):
        if i < b.groups:
            b.score(i)
        if i < slabs:
            a.weigh(i)
    before(b)
    after(a)
    for i, column in enumerate(range(0, KVL, GROUP)):
        combine(a, column)
        for s in range(i * slabs // 2, (i + 1) * slabs // 2):
            b.weigh(s)
    after(b)
    for column in range(0, KVL, GROUP):
        combine(b, column)


SCRATCH = 9


def attend_kernel(owners, capacity, kind, levels, table, pos, q, bias, *refs):
    start, end = kind in ("first", "only"), kind in ("last", "only")
    if not start:
        carry, logs, *refs = refs
    outs = refs[len(refs) - SCRATCH - (1 if end else 2) : len(refs) - SCRATCH]
    kt, *work = refs[len(refs) - SCRATCH :]
    arrived = Arrived(owners, refs[: len(refs) - SCRATCH - len(outs)])
    chunks = arrived.chunks
    step = pl.program_id(0)
    sub = work[0].shape[0]
    index = owners * capacity
    needed = table[index + chunks * owners] if kind == "last" else None

    @pl.when(step == 0)
    def _():
        for c in range(chunks):
            for part, (owner, _) in enumerate(arrived.parts):
                if kind == "last":
                    at = table[index + c * owners + owner]
                    pl.when(at >= 0)(functools.partial(arrived.place, c, part, kt, at * PAIR))
                elif start and c == 0:
                    arrived.place(c, part, kt, owner * PAIR)
                else:
                    at = (c * (owners - 1) + owner + int(start)) * PAIR
                    pl.when(owner < owners - 1)(functools.partial(arrived.place, c, part, kt, at))
        if kind == "last":
            fill = jnp.int32(levels[-1])
            for level in reversed(levels[:-1]):
                fill = jnp.where(needed <= level, level, fill)

            @pl.loop(needed, fill)
            def _(i):
                kt[:, pl.ds(pl.multiple_of(i * PAIR, PAIR), PAIR)] = jnp.zeros((kt.shape[0], PAIR), kt.dtype)

    def attend(keys):
        diagonal = None
        if start:
            key = table[(owners - 1) * capacity] + lax.broadcasted_iota(jnp.int32, (1, PAIR), 1)
            diagonal = ((owners - 1) * PAIR, key, pos, step * (2 * sub // BLOCK))
        a = Half(0, q, kt, bias, *work[0::2], keys, diagonal)
        b = Half(sub, q, kt, bias, *work[1::2], keys, diagonal)

        def before(part):
            part.settle(None if start else logs[pl.ds(part.base, sub), :])

        def after(part):
            rows = pl.ds(part.base, sub)
            total = part.total()
            if not start:
                kept = jnp.exp2(logs[rows, :] - part.tops[...])
                total = total + kept
            inverse = 1.0 / total
            part.sums[...] = inverse
            if not end:
                outs[1][rows, :] = part.tops[...] + jnp.log2(total)
            if not start:
                part.tops[...] = kept * inverse

        def combine(part, column):
            summed = part.combine(column)
            rows = pl.ds(part.base, sub)
            for at in range(0, GROUP, PAIR):
                cols = slice(column + at, column + at + PAIR)
                result = summed[:, at : at + PAIR] * part.sums[...]
                if not start:
                    result = result + carry[rows, cols] * part.tops[...]
                outs[0][rows, cols] = result.astype(outs[0].dtype)

        run_halves(a, b, before, after, combine)

    if kind != "last":
        attend(kt.shape[1])
        return
    below = -1
    for level in levels:
        pl.when(jnp.logical_and(needed > below, needed <= level))(functools.partial(attend, level * PAIR))
        below = level


def attend(table, pos, q, bias, state, arrays, owners, capacity, kind, chunks):
    rows, lat = q.shape
    pairs = len(pair_places(owners, chunks, kind in ("first", "only")))
    keys = pairs * PAIR
    levels = [n for n in (4, 5, 6, 8) if n < pairs] + [pairs]
    sub = 1024 if keys <= 2048 and rows % 2048 == 0 else 512
    step = 2 * sub
    out_shape = [jax.ShapeDtypeStruct((rows, KVL), jnp.float32), jax.ShapeDtypeStruct((rows, PAIR), jnp.float32)]
    if kind in ("last", "only"):
        out_shape = [jax.ShapeDtypeStruct((rows, KVL), jnp.bfloat16)]

    def whole(x):
        return pl.BlockSpec(x.shape, lambda i, *_: (0,) * x.ndim)

    def row_block(x):
        return pl.BlockSpec((step, x.shape[1]), lambda i, *_: (i, 0))

    return pl.pallas_call(
        functools.partial(attend_kernel, owners, capacity, kind, levels),
        out_shape=out_shape,
        grid_spec=pltpu.PrefetchScalarGridSpec(
            num_scalar_prefetch=2,
            grid=(rows // step,),
            in_specs=[row_block(q), whole(bias)] + [row_block(x) for x in state] + [whole(x) for x in arrays],
            out_specs=[row_block(x) for x in out_shape],
            scratch_shapes=[
                pltpu.VMEM((lat, keys), jnp.bfloat16),
                *[pltpu.VMEM((sub, keys), jnp.float32)] * 2,
                *[pltpu.VMEM((sub, keys), jnp.bfloat16)] * 2,
                *[pltpu.VMEM((sub, PAIR), jnp.float32)] * 4,
            ],
        ),
        compiler_params=pltpu.CompilerParams(vmem_limit_bytes=VMEM),
        cost_estimate=pl.CostEstimate(
            flops=2 * rows * keys * (lat + KVL), bytes_accessed=rows * (lat + 2 * KVL) * 2, transcendentals=rows * keys
        ),
        name="attend_" + kind,
    )(table, pos, q, bias, *state, *arrays)


def split_phases(chunks):
    cut = (chunks + 1) // 2
    return [phase for phase in (list(range(cut)), list(range(cut, chunks))) if phase]


def local(queries, latent_cache, positions, block_ids):
    owners = lax.axis_size("ctx")
    capacity = max(2, 2 * SEL // owners)
    shift = log2(latent_cache.shape[0] // BLOCK)
    q_rows, heads, lat = queries.shape
    rows = q_rows * heads
    lists = lax.all_to_all(
        jnp.broadcast_to(block_ids, (owners, SEL)), "ctx", split_axis=0, concat_axis=0, tiled=True
    )
    phases = split_phases(capacity // 2)
    packed = [pack(lists, latent_cache.T, capacity, phase) for phase in phases]
    table, *biases = plan(block_ids[0], owners, capacity, shift, phases)
    steps = partners(owners) + [(owners - 1, owners - 1)]

    def send(own):
        got = []
        for x, ks in zip(own, steps):
            moves = [(2 * c + h, 2 * (c ^ k) + h) for c in range(owners) for h, k in enumerate(ks)]
            got.append(lax.ppermute(x, ("ctx", "head"), moves))
        return got

    def swap(got):
        return [lax.ppermute(x, "head", [(0, 1), (1, 0)]) for x in got]

    q = queries.reshape(rows, lat)
    got = [send(packed[0])]
    for own in packed[1:]:
        both = lax.optimization_barrier((*got[-1], *own[:-1], table))
        got[-1], own[:-1], table = list(both[: len(got[-1])]), both[len(got[-1]) : -1], both[-1]
        got.append(send(own))
    state = []
    for p, phase in enumerate(phases):
        late = got[p]
        if state:
            *late, logs = lax.optimization_barrier((*late, state[1]))
            state = [state[0], logs]
        arrays = [*late, packed[p][-1], *swap(late)]
        kind = "only" if len(phases) == 1 else "first" if p == 0 else "last" if p == len(phases) - 1 else "middle"
        state = attend(table, positions, q, biases[p], state, arrays, owners, capacity, kind, len(phase))
    return state[0].reshape(q_rows, heads, KVL)


def solution(mesh):
    return jax.shard_map(
        local,
        mesh=mesh,
        in_specs=(
            P(("groups", "ctx"), "head", None),
            P(("groups", "ctx"), None),
            P(("groups", "ctx")),
            P(("groups", "ctx"), None),
        ),
        out_specs=P(("groups", "ctx"), "head", None),
        check_vma=False,
    )
```

```python
import functools

import jax
import jax.numpy as jnp
from jax import lax
from jax.experimental import pallas as pl
from jax.experimental.pallas import tpu as pltpu
from jax.sharding import PartitionSpec as P

KVL = 512
BLOCK = 64
SEL = 32
PAIR = 2 * BLOCK
SUB = 512
STEP = 2 * SUB
VMEM = 60 << 20
NEG = -1e30
SCALE = 1.4426950408889634 / 192.0**0.5
NT = (((1,), (1,)), ((), ()))
NN = (((1,), (0,)), ((), ()))


def log2(n):
    shift = n.bit_length() - 1
    assert 1 << shift == n
    return shift


def partners(owners):
    count = (owners - 2) // 2
    low, high = range(1, count + 1), range(count + 1, 2 * count + 1)
    return [(a, b) if i % 2 == 0 else (b, a) for i, (a, b) in enumerate(zip(low, high))]


def pack_kernel(capacity, chunks, ids, cache, *refs):
    dests = ids.shape[0]
    pairs = partners(dests)
    outs = refs[: len(pairs) + 2]
    table, rows, sem = refs[len(pairs) + 2 :]
    lat, tokens = rows.shape
    half = lat // 2
    shift = log2(tokens // BLOCK)
    head = lax.axis_index("head")
    me = lax.axis_index("ctx")
    copy = pltpu.make_async_copy(cache, rows, sem)
    copy.start()
    for k in range(dests):
        at = jnp.int32(k * (capacity + 1))
        for slot in range(capacity + 1):
            table[k * (capacity + 1) + slot] = 0
        for j in range(SEL):
            block = ids[me ^ k, j]
            table[at] = block & ((1 << shift) - 1)
            at = at + (block >> shift == me).astype(jnp.int32)
        table[at] = 0

    def block_pair(k, chunk, start, size):
        first = k * (capacity + 1) + 2 * chunk
        a, b = table[first], table[first + 1]
        left = lax.broadcasted_iota(jnp.int32, (size, PAIR), 1) < BLOCK
        xa = rows[pl.ds(start, size), pl.ds(pl.multiple_of((a >> 1) * PAIR, PAIR), PAIR)].astype(jnp.float32)
        xb = rows[pl.ds(start, size), pl.ds(pl.multiple_of((b >> 1) * PAIR, PAIR), PAIR)].astype(jnp.float32)
        xa = pltpu.roll(xa, (a & 1) * BLOCK, 1)
        xb = pltpu.roll(xb, (1 - (b & 1)) * BLOCK, 1)
        return jnp.where(left, xa, xb).astype(jnp.bfloat16)

    copy.wait()
    for c, chunk in enumerate(chunks):
        for j, (a, b) in enumerate(pairs):
            outs[j][c] = block_pair(jnp.where(head == 0, a, b), chunk, 0, lat)
        outs[-2][c] = block_pair(dests - 1, chunk, pl.multiple_of(head * half, 32), half)
        outs[-1][c] = block_pair(0, chunk, 0, lat)


def pack(ids, cache_t, capacity, chunks):
    dests = ids.shape[0]
    lat, tokens = cache_t.shape
    sizes = [lat] * len(partners(dests)) + [lat // 2, lat]
    shapes = [(len(chunks), size, PAIR) for size in sizes]

    packed = pl.pallas_call(
        functools.partial(pack_kernel, capacity, chunks),
        out_shape=[jax.ShapeDtypeStruct(s, jnp.bfloat16) for s in shapes],
        grid_spec=pltpu.PrefetchScalarGridSpec(
            num_scalar_prefetch=1,
            grid=(1,),
            in_specs=[pl.BlockSpec(memory_space=pl.ANY)],
            out_specs=[pl.BlockSpec(s, lambda i, *_: (0, 0, 0)) for s in shapes],
            scratch_shapes=[
                pltpu.SMEM((dests * (capacity + 1),), jnp.int32),
                pltpu.VMEM((lat, tokens), jnp.bfloat16),
                pltpu.SemaphoreType.DMA,
            ],
        ),
        compiler_params=pltpu.CompilerParams(vmem_limit_bytes=VMEM),
        cost_estimate=pl.CostEstimate(flops=0, bytes_accessed=8 * lat * tokens, transcendentals=0),
        name="pack",
    )(ids, cache_t)
    return list(packed)


def pair_bias(bias, at, start_a, start_b):
    lane = lax.broadcasted_iota(jnp.int32, (8, PAIR), 1)
    start = jnp.where(lane < BLOCK, start_a, start_b)
    bias[:, pl.ds(at, PAIR)] = jnp.where(start >= 0, 0.0, NEG).astype(jnp.float32)


def pair_places(owners, phase, first):
    pairs = [(c, o) for c in range(phase) for o in range(owners - 1)]
    if first:
        pairs.insert(0, (0, owners - 1))
    return {pair: i for i, pair in enumerate(pairs)}


def plan_kernel(owners, capacity, shift, phases, ids, table, *rest):
    biases, count = rest[:-1], rest[-1]
    for slot in range(owners * capacity):
        table[slot] = -1
    for o in range(owners):
        count[o] = 0
    for j in range(SEL):
        block = ids[j]
        owner = block >> shift
        rank = count[owner]
        table[owner * capacity + rank] = block * BLOCK
        count[owner] = rank + 1
    for p, (bias, phase) in enumerate(zip(biases, phases)):
        last = p > 0
        live = jnp.int32(0)
        bias[...] = jnp.full(bias.shape, NEG, bias.dtype)
        for (c, o), i in pair_places(owners, len(phase), p == 0).items():
            slot = o * capacity + 2 * phase[c]
            a, b = table[slot], table[slot + 1]
            if last:
                used = a >= 0
                table[owners * capacity + c * owners + o] = jnp.where(used, live, -1)
                pair_bias(bias, pl.multiple_of(live * PAIR, PAIR), a, b)
                live = live + used.astype(jnp.int32)
            else:
                pair_bias(bias, i * PAIR, a, b)
        if last:
            for c in range(len(phase)):
                table[owners * capacity + c * owners + owners - 1] = -1
            table[owners * capacity + len(phase) * owners] = live


def plan(ids, owners, capacity, shift, phases):
    shapes = []
    for p, phase in enumerate(phases):
        each = group_width(phase_kind(p, phases)) // PAIR
        pairs = len(pair_places(owners, len(phase), p == 0)) + int(p > 0)
        shapes.append((8, -(-pairs // each) * each * PAIR))
    entries = owners * capacity + len(phases[-1]) * owners + 1
    return pl.pallas_call(
        functools.partial(plan_kernel, owners, capacity, shift, phases),
        out_shape=[jax.ShapeDtypeStruct((entries,), jnp.int32)]
        + [jax.ShapeDtypeStruct(s, jnp.float32) for s in shapes],
        grid_spec=pltpu.PrefetchScalarGridSpec(
            num_scalar_prefetch=1,
            grid=(1,),
            in_specs=[],
            out_specs=[pl.BlockSpec(memory_space=pltpu.SMEM)] + [pl.BlockSpec(s, lambda i, ids: (0, 0)) for s in shapes],
            scratch_shapes=[pltpu.SMEM((owners,), jnp.int32)],
        ),
        cost_estimate=pl.CostEstimate(flops=0, bytes_accessed=1 << 20, transcendentals=0),
        name="plan",
    )(ids)


class Arrived:
    def __init__(self, owners, arrays):
        pairs = partners(owners)
        count = len(pairs)
        head, me = lax.axis_index("head"), lax.axis_index("ctx")
        got, shared, own = arrays[:count], arrays[count], arrays[count + 1]
        swapped, shared_other = arrays[count + 2 : 2 * count + 2], arrays[2 * count + 2]
        self.chunks, lat, _ = own.shape
        half = lat // 2
        self.parts = [(me, [(own, 0, lat)])]
        for (a, b), x, y in zip(pairs, got, swapped):
            self.parts.append((me ^ jnp.where(head == 0, a, b), [(x, 0, lat)]))
            self.parts.append((me ^ jnp.where(head == 0, b, a), [(y, 0, lat)]))
        split = [(x, pl.multiple_of(h * half, 32), half) for x, h in ((shared, head), (shared_other, 1 - head))]
        self.parts.append((me ^ (owners - 1), split))

    def place(self, chunk, part, kt, at):
        for x, start, size in self.parts[part][1]:
            kt[pl.ds(start, size), pl.ds(pl.multiple_of(at, PAIR), PAIR)] = x[chunk]


class Half:
    def __init__(self, base, q, kt, bias, width, scores, weights, tops, sums, acc):
        self.base, self.q, self.kt, self.bias, self.width = base, q, kt, bias, width
        self.scores, self.weights, self.tops, self.sums, self.acc = scores, weights, tops, sums, acc

    def start(self):
        self.tops[...] = jnp.full(self.tops.shape, NEG, jnp.float32)
        self.sums[...] = jnp.zeros(self.sums.shape, jnp.float32)
        self.acc[...] = jnp.zeros(self.acc.shape, jnp.float32)

    def group(self, g):
        return pl.multiple_of(g * self.width, self.width)

    def score(self, g, visible=None):
        at = self.group(g)
        part = lax.dot_general(
            self.q[pl.ds(self.base, SUB), :],
            self.kt[:, pl.ds(at, self.width)],
            NN,
            preferred_element_type=jnp.float32,
        )
        part = part + self.bias[0:1, pl.ds(at, self.width)]
        high = self.tops[...]
        for c in range(0, self.width, PAIR):
            column = part[:, c : c + PAIR]
            if c == 0 and visible is not None:
                column = visible(g, self.base, column)
            self.scores[:, pl.ds(at + c, PAIR)] = column
            high = jnp.maximum(high, column)
        self.tops[...] = high

    def settle(self, old=None):
        top = jnp.max(self.tops[...], axis=1, keepdims=True) * SCALE
        top = jnp.broadcast_to(top, (SUB, PAIR))
        self.tops[...] = top if old is None else jnp.maximum(top, old)

    def weigh(self, g):
        at = self.group(g)
        for slab in range(0, SUB, BLOCK):
            rows = pl.ds(slab, BLOCK)
            top = self.tops[rows, :]
            total = self.sums[rows, :]
            for c in range(0, self.width, PAIR):
                part = jnp.exp2(self.scores[rows, pl.ds(at + c, PAIR)] * SCALE - top)
                total = total + part
                self.weights[rows, pl.ds(at + c, PAIR)] = part.astype(jnp.bfloat16)
            self.sums[rows, :] = total

    def total(self):
        return jnp.broadcast_to(jnp.sum(self.sums[...], axis=1, keepdims=True), (SUB, PAIR))

    def combine(self, g):
        at = self.group(g)
        self.acc[...] += lax.dot_general(
            self.weights[:, pl.ds(at, self.width)],
            self.kt[0:KVL, pl.ds(at, self.width)],
            NT,
            preferred_element_type=jnp.float32,
        )


def run_halves(a, b, groups, visible, before, after, finish):
    a.start()
    b.start()

    @pl.loop(0, groups)
    def _(g):
        a.score(g, visible)

    before(a)

    @pl.loop(0, groups)
    def _(g):
        a.weigh(g)
        b.score(g, visible)

    before(b)
    after(a)

    @pl.loop(0, groups)
    def _(g):
        b.weigh(g)
        a.combine(g)

    after(b)

    @pl.loop(0, groups)
    def _(g):
        b.combine(g)

    finish(a)
    finish(b)


SCRATCH = 11


def attend_kernel(owners, capacity, kind, width, table, pos, q, bias, *refs):
    start, end = kind in ("first", "only"), kind in ("last", "only")
    if not start:
        carry, logs, *refs = refs
    outs = refs[len(refs) - SCRATCH - (1 if end else 2) : len(refs) - SCRATCH]
    kt, *work = refs[len(refs) - SCRATCH :]
    arrived = Arrived(owners, refs[: len(refs) - SCRATCH - len(outs)])
    chunks = arrived.chunks
    step = pl.program_id(0)
    index = owners * capacity
    each = width // PAIR
    if start:
        needed = len(pair_places(owners, chunks, True))
        groups = kt.shape[1] // width
    else:
        needed = table[index + chunks * owners]
        groups = (needed + each - 1) // each

    @pl.when(step == 0)
    def _():
        for c in range(chunks):
            for part, (owner, _) in enumerate(arrived.parts):
                if not start:
                    at = table[index + c * owners + owner]
                    pl.when(at >= 0)(functools.partial(arrived.place, c, part, kt, at * PAIR))
                elif c == 0:
                    arrived.place(c, part, kt, lax.rem(owner + 1, owners) * PAIR)
                else:
                    at = (c * (owners - 1) + owner + 1) * PAIR
                    pl.when(owner < owners - 1)(functools.partial(arrived.place, c, part, kt, at))

        @pl.loop(needed, groups * each)
        def _(i):
            kt[:, pl.ds(pl.multiple_of(i * PAIR, PAIR), PAIR)] = jnp.zeros((kt.shape[0], PAIR), kt.dtype)

    visible = None
    if start:
        own = table[(owners - 1) * capacity] + lax.broadcasted_iota(jnp.int32, (1, PAIR), 1)

        def visible(g, base, column):
            key = jnp.broadcast_to(jnp.where(g == 0, own, 0), (BLOCK, PAIR))
            first = (step * STEP + base) // BLOCK
            slabs = [
                jnp.where(key <= pos[first + s], column[s * BLOCK : (s + 1) * BLOCK], NEG) for s in range(SUB // BLOCK)
            ]
            return jnp.concatenate(slabs, axis=0)

    a = Half(0, q, kt, bias, width, *work[0::2])
    b = Half(SUB, q, kt, bias, width, *work[1::2])

    def before(part):
        part.settle(None if start else logs[pl.ds(part.base, SUB), :])

    def after(part):
        rows = pl.ds(part.base, SUB)
        total = part.total()
        if not start:
            kept = jnp.exp2(logs[rows, :] - part.tops[...])
            total = total + kept
        inverse = 1.0 / total
        part.sums[...] = inverse
        if not end:
            outs[1][rows, :] = part.tops[...] + jnp.log2(total)
        if not start:
            part.tops[...] = kept * inverse

    def finish(part):
        @pl.loop(0, SUB // BLOCK)
        def _(s):
            here = pl.ds(pl.multiple_of(s * BLOCK, BLOCK), BLOCK)
            rows = pl.ds(pl.multiple_of(part.base + s * BLOCK, BLOCK), BLOCK)
            for at in range(0, KVL, PAIR):
                cols = slice(at, at + PAIR)
                result = part.acc[here, cols] * part.sums[here, :]
                if not start:
                    result = result + carry[rows, cols] * part.tops[here, :]
                outs[0][rows, cols] = result.astype(outs[0].dtype)

    run_halves(a, b, groups, visible, before, after, finish)


def attend(table, pos, q, bias, state, arrays, owners, capacity, kind):
    rows, lat = q.shape
    keys = bias.shape[1]
    width = group_width(kind)
    out_shape = [jax.ShapeDtypeStruct((rows, KVL), jnp.float32), jax.ShapeDtypeStruct((rows, PAIR), jnp.float32)]
    if kind in ("last", "only"):
        out_shape = [jax.ShapeDtypeStruct((rows, KVL), jnp.bfloat16)]

    def whole(x):
        return pl.BlockSpec(x.shape, lambda i, *_: (0,) * x.ndim)

    def row_block(x):
        return pl.BlockSpec((STEP, x.shape[1]), lambda i, *_: (i, 0))

    return pl.pallas_call(
        functools.partial(attend_kernel, owners, capacity, kind, width),
        out_shape=out_shape,
        grid_spec=pltpu.PrefetchScalarGridSpec(
            num_scalar_prefetch=2,
            grid=(rows // STEP,),
            in_specs=[row_block(q), whole(bias)] + [row_block(x) for x in state] + [whole(x) for x in arrays],
            out_specs=[row_block(x) for x in out_shape],
            scratch_shapes=[
                pltpu.VMEM((lat, keys), jnp.bfloat16),
                *[pltpu.VMEM((SUB, keys), jnp.float32)] * 2,
                *[pltpu.VMEM((SUB, keys), jnp.bfloat16)] * 2,
                *[pltpu.VMEM((SUB, PAIR), jnp.float32)] * 4,
                *[pltpu.VMEM((SUB, KVL), jnp.float32)] * 2,
            ],
        ),
        compiler_params=pltpu.CompilerParams(vmem_limit_bytes=VMEM),
        cost_estimate=pl.CostEstimate(
            flops=2 * rows * keys * (lat + KVL), bytes_accessed=rows * (lat + 2 * KVL) * 2, transcendentals=rows * keys
        ),
        name="attend_" + kind,
    )(table, pos, q, bias, *state, *arrays)


def phase_kind(p, phases):
    return "only" if len(phases) == 1 else "first" if p == 0 else "last"


def group_width(kind):
    return 2 * PAIR if kind == "last" else 4 * PAIR


def split_phases(chunks):
    cut = (chunks + 1) // 2
    return [phase for phase in (list(range(cut)), list(range(cut, chunks))) if phase]


def local(queries, latent_cache, positions, block_ids):
    owners = lax.axis_size("ctx")
    capacity = max(2, 2 * SEL // owners)
    shift = log2(latent_cache.shape[0] // BLOCK)
    q_rows, heads, lat = queries.shape
    rows = q_rows * heads
    lists = lax.all_to_all(
        jnp.broadcast_to(block_ids, (owners, SEL)), "ctx", split_axis=0, concat_axis=0, tiled=True
    )
    phases = split_phases(capacity // 2)
    packed = [pack(lists, latent_cache.T, capacity, phase) for phase in phases]
    table, *biases = plan(block_ids[0], owners, capacity, shift, phases)
    steps = partners(owners) + [(owners - 1, owners - 1)]

    def send(own):
        got = []
        for x, ks in zip(own, steps):
            moves = [(2 * c + h, 2 * (c ^ k) + h) for c in range(owners) for h, k in enumerate(ks)]
            got.append(lax.ppermute(x, ("ctx", "head"), moves))
        return got

    def swap(got):
        return [lax.ppermute(x, "head", [(0, 1), (1, 0)]) for x in got]

    q = queries.reshape(rows, lat)
    got = [send(packed[0])]
    for own in packed[1:]:
        both = lax.optimization_barrier((*got[-1], *own[:-1], table))
        got[-1], own[:-1], table = list(both[: len(got[-1])]), both[len(got[-1]) : -1], both[-1]
        got.append(send(own))
    state = []
    for p, phase in enumerate(phases):
        late = got[p]
        if state:
            *late, logs = lax.optimization_barrier((*late, state[1]))
            state = [state[0], logs]
        arrays = [*late, packed[p][-1], *swap(late)]
        kind = phase_kind(p, phases)
        state = attend(table, positions, q, biases[p], state, arrays, owners, capacity, kind)
    return state[0].reshape(q_rows, heads, KVL)


def solution(mesh):
    return jax.shard_map(
        local,
        mesh=mesh,
        in_specs=(
            P(("groups", "ctx"), "head", None),
            P(("groups", "ctx"), None),
            P(("groups", "ctx")),
            P(("groups", "ctx"), None),
        ),
        out_specs=P(("groups", "ctx"), "head", None),
        check_vma=False,
    )
```

```python
import functools

import jax
import jax.numpy as jnp
from jax import lax
from jax.experimental import pallas as pl
from jax.experimental.pallas import tpu as pltpu
from jax.sharding import PartitionSpec as P

KVL = 512
BLOCK = 64
SEL = 32
PAIR = 2 * BLOCK
GROUP = 2 * PAIR
VMEM = 60 << 20
NEG = -1e30
SCALE = 1.4426950408889634 / 192.0**0.5
NT = (((1,), (1,)), ((), ()))
NN = (((1,), (0,)), ((), ()))


def log2(n):
    shift = n.bit_length() - 1
    assert 1 << shift == n
    return shift


def partners(owners):
    count = (owners - 2) // 2
    low, high = range(1, count + 1), range(count + 1, 2 * count + 1)
    return [(a, b) if i % 2 == 0 else (b, a) for i, (a, b) in enumerate(zip(low, high))]


def pack_kernel(capacity, chunks, spread, ids, cache, *refs):
    dests = ids.shape[0]
    pairs = partners(dests)
    outs, (table, rows, sem) = refs[:-3], refs[-3:]
    lat, tokens = rows.shape
    half = lat // 2
    shift = log2(tokens // BLOCK)
    head = lax.axis_index("head")
    me = lax.axis_index("ctx")
    copy = pltpu.make_async_copy(cache, rows, sem)
    copy.start()
    for k in range(dests):
        at = jnp.int32(k * (capacity + 1))
        for slot in range(capacity + 1):
            table[k * (capacity + 1) + slot] = 0
        for j in range(SEL):
            block = ids[k if spread else me ^ k, j]
            table[at] = block & ((1 << shift) - 1)
            at = at + (block >> shift == me).astype(jnp.int32)
        table[at] = 0

    def block_pair(k, chunk, start, size):
        first = k * (capacity + 1) + 2 * chunk
        a, b = table[first], table[first + 1]
        left = lax.broadcasted_iota(jnp.int32, (size, PAIR), 1) < BLOCK
        xa = rows[pl.ds(start, size), pl.ds(pl.multiple_of((a >> 1) * PAIR, PAIR), PAIR)].astype(jnp.float32)
        xb = rows[pl.ds(start, size), pl.ds(pl.multiple_of((b >> 1) * PAIR, PAIR), PAIR)].astype(jnp.float32)
        xa = pltpu.roll(xa, (a & 1) * BLOCK, 1)
        xb = pltpu.roll(xb, (1 - (b & 1)) * BLOCK, 1)
        return jnp.where(left, xa, xb).astype(jnp.bfloat16)

    copy.wait()
    if spread:
        for c, chunk in enumerate(chunks):
            for d in range(dests):
                outs[0][d, c] = block_pair(d, chunk, pl.multiple_of(head * half, 32), half)
        return
    for c, chunk in enumerate(chunks):
        for j, (a, b) in enumerate(pairs):
            outs[j][c] = block_pair(jnp.where(head == 0, a, b), chunk, 0, lat)
        outs[-2][c] = block_pair(dests - 1, chunk, pl.multiple_of(head * half, 32), half)
        outs[-1][c] = block_pair(0, chunk, 0, lat)


def pack(ids, cache_t, capacity, chunks, spread=False):
    dests = ids.shape[0]
    lat, tokens = cache_t.shape
    sizes = [lat] * len(partners(dests)) + [lat // 2, lat]
    shapes = [(len(chunks), size, PAIR) for size in sizes]
    if spread:
        shapes = [(dests, len(chunks), lat // 2, PAIR)]

    packed = pl.pallas_call(
        functools.partial(pack_kernel, capacity, chunks, spread),
        out_shape=[jax.ShapeDtypeStruct(s, jnp.bfloat16) for s in shapes],
        grid_spec=pltpu.PrefetchScalarGridSpec(
            num_scalar_prefetch=1,
            grid=(1,),
            in_specs=[pl.BlockSpec(memory_space=pl.ANY)],
            out_specs=[pl.BlockSpec(s, lambda i, *_, n=len(s): (0,) * n) for s in shapes],
            scratch_shapes=[
                pltpu.SMEM((dests * (capacity + 1),), jnp.int32),
                pltpu.VMEM((lat, tokens), jnp.bfloat16),
                pltpu.SemaphoreType.DMA,
            ],
        ),
        compiler_params=pltpu.CompilerParams(vmem_limit_bytes=VMEM),
        cost_estimate=pl.CostEstimate(flops=0, bytes_accessed=8 * lat * tokens, transcendentals=0),
        name="pack",
    )(ids, cache_t)
    return list(packed)


def pair_bias(bias, at, start_a, start_b):
    lane = lax.broadcasted_iota(jnp.int32, (8, PAIR), 1)
    start = jnp.where(lane < BLOCK, start_a, start_b)
    bias[:, pl.ds(at, PAIR)] = jnp.where(start >= 0, 0.0, NEG).astype(jnp.float32)


def pair_places(owners, phase, first):
    return {
        (c, o): i
        for i, (c, o) in enumerate((c, o) for c in range(phase) for o in range(owners) if o < owners - 1 or first and c == 0)
    }


def plan_kernel(owners, capacity, shift, phases, ids, table, *rest):
    biases, count = rest[:-1], rest[-1]
    for slot in range(owners * capacity):
        table[slot] = -1
    for o in range(owners):
        count[o] = 0
    for j in range(SEL):
        block = ids[j]
        owner = block >> shift
        rank = count[owner]
        table[owner * capacity + rank] = block * BLOCK
        count[owner] = rank + 1
    for p, (bias, phase) in enumerate(zip(biases, phases)):
        last = p > 0 and p == len(phases) - 1
        if last:
            bias[...] = jnp.full(bias.shape, NEG, bias.dtype)
            live = jnp.int32(0)
        for (c, o), i in pair_places(owners, len(phase), p == 0).items():
            slot = o * capacity + 2 * phase[c]
            a, b = table[slot], table[slot + 1]
            if last:
                used = a >= 0
                table[owners * capacity + c * owners + o] = jnp.where(used, live, -1)
                pair_bias(bias, pl.multiple_of(live * PAIR, PAIR), a, b)
                live = live + used.astype(jnp.int32)
            else:
                pair_bias(bias, i * PAIR, a, b)
        if last:
            for c in range(len(phase)):
                table[owners * capacity + c * owners + owners - 1] = -1
            table[owners * capacity + len(phase) * owners] = live


def plan(ids, owners, capacity, shift, phases):
    shapes = [(8, len(pair_places(owners, len(phase), p == 0)) * PAIR) for p, phase in enumerate(phases)]
    if len(phases) > 1:
        shapes[-1] = (8, shapes[-1][1] + PAIR)
    entries = owners * capacity + len(phases[-1]) * owners + 1
    return pl.pallas_call(
        functools.partial(plan_kernel, owners, capacity, shift, phases),
        out_shape=[jax.ShapeDtypeStruct((entries,), jnp.int32)]
        + [jax.ShapeDtypeStruct(s, jnp.float32) for s in shapes],
        grid_spec=pltpu.PrefetchScalarGridSpec(
            num_scalar_prefetch=1,
            grid=(1,),
            in_specs=[],
            out_specs=[pl.BlockSpec(memory_space=pltpu.SMEM)] + [pl.BlockSpec(s, lambda i, ids: (0, 0)) for s in shapes],
            scratch_shapes=[pltpu.SMEM((owners,), jnp.int32)],
        ),
        cost_estimate=pl.CostEstimate(flops=0, bytes_accessed=1 << 20, transcendentals=0),
        name="plan",
    )(ids)


class Arrived:
    def __init__(self, owners, arrays):
        pairs = partners(owners)
        count = len(pairs)
        head, me = lax.axis_index("head"), lax.axis_index("ctx")
        if len(arrays) == 2:
            _, self.chunks, half, _ = arrays[0].shape
            starts = [pl.multiple_of(h * half, 32) for h in (head, 1 - head)]
            self.parts = [
                (o, [(x.at[o], start, half) for x, start in zip(arrays, starts)]) for o in range(owners)
            ]
            return
        got, shared, own = arrays[:count], arrays[count], arrays[count + 1]
        swapped, shared_other = arrays[count + 2 : 2 * count + 2], arrays[2 * count + 2]
        self.chunks, lat, _ = own.shape
        half = lat // 2
        self.parts = [(me, [(own, 0, lat)])]
        for (a, b), x, y in zip(pairs, got, swapped):
            self.parts.append((me ^ jnp.where(head == 0, a, b), [(x, 0, lat)]))
            self.parts.append((me ^ jnp.where(head == 0, b, a), [(y, 0, lat)]))
        split = [(x, pl.multiple_of(h * half, 32), half) for x, h in ((shared, head), (shared_other, 1 - head))]
        self.parts.append((me ^ (owners - 1), split))

    def place(self, chunk, part, kt, at):
        for x, start, size in self.parts[part][1]:
            kt[pl.ds(start, size), pl.ds(pl.multiple_of(at, PAIR), PAIR)] = x[chunk]


class Half:
    def __init__(self, base, q, kt, bias, scores, weights, tops, sums, keys, diagonal=None):
        self.base, self.q, self.kt, self.bias = base, q, kt, bias
        self.scores, self.weights, self.tops, self.sums = scores, weights, tops, sums
        self.keys, self.diagonal = keys, diagonal
        self.groups = -(-keys // GROUP)
        self.size = scores.shape[0]

    def score(self, group):
        at = group * GROUP
        end = min(at + GROUP, self.keys)
        part = lax.dot_general(
            self.q[pl.ds(self.base, self.size), :], self.kt[:, at:end], NN, preferred_element_type=jnp.float32
        )
        part = part + self.bias[0:1, at:end]
        columns = [part[:, c : c + PAIR] for c in range(0, end - at, PAIR)]
        if self.diagonal is not None:
            where, key, pos, first = self.diagonal
            if at <= where < end:
                seen = jnp.concatenate(
                    [
                        jnp.broadcast_to(key, (BLOCK, PAIR)) <= pos[first + self.base // BLOCK + s]
                        for s in range(self.size // BLOCK)
                    ],
                    axis=0,
                )
                index = (where - at) // PAIR
                columns[index] = jnp.where(seen, columns[index], NEG)
        high = columns[0]
        for i, column in enumerate(columns):
            self.scores[:, at + i * PAIR : at + (i + 1) * PAIR] = column
            high = jnp.maximum(high, column) if i else high
        self.tops[...] = high if group == 0 else jnp.maximum(self.tops[...], high)

    def settle(self, old=None):
        top = jnp.max(self.tops[...], axis=1, keepdims=True) * SCALE
        top = jnp.broadcast_to(top, (self.size, PAIR))
        self.tops[...] = top if old is None else jnp.maximum(top, old)

    def weigh(self, slab):
        rows = pl.ds(slab * BLOCK, BLOCK)
        top = self.tops[rows, :]
        total = jnp.zeros((BLOCK, PAIR), jnp.float32)
        for at in range(0, self.keys, PAIR):
            part = jnp.exp2(self.scores[rows, at : at + PAIR] * SCALE - top)
            total = total + part
            self.weights[rows, at : at + PAIR] = part.astype(jnp.bfloat16)
        self.sums[rows, :] = total

    def total(self):
        return jnp.broadcast_to(jnp.sum(self.sums[...], axis=1, keepdims=True), (self.size, PAIR))

    def combine(self, column):
        return lax.dot_general(
            self.weights[:, 0 : self.keys],
            self.kt[column : column + GROUP, 0 : self.keys],
            NT,
            preferred_element_type=jnp.float32,
        )


def run_halves(a, b, before, after, combine):
    slabs = a.size // BLOCK
    for g in range(a.groups):
        a.score(g)
    before(a)
    for i in range(max(a.groups, slabs)):
        if i < b.groups:
            b.score(i)
        if i < slabs:
            a.weigh(i)
    before(b)
    after(a)
    for i, column in enumerate(range(0, KVL, GROUP)):
        combine(a, column)
        for s in range(i * slabs // 2, (i + 1) * slabs // 2):
            b.weigh(s)
    after(b)
    for column in range(0, KVL, GROUP):
        combine(b, column)


SCRATCH = 9


def attend_kernel(owners, capacity, kind, levels, table, pos, q, bias, *refs):
    start, end = kind in ("first", "only"), kind in ("last", "only")
    if not start:
        carry, logs, *refs = refs
    outs = refs[len(refs) - SCRATCH - (1 if end else 2) : len(refs) - SCRATCH]
    kt, *work = refs[len(refs) - SCRATCH :]
    arrived = Arrived(owners, refs[: len(refs) - SCRATCH - len(outs)])
    chunks = arrived.chunks
    step = pl.program_id(0)
    sub = work[0].shape[0]
    index = owners * capacity
    needed = table[index + chunks * owners] if kind == "last" else None

    @pl.when(step == 0)
    def _():
        for c in range(chunks):
            for part, (owner, _) in enumerate(arrived.parts):
                if kind == "last":
                    at = table[index + c * owners + owner]
                    pl.when(at >= 0)(functools.partial(arrived.place, c, part, kt, at * PAIR))
                elif start and c == 0:
                    arrived.place(c, part, kt, owner * PAIR)
                else:
                    at = (c * (owners - 1) + owner + int(start)) * PAIR
                    pl.when(owner < owners - 1)(functools.partial(arrived.place, c, part, kt, at))
        if kind == "last":
            fill = jnp.int32(levels[-1])
            for level in reversed(levels[:-1]):
                fill = jnp.where(needed <= level, level, fill)

            @pl.loop(needed, fill)
            def _(i):
                kt[:, pl.ds(pl.multiple_of(i * PAIR, PAIR), PAIR)] = jnp.zeros((kt.shape[0], PAIR), kt.dtype)

    def attend(keys):
        diagonal = None
        if start:
            key = table[(owners - 1) * capacity] + lax.broadcasted_iota(jnp.int32, (1, PAIR), 1)
            diagonal = ((owners - 1) * PAIR, key, pos, step * (2 * sub // BLOCK))
        a = Half(0, q, kt, bias, *work[0::2], keys, diagonal)
        b = Half(sub, q, kt, bias, *work[1::2], keys, diagonal)

        def before(part):
            part.settle(None if start else logs[pl.ds(part.base, sub), :])

        def after(part):
            rows = pl.ds(part.base, sub)
            total = part.total()
            if not start:
                kept = jnp.exp2(logs[rows, :] - part.tops[...])
                total = total + kept
            inverse = 1.0 / total
            part.sums[...] = inverse
            if not end:
                outs[1][rows, :] = part.tops[...] + jnp.log2(total)
            if not start:
                part.tops[...] = kept * inverse

        def combine(part, column):
            summed = part.combine(column)
            rows = pl.ds(part.base, sub)
            for at in range(0, GROUP, PAIR):
                cols = slice(column + at, column + at + PAIR)
                result = summed[:, at : at + PAIR] * part.sums[...]
                if not start:
                    result = result + carry[rows, cols] * part.tops[...]
                outs[0][rows, cols] = result.astype(outs[0].dtype)

        run_halves(a, b, before, after, combine)

    if kind != "last":
        attend(kt.shape[1])
        return
    below = -1
    for level in levels:
        pl.when(jnp.logical_and(needed > below, needed <= level))(functools.partial(attend, level * PAIR))
        below = level


def attend(table, pos, q, bias, state, arrays, owners, capacity, kind, chunks):
    rows, lat = q.shape
    pairs = len(pair_places(owners, chunks, kind in ("first", "only")))
    keys = pairs * PAIR
    levels = [n for n in (4, 5, 6, 8) if n < pairs] + [pairs]
    sub = 512
    step = 2 * sub
    out_shape = [jax.ShapeDtypeStruct((rows, KVL), jnp.float32), jax.ShapeDtypeStruct((rows, PAIR), jnp.float32)]
    if kind in ("last", "only"):
        out_shape = [jax.ShapeDtypeStruct((rows, KVL), jnp.bfloat16)]

    def whole(x):
        return pl.BlockSpec(x.shape, lambda i, *_: (0,) * x.ndim)

    def row_block(x):
        return pl.BlockSpec((step, x.shape[1]), lambda i, *_: (i, 0))

    return pl.pallas_call(
        functools.partial(attend_kernel, owners, capacity, kind, levels),
        out_shape=out_shape,
        grid_spec=pltpu.PrefetchScalarGridSpec(
            num_scalar_prefetch=2,
            grid=(rows // step,),
            in_specs=[row_block(q), whole(bias)] + [row_block(x) for x in state] + [whole(x) for x in arrays],
            out_specs=[row_block(x) for x in out_shape],
            scratch_shapes=[
                pltpu.VMEM((lat, keys), jnp.bfloat16),
                *[pltpu.VMEM((sub, keys), jnp.float32)] * 2,
                *[pltpu.VMEM((sub, keys), jnp.bfloat16)] * 2,
                *[pltpu.VMEM((sub, PAIR), jnp.float32)] * 4,
            ],
        ),
        compiler_params=pltpu.CompilerParams(vmem_limit_bytes=VMEM),
        cost_estimate=pl.CostEstimate(
            flops=2 * rows * keys * (lat + KVL), bytes_accessed=rows * (lat + 2 * KVL) * 2, transcendentals=rows * keys
        ),
        name="attend_" + kind,
    )(table, pos, q, bias, *state, *arrays)


def split_phases(chunks):
    cut = (chunks + 1) // 2
    return [phase for phase in (list(range(cut)), list(range(cut, chunks))) if phase]


def local(queries, latent_cache, positions, block_ids):
    owners = lax.axis_size("ctx")
    capacity = max(2, 2 * SEL // owners)
    shift = log2(latent_cache.shape[0] // BLOCK)
    q_rows, heads, lat = queries.shape
    rows = q_rows * heads
    lists = lax.all_to_all(
        jnp.broadcast_to(block_ids, (owners, SEL)), "ctx", split_axis=0, concat_axis=0, tiled=True
    )
    phases = split_phases(capacity // 2)
    packed = pack(lists, latent_cache.T, capacity, phases[0])
    table, *biases = plan(block_ids[0], owners, capacity, shift, phases)
    steps = partners(owners) + [(owners - 1, owners - 1)]

    def send(own):
        got = []
        for x, ks in zip(own, steps):
            moves = [(2 * c + h, 2 * (c ^ k) + h) for c in range(owners) for h, k in enumerate(ks)]
            got.append(lax.ppermute(x, ("ctx", "head"), moves))
        return got

    def swap(got):
        return [lax.ppermute(x, "head", [(0, 1), (1, 0)]) for x in got]

    q = queries.reshape(rows, lat)
    got = send(packed)
    if len(phases) == 1:
        arrays = [*got, packed[-1], *swap(got)]
        state = attend(table, positions, q, biases[0], [], arrays, owners, capacity, "only", len(phases[0]))
        return state[0].reshape(q_rows, heads, KVL)
    (more,) = pack(lists, latent_cache.T, capacity, phases[1], spread=True)
    *got, more, table = lax.optimization_barrier((*got, more, table))
    late = lax.all_to_all(more, "ctx", split_axis=0, concat_axis=0, tiled=True)
    arrays = [*got, packed[-1], *swap(got)]
    carry, logs = attend(table, positions, q, biases[0], [], arrays, owners, capacity, "first", len(phases[0]))
    late, logs = lax.optimization_barrier((late, logs))
    arrays = [late, *swap([late])]
    state = attend(table, positions, q, biases[1], [carry, logs], arrays, owners, capacity, "last", len(phases[1]))
    return state[0].reshape(q_rows, heads, KVL)


def solution(mesh):
    return jax.shard_map(
        local,
        mesh=mesh,
        in_specs=(
            P(("groups", "ctx"), "head", None),
            P(("groups", "ctx"), None),
            P(("groups", "ctx")),
            P(("groups", "ctx"), None),
        ),
        out_specs=P(("groups", "ctx"), "head", None),
        check_vma=False,
    )
```

```python
import functools

import jax
import jax.numpy as jnp
from jax import lax
from jax.experimental import pallas as pl
from jax.experimental.pallas import tpu as pltpu
from jax.sharding import PartitionSpec as P

KVL = 512
BLOCK = 64
SEL = 32
PAIR = 2 * BLOCK
GROUP = 2 * PAIR
VMEM = 60 << 20
NEG = -1e30
SCALE = 1.4426950408889634 / 192.0**0.5
NT = (((1,), (1,)), ((), ()))
NN = (((1,), (0,)), ((), ()))


def log2(n):
    shift = n.bit_length() - 1
    assert 1 << shift == n
    return shift


def partners(owners):
    count = (owners - 2) // 2
    low, high = range(1, count + 1), range(count + 1, 2 * count + 1)
    return [(a, b) if i % 2 == 0 else (b, a) for i, (a, b) in enumerate(zip(low, high))]


def pack_kernel(capacity, chunks, spread, ids, cache, *refs):
    dests = ids.shape[0]
    pairs = partners(dests)
    outs, (table, rows, sem) = refs[:-3], refs[-3:]
    lat, tokens = rows.shape
    half = lat // 2
    shift = log2(tokens // BLOCK)
    head = lax.axis_index("head")
    me = lax.axis_index("ctx")
    copy = pltpu.make_async_copy(cache, rows, sem)
    copy.start()
    for k in range(dests):
        at = jnp.int32(k * (capacity + 1))
        for slot in range(capacity + 1):
            table[k * (capacity + 1) + slot] = 0
        for j in range(SEL):
            block = ids[k if spread else me ^ k, j]
            table[at] = block & ((1 << shift) - 1)
            at = at + (block >> shift == me).astype(jnp.int32)
        table[at] = 0

    def block_pair(k, chunk, start, size):
        first = k * (capacity + 1) + 2 * chunk
        a, b = table[first], table[first + 1]
        left = lax.broadcasted_iota(jnp.int32, (size, PAIR), 1) < BLOCK
        xa = rows[pl.ds(start, size), pl.ds(pl.multiple_of((a >> 1) * PAIR, PAIR), PAIR)]
        xb = rows[pl.ds(start, size), pl.ds(pl.multiple_of((b >> 1) * PAIR, PAIR), PAIR)]
        xa = jnp.where((a & 1) == 0, xa, pltpu.roll(xa, BLOCK, 1))
        xb = jnp.where((b & 1) == 1, xb, pltpu.roll(xb, BLOCK, 1))
        return jnp.where(left, xa, xb)

    copy.wait()
    if spread:
        for c, chunk in enumerate(spread):
            outs[0][c] = block_pair(me, chunk, 0, lat)
        for c, chunk in enumerate(chunks):
            for d in range(dests):
                outs[1][d, c] = block_pair(d, chunk, pl.multiple_of(head * half, 32), half)
        return
    for c, chunk in enumerate(chunks):
        for j, (a, b) in enumerate(pairs):
            outs[j][c] = block_pair(jnp.where(head == 0, a, b), chunk, 0, lat)
        outs[-1][c] = block_pair(dests - 1, chunk, pl.multiple_of(head * half, 32), half)


def pack(ids, cache_t, capacity, chunks, spread=None):
    dests = ids.shape[0]
    lat, tokens = cache_t.shape
    sizes = [lat] * len(partners(dests)) + [lat // 2]
    shapes = [(len(chunks), size, PAIR) for size in sizes]
    if spread:
        shapes = [(len(spread), lat, PAIR)] + ([(dests, len(chunks), lat // 2, PAIR)] if chunks else [])

    packed = pl.pallas_call(
        functools.partial(pack_kernel, capacity, chunks, spread),
        out_shape=[jax.ShapeDtypeStruct(s, jnp.bfloat16) for s in shapes],
        grid_spec=pltpu.PrefetchScalarGridSpec(
            num_scalar_prefetch=1,
            grid=(1,),
            in_specs=[pl.BlockSpec(memory_space=pl.ANY)],
            out_specs=[pl.BlockSpec(s, lambda i, *_, n=len(s): (0,) * n) for s in shapes],
            scratch_shapes=[
                pltpu.SMEM((dests * (capacity + 1),), jnp.int32),
                pltpu.VMEM((lat, tokens), jnp.bfloat16),
                pltpu.SemaphoreType.DMA,
            ],
        ),
        compiler_params=pltpu.CompilerParams(vmem_limit_bytes=VMEM),
        cost_estimate=pl.CostEstimate(flops=0, bytes_accessed=8 * lat * tokens, transcendentals=0),
        name="pack",
    )(ids, cache_t)
    return list(packed)


def pair_bias(bias, at, start_a, start_b):
    lane = lax.broadcasted_iota(jnp.int32, (8, PAIR), 1)
    start = jnp.where(lane < BLOCK, start_a, start_b)
    bias[:, pl.ds(at, PAIR)] = jnp.where(start >= 0, 0.0, NEG).astype(jnp.float32)


def pair_places(owners, phase, first):
    return {
        (c, o): i
        for i, (c, o) in enumerate((c, o) for c in range(phase) for o in range(owners) if o < owners - 1 or first and c == 0)
    }


def plan_kernel(owners, capacity, shift, phases, ids, table, *rest):
    biases, count = rest[:-1], rest[-1]
    for slot in range(owners * capacity):
        table[slot] = -1
    for o in range(owners):
        count[o] = 0
    for j in range(SEL):
        block = ids[j]
        owner = block >> shift
        rank = count[owner]
        table[owner * capacity + rank] = block * BLOCK
        count[owner] = rank + 1
    for p, (bias, phase) in enumerate(zip(biases, phases)):
        last = p > 0 and p == len(phases) - 1
        if last:
            bias[...] = jnp.full(bias.shape, NEG, bias.dtype)
            live = jnp.int32(0)
        for (c, o), i in pair_places(owners, len(phase), p == 0).items():
            slot = o * capacity + 2 * phase[c]
            a, b = table[slot], table[slot + 1]
            if last:
                used = a >= 0
                table[owners * capacity + c * owners + o] = jnp.where(used, live, -1)
                pair_bias(bias, pl.multiple_of(live * PAIR, PAIR), a, b)
                live = live + used.astype(jnp.int32)
            else:
                pair_bias(bias, i * PAIR, a, b)
        if last:
            for c in range(len(phase)):
                table[owners * capacity + c * owners + owners - 1] = -1
            table[owners * capacity + len(phase) * owners] = live


def plan(ids, owners, capacity, shift, phases):
    shapes = [(8, len(pair_places(owners, len(phase), p == 0)) * PAIR) for p, phase in enumerate(phases)]
    if len(phases) > 1:
        shapes[-1] = (8, shapes[-1][1] + PAIR)
    entries = owners * capacity + len(phases[-1]) * owners + 1
    return pl.pallas_call(
        functools.partial(plan_kernel, owners, capacity, shift, phases),
        out_shape=[jax.ShapeDtypeStruct((entries,), jnp.int32)]
        + [jax.ShapeDtypeStruct(s, jnp.float32) for s in shapes],
        grid_spec=pltpu.PrefetchScalarGridSpec(
            num_scalar_prefetch=1,
            grid=(1,),
            in_specs=[],
            out_specs=[pl.BlockSpec(memory_space=pltpu.SMEM)] + [pl.BlockSpec(s, lambda i, ids: (0, 0)) for s in shapes],
            scratch_shapes=[pltpu.SMEM((owners,), jnp.int32)],
        ),
        cost_estimate=pl.CostEstimate(flops=0, bytes_accessed=1 << 20, transcendentals=0),
        name="plan",
    )(ids)


class Arrived:
    def __init__(self, owners, arrays):
        pairs = partners(owners)
        count = len(pairs)
        head, me = lax.axis_index("head"), lax.axis_index("ctx")
        if len(arrays) == 2:
            _, self.chunks, half, _ = arrays[0].shape
            starts = [pl.multiple_of(h * half, 32) for h in (head, 1 - head)]
            self.parts = [
                (o, [(x.at[o], start, half) for x, start in zip(arrays, starts)]) for o in range(owners)
            ]
            return
        got, shared, own = arrays[:count], arrays[count], arrays[count + 1]
        swapped, shared_other = arrays[count + 2 : 2 * count + 2], arrays[2 * count + 2]
        self.chunks, lat, _ = own.shape
        half = lat // 2
        self.parts = [(me, [(own, 0, lat)])]
        for (a, b), x, y in zip(pairs, got, swapped):
            self.parts.append((me ^ jnp.where(head == 0, a, b), [(x, 0, lat)]))
            self.parts.append((me ^ jnp.where(head == 0, b, a), [(y, 0, lat)]))
        split = [(x, pl.multiple_of(h * half, 32), half) for x, h in ((shared, head), (shared_other, 1 - head))]
        self.parts.append((me ^ (owners - 1), split))

    def place(self, chunk, part, kt, at):
        for x, start, size in self.parts[part][1]:
            kt[pl.ds(start, size), pl.ds(pl.multiple_of(at, PAIR), PAIR)] = x[chunk]


class Half:
    def __init__(self, base, q, kt, bias, scores, weights, tops, sums, keys, diagonal=None):
        self.base, self.q, self.kt, self.bias = base, q, kt, bias
        self.scores, self.weights, self.tops, self.sums = scores, weights, tops, sums
        self.keys, self.diagonal = keys, diagonal
        self.groups = -(-keys // GROUP)
        self.size = scores.shape[0]

    def score(self, group):
        at = group * GROUP
        end = min(at + GROUP, self.keys)
        part = lax.dot_general(
            self.q[pl.ds(self.base, self.size), :], self.kt[:, at:end], NN, preferred_element_type=jnp.float32
        )
        part = part + self.bias[0:1, at:end]
        columns = [part[:, c : c + PAIR] for c in range(0, end - at, PAIR)]
        if self.diagonal is not None:
            where, key, pos, first = self.diagonal
            if at <= where < end:
                seen = jnp.concatenate(
                    [
                        jnp.broadcast_to(key, (BLOCK, PAIR)) <= pos[first + self.base // BLOCK + s]
                        for s in range(self.size // BLOCK)
                    ],
                    axis=0,
                )
                index = (where - at) // PAIR
                columns[index] = jnp.where(seen, columns[index], NEG)
        high = columns[0]
        for i, column in enumerate(columns):
            self.scores[:, at + i * PAIR : at + (i + 1) * PAIR] = column
            high = jnp.maximum(high, column) if i else high
        self.tops[...] = high if group == 0 else jnp.maximum(self.tops[...], high)

    def settle(self, old=None):
        top = jnp.max(self.tops[...], axis=1, keepdims=True) * SCALE
        top = jnp.broadcast_to(top, (self.size, PAIR))
        self.tops[...] = top if old is None else jnp.maximum(top, old)

    def weigh(self, slab):
        rows = pl.ds(slab * BLOCK, BLOCK)
        top = self.tops[rows, :]
        total = jnp.zeros((BLOCK, PAIR), jnp.float32)
        for at in range(0, self.keys, PAIR):
            part = jnp.exp2(self.scores[rows, at : at + PAIR] * SCALE - top)
            total = total + part
            self.weights[rows, at : at + PAIR] = part.astype(jnp.bfloat16)
        self.sums[rows, :] = total

    def total(self):
        return jnp.broadcast_to(jnp.sum(self.sums[...], axis=1, keepdims=True), (self.size, PAIR))

    def combine(self, column):
        return lax.dot_general(
            self.weights[:, 0 : self.keys],
            self.kt[column : column + GROUP, 0 : self.keys],
            NT,
            preferred_element_type=jnp.float32,
        )


def run_halves(a, b, before, after, combine):
    slabs = a.size // BLOCK
    for g in range(a.groups):
        a.score(g)
    before(a)
    for i in range(max(a.groups, slabs)):
        if i < b.groups:
            b.score(i)
        if i < slabs:
            a.weigh(i)
    before(b)
    after(a)
    for i, column in enumerate(range(0, KVL, GROUP)):
        combine(a, column)
        for s in range(i * slabs // 2, (i + 1) * slabs // 2):
            b.weigh(s)
    after(b)
    for column in range(0, KVL, GROUP):
        combine(b, column)


SCRATCH = 9


def attend_kernel(owners, capacity, kind, levels, table, pos, q, bias, *refs):
    start, end = kind in ("first", "only"), kind in ("last", "only")
    if not start:
        carry, logs, *refs = refs
    outs = refs[len(refs) - SCRATCH - (1 if end else 2) : len(refs) - SCRATCH]
    kt, *work = refs[len(refs) - SCRATCH :]
    arrived = Arrived(owners, refs[: len(refs) - SCRATCH - len(outs)])
    chunks = arrived.chunks
    step = pl.program_id(0)
    sub = work[0].shape[0]
    index = owners * capacity
    needed = table[index + chunks * owners] if kind == "last" else None

    @pl.when(step == 0)
    def _():
        for c in range(chunks):
            for part, (owner, _) in enumerate(arrived.parts):
                if kind == "last":
                    at = table[index + c * owners + owner]
                    pl.when(at >= 0)(functools.partial(arrived.place, c, part, kt, at * PAIR))
                elif start and c == 0:
                    arrived.place(c, part, kt, owner * PAIR)
                else:
                    at = (c * (owners - 1) + owner + int(start)) * PAIR
                    pl.when(owner < owners - 1)(functools.partial(arrived.place, c, part, kt, at))
        if kind == "last":
            fill = jnp.int32(levels[-1])
            for level in reversed(levels[:-1]):
                fill = jnp.where(needed <= level, level, fill)

            @pl.loop(needed, fill)
            def _(i):
                kt[:, pl.ds(pl.multiple_of(i * PAIR, PAIR), PAIR)] = jnp.zeros((kt.shape[0], PAIR), kt.dtype)

    def attend(keys):
        diagonal = None
        if start:
            key = table[(owners - 1) * capacity] + lax.broadcasted_iota(jnp.int32, (1, PAIR), 1)
            diagonal = ((owners - 1) * PAIR, key, pos, step * (2 * sub // BLOCK))
        a = Half(0, q, kt, bias, *work[0::2], keys, diagonal)
        b = Half(sub, q, kt, bias, *work[1::2], keys, diagonal)

        def before(part):
            part.settle(None if start else logs[pl.ds(part.base, sub), :])

        def after(part):
            rows = pl.ds(part.base, sub)
            total = part.total()
            if not start:
                kept = jnp.exp2(logs[rows, :] - part.tops[...])
                total = total + kept
            inverse = 1.0 / total
            part.sums[...] = inverse
            if not end:
                outs[1][rows, :] = part.tops[...] + jnp.log2(total)
            if not start:
                part.tops[...] = kept * inverse

        def combine(part, column):
            summed = part.combine(column)
            rows = pl.ds(part.base, sub)
            for at in range(0, GROUP, PAIR):
                cols = slice(column + at, column + at + PAIR)
                result = summed[:, at : at + PAIR] * part.sums[...]
                if not start:
                    result = result + carry[rows, cols] * part.tops[...]
                outs[0][rows, cols] = result.astype(outs[0].dtype)

        run_halves(a, b, before, after, combine)

    if kind != "last":
        attend(kt.shape[1])
        return
    below = -1
    for level in levels:
        pl.when(jnp.logical_and(needed > below, needed <= level))(functools.partial(attend, level * PAIR))
        below = level


def attend(table, pos, q, bias, state, arrays, owners, capacity, kind, chunks):
    rows, lat = q.shape
    pairs = len(pair_places(owners, chunks, kind in ("first", "only")))
    keys = pairs * PAIR
    levels = [n for n in (4, 5, 6, 8) if n < pairs] + [pairs]
    sub = 512
    step = 2 * sub
    out_shape = [jax.ShapeDtypeStruct((rows, KVL), jnp.float32), jax.ShapeDtypeStruct((rows, PAIR), jnp.float32)]
    if kind in ("last", "only"):
        out_shape = [jax.ShapeDtypeStruct((rows, KVL), jnp.bfloat16)]

    def whole(x):
        return pl.BlockSpec(x.shape, lambda i, *_: (0,) * x.ndim)

    def row_block(x):
        return pl.BlockSpec((step, x.shape[1]), lambda i, *_: (i, 0))

    return pl.pallas_call(
        functools.partial(attend_kernel, owners, capacity, kind, levels),
        out_shape=out_shape,
        grid_spec=pltpu.PrefetchScalarGridSpec(
            num_scalar_prefetch=2,
            grid=(rows // step,),
            in_specs=[row_block(q), whole(bias)] + [row_block(x) for x in state] + [whole(x) for x in arrays],
            out_specs=[row_block(x) for x in out_shape],
            scratch_shapes=[
                pltpu.VMEM((lat, keys), jnp.bfloat16),
                *[pltpu.VMEM((sub, keys), jnp.float32)] * 2,
                *[pltpu.VMEM((sub, keys), jnp.bfloat16)] * 2,
                *[pltpu.VMEM((sub, PAIR), jnp.float32)] * 4,
            ],
        ),
        compiler_params=pltpu.CompilerParams(vmem_limit_bytes=min(VMEM, (18 << 20) + keys * 10240)),
        cost_estimate=pl.CostEstimate(
            flops=2 * rows * keys * (lat + KVL), bytes_accessed=rows * (lat + 2 * KVL) * 2, transcendentals=rows * keys
        ),
        name="attend_" + kind,
    )(table, pos, q, bias, *state, *arrays)


def split_phases(chunks):
    cut = (chunks + 1) // 2
    return [phase for phase in (list(range(cut)), list(range(cut, chunks))) if phase]


def local(queries, latent_cache, positions, block_ids):
    owners = lax.axis_size("ctx")
    capacity = max(2, 2 * SEL // owners)
    shift = log2(latent_cache.shape[0] // BLOCK)
    q_rows, heads, lat = queries.shape
    rows = q_rows * heads
    lists = lax.all_to_all(
        jnp.broadcast_to(block_ids, (owners, SEL)), "ctx", split_axis=0, concat_axis=0, tiled=True
    )
    phases = split_phases(capacity // 2)
    packed = pack(lists, latent_cache.T, capacity, phases[0])
    table, *biases = plan(block_ids[0], owners, capacity, shift, phases)
    steps = partners(owners) + [(owners - 1, owners - 1)]

    def send(own):
        got = []
        for x, ks in zip(own, steps):
            moves = [(2 * c + h, 2 * (c ^ k) + h) for c in range(owners) for h, k in enumerate(ks)]
            got.append(lax.ppermute(x, ("ctx", "head"), moves))
        return got

    def swap(got):
        return [lax.ppermute(x, "head", [(0, 1), (1, 0)]) for x in got]

    q = queries.reshape(rows, lat)
    got = send(packed)
    if len(phases) == 1:
        (own,) = pack(lists, latent_cache.T, capacity, [], spread=phases[0])
        arrays = [*got, own, *swap(got)]
        state = attend(table, positions, q, biases[0], [], arrays, owners, capacity, "only", len(phases[0]))
        return state[0].reshape(q_rows, heads, KVL)
    *own, more = pack(lists, latent_cache.T, capacity, phases[1], spread=phases[0])
    got[-1], more = lax.optimization_barrier((got[-1], more))
    swapped = swap(got)
    *got, more, table = lax.optimization_barrier((*got, more, table))
    late = lax.all_to_all(more, "ctx", split_axis=0, concat_axis=0, tiled=True)
    arrays = [*got, *own, *swapped]
    carry, logs = attend(table, positions, q, biases[0], [], arrays, owners, capacity, "first", len(phases[0]))
    late, logs = lax.optimization_barrier((late, logs))
    arrays = [late, *swap([late])]
    state = attend(table, positions, q, biases[1], [carry, logs], arrays, owners, capacity, "last", len(phases[1]))
    return state[0].reshape(q_rows, heads, KVL)


def solution(mesh):
    return jax.shard_map(
        local,
        mesh=mesh,
        in_specs=(
            P(("groups", "ctx"), "head", None),
            P(("groups", "ctx"), None),
            P(("groups", "ctx")),
            P(("groups", "ctx"), None),
        ),
        out_specs=P(("groups", "ctx"), "head", None),
        check_vma=False,
    )
```

```python
import functools

import jax
import jax.numpy as jnp
from jax import lax
from jax.experimental import pallas as pl
from jax.experimental.pallas import tpu as pltpu
from jax.sharding import PartitionSpec as P

KVL = 512
BLOCK = 64
SEL = 32
PAIR = 2 * BLOCK
GROUP = 2 * PAIR
VMEM = 60 << 20
NEG = -1e30
SCALE = 1.4426950408889634 / 192.0**0.5
NT = (((1,), (1,)), ((), ()))
NN = (((1,), (0,)), ((), ()))


def log2(n):
    shift = n.bit_length() - 1
    assert 1 << shift == n
    return shift


def partners(owners):
    count = (owners - 2) // 2
    low, high = range(1, count + 1), range(count + 1, 2 * count + 1)
    return [(a, b) if i % 2 == 0 else (b, a) for i, (a, b) in enumerate(zip(low, high))]


def pack_kernel(capacity, chunks, spread, ids, cache, *refs):
    dests = ids.shape[0]
    pairs = partners(dests)
    outs, (table, rows, sem) = refs[:-3], refs[-3:]
    lat, tokens = rows.shape
    half = lat // 2
    shift = log2(tokens // BLOCK)
    head = lax.axis_index("head")
    me = lax.axis_index("ctx")
    copy = pltpu.make_async_copy(cache, rows, sem)
    copy.start()
    for k in range(dests):
        at = jnp.int32(k * (capacity + 1))
        for slot in range(capacity + 1):
            table[k * (capacity + 1) + slot] = 0
        for j in range(SEL):
            block = ids[k if spread else me ^ k, j]
            table[at] = block & ((1 << shift) - 1)
            at = at + (block >> shift == me).astype(jnp.int32)
        table[at] = 0

    def block_pair(k, chunk, start, size):
        first = k * (capacity + 1) + 2 * chunk
        a, b = table[first], table[first + 1]
        left = lax.broadcasted_iota(jnp.int32, (size, PAIR), 1) < BLOCK
        xa = rows[pl.ds(start, size), pl.ds(pl.multiple_of((a >> 1) * PAIR, PAIR), PAIR)]
        xb = rows[pl.ds(start, size), pl.ds(pl.multiple_of((b >> 1) * PAIR, PAIR), PAIR)]
        xa = jnp.where((a & 1) == 0, xa, pltpu.roll(xa, BLOCK, 1))
        xb = jnp.where((b & 1) == 1, xb, pltpu.roll(xb, BLOCK, 1))
        return jnp.where(left, xa, xb)

    copy.wait()
    if spread:
        for c, chunk in enumerate(spread):
            outs[0][c] = block_pair(me, chunk, 0, lat)
        for c, chunk in enumerate(chunks):
            for d in range(dests):
                outs[1][d, c] = block_pair(d, chunk, pl.multiple_of(head * half, 32), half)
        return
    for c, chunk in enumerate(chunks):
        for j, (a, b) in enumerate(pairs):
            outs[j][c] = block_pair(jnp.where(head == 0, a, b), chunk, 0, lat)
        outs[-1][c] = block_pair(dests - 1, chunk, pl.multiple_of(head * half, 32), half)


def pack(ids, cache_t, capacity, chunks, spread=None):
    dests = ids.shape[0]
    lat, tokens = cache_t.shape
    sizes = [lat] * len(partners(dests)) + [lat // 2]
    shapes = [(len(chunks), size, PAIR) for size in sizes]
    if spread:
        shapes = [(len(spread), lat, PAIR)] + ([(dests, len(chunks), lat // 2, PAIR)] if chunks else [])

    packed = pl.pallas_call(
        functools.partial(pack_kernel, capacity, chunks, spread),
        out_shape=[jax.ShapeDtypeStruct(s, jnp.bfloat16) for s in shapes],
        grid_spec=pltpu.PrefetchScalarGridSpec(
            num_scalar_prefetch=1,
            grid=(1,),
            in_specs=[pl.BlockSpec(memory_space=pl.ANY)],
            out_specs=[pl.BlockSpec(s, lambda i, *_, n=len(s): (0,) * n) for s in shapes],
            scratch_shapes=[
                pltpu.SMEM((dests * (capacity + 1),), jnp.int32),
                pltpu.VMEM((lat, tokens), jnp.bfloat16),
                pltpu.SemaphoreType.DMA,
            ],
        ),
        compiler_params=pltpu.CompilerParams(vmem_limit_bytes=VMEM),
        cost_estimate=pl.CostEstimate(flops=0, bytes_accessed=8 * lat * tokens, transcendentals=0),
        name="pack",
    )(ids, cache_t)
    return list(packed)


def pair_bias(bias, at, start_a, start_b):
    lane = lax.broadcasted_iota(jnp.int32, (8, PAIR), 1)
    start = jnp.where(lane < BLOCK, start_a, start_b)
    bias[:, pl.ds(at, PAIR)] = jnp.where(start >= 0, 0.0, NEG).astype(jnp.float32)


def pair_places(owners, phase, first):
    return {
        (c, o): i
        for i, (c, o) in enumerate((c, o) for c in range(phase) for o in range(owners) if o < owners - 1 or first and c == 0)
    }


def plan_kernel(owners, capacity, shift, phases, ids, table, *rest):
    biases, count = rest[:-1], rest[-1]
    for slot in range(owners * capacity):
        table[slot] = -1
    for o in range(owners):
        count[o] = 0
    for j in range(SEL):
        block = ids[j]
        owner = block >> shift
        rank = count[owner]
        table[owner * capacity + rank] = block * BLOCK
        count[owner] = rank + 1
    for p, (bias, phase) in enumerate(zip(biases, phases)):
        last = p > 0 and p == len(phases) - 1
        if last:
            bias[...] = jnp.full(bias.shape, NEG, bias.dtype)
            live = jnp.int32(0)
        for (c, o), i in pair_places(owners, len(phase), p == 0).items():
            slot = o * capacity + 2 * phase[c]
            a, b = table[slot], table[slot + 1]
            if last:
                used = a >= 0
                table[owners * capacity + c * owners + o] = jnp.where(used, live, -1)
                pair_bias(bias, pl.multiple_of(live * PAIR, PAIR), a, b)
                live = live + used.astype(jnp.int32)
            else:
                pair_bias(bias, i * PAIR, a, b)
        if last:
            for c in range(len(phase)):
                table[owners * capacity + c * owners + owners - 1] = -1
            table[owners * capacity + len(phase) * owners] = live


def plan(ids, owners, capacity, shift, phases):
    shapes = [(8, len(pair_places(owners, len(phase), p == 0)) * PAIR) for p, phase in enumerate(phases)]
    if len(phases) > 1:
        shapes[-1] = (8, shapes[-1][1] + PAIR)
    entries = owners * capacity + len(phases[-1]) * owners + 1
    return pl.pallas_call(
        functools.partial(plan_kernel, owners, capacity, shift, phases),
        out_shape=[jax.ShapeDtypeStruct((entries,), jnp.int32)]
        + [jax.ShapeDtypeStruct(s, jnp.float32) for s in shapes],
        grid_spec=pltpu.PrefetchScalarGridSpec(
            num_scalar_prefetch=1,
            grid=(1,),
            in_specs=[],
            out_specs=[pl.BlockSpec(memory_space=pltpu.SMEM)] + [pl.BlockSpec(s, lambda i, ids: (0, 0)) for s in shapes],
            scratch_shapes=[pltpu.SMEM((owners,), jnp.int32)],
        ),
        cost_estimate=pl.CostEstimate(flops=0, bytes_accessed=1 << 20, transcendentals=0),
        name="plan",
    )(ids)


class Arrived:
    def __init__(self, owners, arrays):
        pairs = partners(owners)
        count = len(pairs)
        head, me = lax.axis_index("head"), lax.axis_index("ctx")
        if len(arrays) == 2:
            _, self.chunks, half, _ = arrays[0].shape
            starts = [pl.multiple_of(h * half, 32) for h in (head, 1 - head)]
            self.parts = [
                (o, [(x.at[o], start, half) for x, start in zip(arrays, starts)]) for o in range(owners)
            ]
            return
        got, shared, own = arrays[:count], arrays[count], arrays[count + 1]
        swapped, shared_other = arrays[count + 2 : 2 * count + 2], arrays[2 * count + 2]
        self.chunks, lat, _ = own.shape
        half = lat // 2
        self.parts = [(me, [(own, 0, lat)])]
        for (a, b), x, y in zip(pairs, got, swapped):
            self.parts.append((me ^ jnp.where(head == 0, a, b), [(x, 0, lat)]))
            self.parts.append((me ^ jnp.where(head == 0, b, a), [(y, 0, lat)]))
        split = [(x, pl.multiple_of(h * half, 32), half) for x, h in ((shared, head), (shared_other, 1 - head))]
        self.parts.append((me ^ (owners - 1), split))

    def place(self, chunk, part, kt, at):
        for x, start, size in self.parts[part][1]:
            kt[pl.ds(start, size), pl.ds(pl.multiple_of(at, PAIR), PAIR)] = x[chunk]


class Half:
    def __init__(self, base, q, kt, bias, scores, weights, tops, sums, keys, diagonal=None):
        self.base, self.q, self.kt, self.bias = base, q, kt, bias
        self.scores, self.weights, self.tops, self.sums = scores, weights, tops, sums
        self.keys, self.diagonal = keys, diagonal
        self.groups = -(-keys // GROUP)
        self.size = scores.shape[0]

    def score(self, group):
        at = group * GROUP
        end = min(at + GROUP, self.keys)
        part = lax.dot_general(
            self.q[pl.ds(self.base, self.size), :], self.kt[:, at:end], NN, preferred_element_type=jnp.float32
        )
        part = part + self.bias[0:1, at:end]
        columns = [part[:, c : c + PAIR] for c in range(0, end - at, PAIR)]
        if self.diagonal is not None:
            where, key, pos, first = self.diagonal
            if at <= where < end:
                seen = jnp.concatenate(
                    [
                        jnp.broadcast_to(key, (BLOCK, PAIR)) <= pos[first + self.base // BLOCK + s]
                        for s in range(self.size // BLOCK)
                    ],
                    axis=0,
                )
                index = (where - at) // PAIR
                columns[index] = jnp.where(seen, columns[index], NEG)
        high = columns[0]
        for i, column in enumerate(columns):
            self.scores[:, at + i * PAIR : at + (i + 1) * PAIR] = column
            high = jnp.maximum(high, column) if i else high
        self.tops[...] = high if group == 0 else jnp.maximum(self.tops[...], high)

    def settle(self, old=None):
        top = jnp.max(self.tops[...], axis=1, keepdims=True) * SCALE
        top = jnp.broadcast_to(top, (self.size, PAIR))
        self.tops[...] = top if old is None else jnp.maximum(top, old)

    def weigh(self, slab):
        rows = pl.ds(slab * BLOCK, BLOCK)
        top = self.tops[rows, :]
        total = jnp.zeros((BLOCK, PAIR), jnp.float32)
        for at in range(0, self.keys, PAIR):
            part = jnp.exp2(self.scores[rows, at : at + PAIR] * SCALE - top)
            total = total + part
            self.weights[rows, at : at + PAIR] = part.astype(jnp.bfloat16)
        self.sums[rows, :] = total

    def total(self):
        return jnp.broadcast_to(jnp.sum(self.sums[...], axis=1, keepdims=True), (self.size, PAIR))

    def combine(self, column):
        return lax.dot_general(
            self.weights[:, 0 : self.keys],
            self.kt[column : column + GROUP, 0 : self.keys],
            NT,
            preferred_element_type=jnp.float32,
        )


def run_halves(a, b, before, after, combine):
    slabs = a.size // BLOCK
    for g in range(a.groups):
        a.score(g)
    before(a)
    for i in range(max(a.groups, slabs)):
        if i < b.groups:
            b.score(i)
        if i < slabs:
            a.weigh(i)
    before(b)
    after(a)
    for i, column in enumerate(range(0, KVL, GROUP)):
        combine(a, column)
        for s in range(i * slabs // 2, (i + 1) * slabs // 2):
            b.weigh(s)
    after(b)
    for column in range(0, KVL, GROUP):
        combine(b, column)


SCRATCH = 9


def attend_kernel(owners, capacity, kind, levels, table, pos, q, bias, *refs):
    start, end = kind in ("first", "only"), kind in ("last", "only")
    if not start:
        carry, logs, *refs = refs
    outs = refs[len(refs) - SCRATCH - (1 if end else 2) : len(refs) - SCRATCH]
    kt, *work = refs[len(refs) - SCRATCH :]
    arrived = Arrived(owners, refs[: len(refs) - SCRATCH - len(outs)])
    chunks = arrived.chunks
    step = pl.program_id(0)
    sub = work[0].shape[0]
    index = owners * capacity
    needed = table[index + chunks * owners] if kind == "last" else None

    @pl.when(step == 0)
    def _():
        for c in range(chunks):
            for part, (owner, _) in enumerate(arrived.parts):
                if kind == "last":
                    at = table[index + c * owners + owner]
                    pl.when(at >= 0)(functools.partial(arrived.place, c, part, kt, at * PAIR))
                elif start and c == 0:
                    arrived.place(c, part, kt, owner * PAIR)
                else:
                    at = (c * (owners - 1) + owner + int(start)) * PAIR
                    pl.when(owner < owners - 1)(functools.partial(arrived.place, c, part, kt, at))
        if kind == "last":
            fill = jnp.int32(levels[-1])
            for level in reversed(levels[:-1]):
                fill = jnp.where(needed <= level, level, fill)

            @pl.loop(needed, fill)
            def _(i):
                kt[:, pl.ds(pl.multiple_of(i * PAIR, PAIR), PAIR)] = jnp.zeros((kt.shape[0], PAIR), kt.dtype)

    def attend(keys):
        diagonal = None
        if start:
            key = table[(owners - 1) * capacity] + lax.broadcasted_iota(jnp.int32, (1, PAIR), 1)
            diagonal = ((owners - 1) * PAIR, key, pos, step * (2 * sub // BLOCK))
        a = Half(0, q, kt, bias, *work[0::2], keys, diagonal)
        b = Half(sub, q, kt, bias, *work[1::2], keys, diagonal)

        def before(part):
            part.settle(None if start else logs[pl.ds(part.base, sub), :])

        def after(part):
            rows = pl.ds(part.base, sub)
            total = part.total()
            if not start:
                kept = jnp.exp2(logs[rows, :] - part.tops[...])
                total = total + kept
            inverse = 1.0 / total
            part.sums[...] = inverse
            if not end:
                outs[1][rows, :] = part.tops[...] + jnp.log2(total)
            if not start:
                part.tops[...] = kept * inverse

        def combine(part, column):
            summed = part.combine(column)
            rows = pl.ds(part.base, sub)
            for at in range(0, GROUP, PAIR):
                cols = slice(column + at, column + at + PAIR)
                result = summed[:, at : at + PAIR] * part.sums[...]
                if not start:
                    result = result + carry[rows, cols] * part.tops[...]
                outs[0][rows, cols] = result.astype(outs[0].dtype)

        run_halves(a, b, before, after, combine)

    if kind != "last":
        attend(kt.shape[1])
        return
    below = -1
    for level in levels:
        pl.when(jnp.logical_and(needed > below, needed <= level))(functools.partial(attend, level * PAIR))
        below = level


def attend(table, pos, q, bias, state, arrays, owners, capacity, kind, chunks):
    rows, lat = q.shape
    pairs = len(pair_places(owners, chunks, kind in ("first", "only")))
    keys = pairs * PAIR
    levels = [n for n in (4, 5, 6, 8) if n < pairs] + [pairs]
    sub = 256 if kind == "last" else 512
    step = 2 * sub
    out_shape = [jax.ShapeDtypeStruct((rows, KVL), jnp.float32), jax.ShapeDtypeStruct((rows, PAIR), jnp.float32)]
    if kind in ("last", "only"):
        out_shape = [jax.ShapeDtypeStruct((rows, KVL), jnp.bfloat16)]

    def whole(x):
        return pl.BlockSpec(x.shape, lambda i, *_: (0,) * x.ndim)

    def row_block(x):
        return pl.BlockSpec((step, x.shape[1]), lambda i, *_: (i, 0))

    return pl.pallas_call(
        functools.partial(attend_kernel, owners, capacity, kind, levels),
        out_shape=out_shape,
        grid_spec=pltpu.PrefetchScalarGridSpec(
            num_scalar_prefetch=2,
            grid=(rows // step,),
            in_specs=[row_block(q), whole(bias)] + [row_block(x) for x in state] + [whole(x) for x in arrays],
            out_specs=[row_block(x) for x in out_shape],
            scratch_shapes=[
                pltpu.VMEM((lat, keys), jnp.bfloat16),
                *[pltpu.VMEM((sub, keys), jnp.float32)] * 2,
                *[pltpu.VMEM((sub, keys), jnp.bfloat16)] * 2,
                *[pltpu.VMEM((sub, PAIR), jnp.float32)] * 4,
            ],
        ),
        compiler_params=pltpu.CompilerParams(vmem_limit_bytes=VMEM - (4 << 20)),
        cost_estimate=pl.CostEstimate(
            flops=2 * rows * keys * (lat + KVL), bytes_accessed=rows * (lat + 2 * KVL) * 2, transcendentals=rows * keys
        ),
        name="attend_" + kind,
    )(table, pos, q, bias, *state, *arrays)


def split_phases(chunks):
    cut = (chunks + 1) // 2
    return [phase for phase in (list(range(cut)), list(range(cut, chunks))) if phase]


def local(queries, latent_cache, positions, block_ids):
    owners = lax.axis_size("ctx")
    capacity = max(2, 2 * SEL // owners)
    shift = log2(latent_cache.shape[0] // BLOCK)
    q_rows, heads, lat = queries.shape
    rows = q_rows * heads
    lists = lax.all_to_all(
        jnp.broadcast_to(block_ids, (owners, SEL)), "ctx", split_axis=0, concat_axis=0, tiled=True
    )
    phases = split_phases(capacity // 2)
    packed = pack(lists, latent_cache.T, capacity, phases[0])
    table, *biases = plan(block_ids[0], owners, capacity, shift, phases)
    steps = partners(owners) + [(owners - 1, owners - 1)]

    def send(own):
        got = []
        for x, ks in zip(own, steps):
            moves = [(2 * c + h, 2 * (c ^ k) + h) for c in range(owners) for h, k in enumerate(ks)]
            got.append(lax.ppermute(x, ("ctx", "head"), moves))
        return got

    def swap(got):
        return [lax.ppermute(x, "head", [(0, 1), (1, 0)]) for x in got]

    q = queries.reshape(rows, lat)
    got = send(packed)
    if len(phases) == 1:
        (own,) = pack(lists, latent_cache.T, capacity, [], spread=phases[0])
        arrays = [*got, own, *swap(got)]
        state = attend(table, positions, q, biases[0], [], arrays, owners, capacity, "only", len(phases[0]))
        return state[0].reshape(q_rows, heads, KVL)
    *own, more = pack(lists, latent_cache.T, capacity, phases[1], spread=phases[0])
    got[-1], more = lax.optimization_barrier((got[-1], more))
    swapped = swap(got)
    *got, more, table = lax.optimization_barrier((*got, more, table))
    late = lax.all_to_all(more, "ctx", split_axis=0, concat_axis=0, tiled=True)
    arrays = [*got, *own, *swapped]
    carry, logs = attend(table, positions, q, biases[0], [], arrays, owners, capacity, "first", len(phases[0]))
    late, logs = lax.optimization_barrier((late, logs))
    arrays = [late, *swap([late])]
    state = attend(table, positions, q, biases[1], [carry, logs], arrays, owners, capacity, "last", len(phases[1]))
    return state[0].reshape(q_rows, heads, KVL)


def solution(mesh):
    return jax.shard_map(
        local,
        mesh=mesh,
        in_specs=(
            P(("groups", "ctx"), "head", None),
            P(("groups", "ctx"), None),
            P(("groups", "ctx")),
            P(("groups", "ctx"), None),
        ),
        out_specs=P(("groups", "ctx"), "head", None),
        check_vma=False,
    )
```

```python
import functools

import jax
import jax.numpy as jnp
from jax import lax
from jax.experimental import pallas as pl
from jax.experimental.pallas import tpu as pltpu
from jax.sharding import PartitionSpec as P

KVL = 512
BLOCK = 64
SEL = 32
PAIR = 2 * BLOCK
GROUP = 2 * PAIR
VMEM = 60 << 20
NEG = -1e30
SCALE = 1.4426950408889634 / 192.0**0.5
NT = (((1,), (1,)), ((), ()))
NN = (((1,), (0,)), ((), ()))


def log2(n):
    shift = n.bit_length() - 1
    assert 1 << shift == n
    return shift


def partners(owners):
    count = (owners - 2) // 2
    low, high = range(1, count + 1), range(count + 1, 2 * count + 1)
    return [(a, b) if i % 2 == 0 else (b, a) for i, (a, b) in enumerate(zip(low, high))]


def pack_kernel(capacity, chunks, spread, ids, cache, *refs):
    dests = ids.shape[0]
    pairs = partners(dests)
    outs, (table, rows, sem) = refs[:-3], refs[-3:]
    lat, tokens = rows.shape
    half = lat // 2
    shift = log2(tokens // BLOCK)
    head = lax.axis_index("head")
    me = lax.axis_index("ctx")
    copy = pltpu.make_async_copy(cache, rows, sem)
    copy.start()
    for k in range(dests):
        at = jnp.int32(k * (capacity + 1))
        for slot in range(capacity + 1):
            table[k * (capacity + 1) + slot] = 0
        for j in range(SEL):
            block = ids[k if spread else me ^ k, j]
            table[at] = block & ((1 << shift) - 1)
            at = at + (block >> shift == me).astype(jnp.int32)
        table[at] = 0

    def block_pair(k, chunk, start, size):
        first = k * (capacity + 1) + 2 * chunk
        a, b = table[first], table[first + 1]
        left = lax.broadcasted_iota(jnp.int32, (size, PAIR), 1) < BLOCK
        xa = rows[pl.ds(start, size), pl.ds(pl.multiple_of((a >> 1) * PAIR, PAIR), PAIR)]
        xb = rows[pl.ds(start, size), pl.ds(pl.multiple_of((b >> 1) * PAIR, PAIR), PAIR)]
        xa = jnp.where((a & 1) == 0, xa, pltpu.roll(xa, BLOCK, 1))
        xb = jnp.where((b & 1) == 1, xb, pltpu.roll(xb, BLOCK, 1))
        return jnp.where(left, xa, xb)

    copy.wait()
    if spread:
        for c, chunk in enumerate(spread):
            outs[0][c] = block_pair(me, chunk, 0, lat)
        for c, chunk in enumerate(chunks):
            for d in range(dests):
                outs[1][d, c] = block_pair(d, chunk, pl.multiple_of(head * half, 32), half)
        return
    for c, chunk in enumerate(chunks):
        for j, (a, b) in enumerate(pairs):
            outs[j][c] = block_pair(jnp.where(head == 0, a, b), chunk, 0, lat)
        outs[-1][c] = block_pair(dests - 1, chunk, pl.multiple_of(head * half, 32), half)


def pack(ids, cache_t, capacity, chunks, spread=None):
    dests = ids.shape[0]
    lat, tokens = cache_t.shape
    sizes = [lat] * len(partners(dests)) + [lat // 2]
    shapes = [(len(chunks), size, PAIR) for size in sizes]
    if spread:
        shapes = [(len(spread), lat, PAIR)] + ([(dests, len(chunks), lat // 2, PAIR)] if chunks else [])

    packed = pl.pallas_call(
        functools.partial(pack_kernel, capacity, chunks, spread),
        out_shape=[jax.ShapeDtypeStruct(s, jnp.bfloat16) for s in shapes],
        grid_spec=pltpu.PrefetchScalarGridSpec(
            num_scalar_prefetch=1,
            grid=(1,),
            in_specs=[pl.BlockSpec(memory_space=pl.ANY)],
            out_specs=[pl.BlockSpec(s, lambda i, *_, n=len(s): (0,) * n) for s in shapes],
            scratch_shapes=[
                pltpu.SMEM((dests * (capacity + 1),), jnp.int32),
                pltpu.VMEM((lat, tokens), jnp.bfloat16),
                pltpu.SemaphoreType.DMA,
            ],
        ),
        compiler_params=pltpu.CompilerParams(vmem_limit_bytes=24 << 20 if spread else VMEM),
        cost_estimate=pl.CostEstimate(flops=0, bytes_accessed=8 * lat * tokens, transcendentals=0),
        name="pack",
    )(ids, cache_t)
    return list(packed)


def pair_bias(bias, at, start_a, start_b):
    lane = lax.broadcasted_iota(jnp.int32, (8, PAIR), 1)
    start = jnp.where(lane < BLOCK, start_a, start_b)
    bias[:, pl.ds(at, PAIR)] = jnp.where(start >= 0, 0.0, NEG).astype(jnp.float32)


def pair_places(owners, phase, first):
    return {
        (c, o): i
        for i, (c, o) in enumerate((c, o) for c in range(phase) for o in range(owners) if o < owners - 1 or first and c == 0)
    }


def plan_kernel(owners, capacity, shift, phases, ids, table, *rest):
    biases, count = rest[:-1], rest[-1]
    for slot in range(owners * capacity):
        table[slot] = -1
    for o in range(owners):
        count[o] = 0
    for j in range(SEL):
        block = ids[j]
        owner = block >> shift
        rank = count[owner]
        table[owner * capacity + rank] = block * BLOCK
        count[owner] = rank + 1
    for p, (bias, phase) in enumerate(zip(biases, phases)):
        last = p > 0 and p == len(phases) - 1
        if last:
            bias[...] = jnp.full(bias.shape, NEG, bias.dtype)
            live = jnp.int32(0)
        for (c, o), i in pair_places(owners, len(phase), p == 0).items():
            slot = o * capacity + 2 * phase[c]
            a, b = table[slot], table[slot + 1]
            if last:
                used = a >= 0
                table[owners * capacity + c * owners + o] = jnp.where(used, live, -1)
                pair_bias(bias, pl.multiple_of(live * PAIR, PAIR), a, b)
                live = live + used.astype(jnp.int32)
            else:
                pair_bias(bias, i * PAIR, a, b)
        if last:
            for c in range(len(phase)):
                table[owners * capacity + c * owners + owners - 1] = -1
            table[owners * capacity + len(phase) * owners] = live


def plan(ids, owners, capacity, shift, phases):
    shapes = [(8, len(pair_places(owners, len(phase), p == 0)) * PAIR) for p, phase in enumerate(phases)]
    if len(phases) > 1:
        shapes[-1] = (8, shapes[-1][1] + PAIR)
    entries = owners * capacity + len(phases[-1]) * owners + 1
    return pl.pallas_call(
        functools.partial(plan_kernel, owners, capacity, shift, phases),
        out_shape=[jax.ShapeDtypeStruct((entries,), jnp.int32)]
        + [jax.ShapeDtypeStruct(s, jnp.float32) for s in shapes],
        grid_spec=pltpu.PrefetchScalarGridSpec(
            num_scalar_prefetch=1,
            grid=(1,),
            in_specs=[],
            out_specs=[pl.BlockSpec(memory_space=pltpu.SMEM)] + [pl.BlockSpec(s, lambda i, ids: (0, 0)) for s in shapes],
            scratch_shapes=[pltpu.SMEM((owners,), jnp.int32)],
        ),
        cost_estimate=pl.CostEstimate(flops=0, bytes_accessed=1 << 20, transcendentals=0),
        name="plan",
    )(ids)


class Arrived:
    def __init__(self, owners, arrays):
        pairs = partners(owners)
        count = len(pairs)
        head, me = lax.axis_index("head"), lax.axis_index("ctx")
        if len(arrays) == 2:
            _, self.chunks, half, _ = arrays[0].shape
            starts = [pl.multiple_of(h * half, 32) for h in (head, 1 - head)]
            self.parts = [
                (o, [(x.at[o], start, half) for x, start in zip(arrays, starts)]) for o in range(owners)
            ]
            return
        got, shared, own = arrays[:count], arrays[count], arrays[count + 1]
        swapped, shared_other = arrays[count + 2 : 2 * count + 2], arrays[2 * count + 2]
        self.chunks, lat, _ = own.shape
        half = lat // 2
        self.parts = [(me, [(own, 0, lat)])]
        for (a, b), x, y in zip(pairs, got, swapped):
            self.parts.append((me ^ jnp.where(head == 0, a, b), [(x, 0, lat)]))
            self.parts.append((me ^ jnp.where(head == 0, b, a), [(y, 0, lat)]))
        split = [(x, pl.multiple_of(h * half, 32), half) for x, h in ((shared, head), (shared_other, 1 - head))]
        self.parts.append((me ^ (owners - 1), split))

    def place(self, chunk, part, kt, at):
        for x, start, size in self.parts[part][1]:
            kt[pl.ds(start, size), pl.ds(pl.multiple_of(at, PAIR), PAIR)] = x[chunk]


class Half:
    def __init__(self, base, q, kt, bias, scores, weights, tops, sums, keys, diagonal=None):
        self.base, self.q, self.kt, self.bias = base, q, kt, bias
        self.scores, self.weights, self.tops, self.sums = scores, weights, tops, sums
        self.keys, self.diagonal = keys, diagonal
        self.groups = -(-keys // GROUP)
        self.size = scores.shape[0]

    def score(self, group):
        at = group * GROUP
        end = min(at + GROUP, self.keys)
        part = lax.dot_general(
            self.q[pl.ds(self.base, self.size), :], self.kt[:, at:end], NN, preferred_element_type=jnp.float32
        )
        part = part + self.bias[0:1, at:end]
        columns = [part[:, c : c + PAIR] for c in range(0, end - at, PAIR)]
        if self.diagonal is not None:
            where, key, pos, first = self.diagonal
            if at <= where < end:
                seen = jnp.concatenate(
                    [
                        jnp.broadcast_to(key, (BLOCK, PAIR)) <= pos[first + self.base // BLOCK + s]
                        for s in range(self.size // BLOCK)
                    ],
                    axis=0,
                )
                index = (where - at) // PAIR
                columns[index] = jnp.where(seen, columns[index], NEG)
        high = columns[0]
        for i, column in enumerate(columns):
            self.scores[:, at + i * PAIR : at + (i + 1) * PAIR] = column
            high = jnp.maximum(high, column) if i else high
        self.tops[...] = high if group == 0 else jnp.maximum(self.tops[...], high)

    def settle(self, old=None):
        top = jnp.max(self.tops[...], axis=1, keepdims=True) * SCALE
        top = jnp.broadcast_to(top, (self.size, PAIR))
        self.tops[...] = top if old is None else jnp.maximum(top, old)

    def weigh(self, slab):
        rows = pl.ds(slab * BLOCK, BLOCK)
        top = self.tops[rows, :]
        total = jnp.zeros((BLOCK, PAIR), jnp.float32)
        for at in range(0, self.keys, PAIR):
            part = jnp.exp2(self.scores[rows, at : at + PAIR] * SCALE - top)
            total = total + part
            self.weights[rows, at : at + PAIR] = part.astype(jnp.bfloat16)
        self.sums[rows, :] = total

    def total(self):
        return jnp.broadcast_to(jnp.sum(self.sums[...], axis=1, keepdims=True), (self.size, PAIR))

    def combine(self, column):
        return lax.dot_general(
            self.weights[:, 0 : self.keys],
            self.kt[column : column + GROUP, 0 : self.keys],
            NT,
            preferred_element_type=jnp.float32,
        )


def run_halves(a, b, before, after, combine):
    slabs = a.size // BLOCK
    for g in range(a.groups):
        a.score(g)
    before(a)
    for i in range(max(a.groups, slabs)):
        if i < b.groups:
            b.score(i)
        if i < slabs:
            a.weigh(i)
    before(b)
    after(a)
    for i, column in enumerate(range(0, KVL, GROUP)):
        combine(a, column)
        for s in range(i * slabs // 2, (i + 1) * slabs // 2):
            b.weigh(s)
    after(b)
    for column in range(0, KVL, GROUP):
        combine(b, column)


SCRATCH = 9


def attend_kernel(owners, capacity, kind, levels, table, pos, q, bias, *refs):
    start, end = kind in ("first", "only"), kind in ("last", "only")
    if not start:
        carry, logs, *refs = refs
    outs = refs[len(refs) - SCRATCH - (1 if end else 2) : len(refs) - SCRATCH]
    kt, *work = refs[len(refs) - SCRATCH :]
    arrived = Arrived(owners, refs[: len(refs) - SCRATCH - len(outs)])
    chunks = arrived.chunks
    step = pl.program_id(0)
    sub = work[0].shape[0]
    index = owners * capacity
    needed = table[index + chunks * owners] if kind == "last" else None

    @pl.when(step == 0)
    def _():
        for c in range(chunks):
            for part, (owner, _) in enumerate(arrived.parts):
                if kind == "last":
                    at = table[index + c * owners + owner]
                    pl.when(at >= 0)(functools.partial(arrived.place, c, part, kt, at * PAIR))
                elif start and c == 0:
                    arrived.place(c, part, kt, owner * PAIR)
                else:
                    at = (c * (owners - 1) + owner + int(start)) * PAIR
                    pl.when(owner < owners - 1)(functools.partial(arrived.place, c, part, kt, at))
        if kind == "last":
            fill = jnp.int32(levels[-1])
            for level in reversed(levels[:-1]):
                fill = jnp.where(needed <= level, level, fill)

            @pl.loop(needed, fill)
            def _(i):
                kt[:, pl.ds(pl.multiple_of(i * PAIR, PAIR), PAIR)] = jnp.zeros((kt.shape[0], PAIR), kt.dtype)

    def attend(keys):
        diagonal = None
        if start:
            key = table[(owners - 1) * capacity] + lax.broadcasted_iota(jnp.int32, (1, PAIR), 1)
            diagonal = ((owners - 1) * PAIR, key, pos, step * (2 * sub // BLOCK))
        a = Half(0, q, kt, bias, *work[0::2], keys, diagonal)
        b = Half(sub, q, kt, bias, *work[1::2], keys, diagonal)

        def before(part):
            part.settle(None if start else logs[pl.ds(part.base, sub), :])

        def after(part):
            rows = pl.ds(part.base, sub)
            total = part.total()
            if not start:
                kept = jnp.exp2(logs[rows, :] - part.tops[...])
                total = total + kept
            inverse = 1.0 / total
            part.sums[...] = inverse
            if not end:
                outs[1][rows, :] = part.tops[...] + jnp.log2(total)
            if not start:
                part.tops[...] = kept * inverse

        def combine(part, column):
            summed = part.combine(column)
            rows = pl.ds(part.base, sub)
            for at in range(0, GROUP, PAIR):
                cols = slice(column + at, column + at + PAIR)
                result = summed[:, at : at + PAIR] * part.sums[...]
                if not start:
                    result = result + carry[rows, cols] * part.tops[...]
                outs[0][rows, cols] = result.astype(outs[0].dtype)

        run_halves(a, b, before, after, combine)

    if kind != "last":
        attend(kt.shape[1])
        return
    below = -1
    for level in levels:
        pl.when(jnp.logical_and(needed > below, needed <= level))(functools.partial(attend, level * PAIR))
        below = level


def attend(table, pos, q, bias, state, arrays, owners, capacity, kind, chunks):
    rows, lat = q.shape
    pairs = len(pair_places(owners, chunks, kind in ("first", "only")))
    keys = pairs * PAIR
    levels = [n for n in (4, 5, 6, 8) if n < pairs] + [pairs]
    sub = 512
    step = 2 * sub
    out_shape = [jax.ShapeDtypeStruct((rows, KVL), jnp.float32), jax.ShapeDtypeStruct((rows, PAIR), jnp.float32)]
    if kind in ("last", "only"):
        out_shape = [jax.ShapeDtypeStruct((rows, KVL), jnp.bfloat16)]

    def whole(x):
        return pl.BlockSpec(x.shape, lambda i, *_: (0,) * x.ndim)

    def row_block(x):
        return pl.BlockSpec((step, x.shape[1]), lambda i, *_: (i, 0))

    return pl.pallas_call(
        functools.partial(attend_kernel, owners, capacity, kind, levels),
        out_shape=out_shape,
        grid_spec=pltpu.PrefetchScalarGridSpec(
            num_scalar_prefetch=2,
            grid=(rows // step,),
            in_specs=[row_block(q), whole(bias)] + [row_block(x) for x in state] + [whole(x) for x in arrays],
            out_specs=[row_block(x) for x in out_shape],
            scratch_shapes=[
                pltpu.VMEM((lat, keys), jnp.bfloat16),
                *[pltpu.VMEM((sub, keys), jnp.float32)] * 2,
                *[pltpu.VMEM((sub, keys), jnp.bfloat16)] * 2,
                *[pltpu.VMEM((sub, PAIR), jnp.float32)] * 4,
            ],
        ),
        compiler_params=pltpu.CompilerParams(vmem_limit_bytes=VMEM if kind == "last" else min(VMEM, (18 << 20) + keys * 10240)),
        cost_estimate=pl.CostEstimate(
            flops=2 * rows * keys * (lat + KVL), bytes_accessed=rows * (lat + 2 * KVL) * 2, transcendentals=rows * keys
        ),
        name="attend_" + kind,
    )(table, pos, q, bias, *state, *arrays)


def split_phases(chunks):
    cut = (chunks + 1) // 2
    return [phase for phase in (list(range(cut)), list(range(cut, chunks))) if phase]


def local(queries, latent_cache, positions, block_ids):
    owners = lax.axis_size("ctx")
    capacity = max(2, 2 * SEL // owners)
    shift = log2(latent_cache.shape[0] // BLOCK)
    q_rows, heads, lat = queries.shape
    rows = q_rows * heads
    lists = lax.all_to_all(
        jnp.broadcast_to(block_ids, (owners, SEL)), "ctx", split_axis=0, concat_axis=0, tiled=True
    )
    phases = split_phases(capacity // 2)
    packed = pack(lists, latent_cache.T, capacity, phases[0])
    table, *biases = plan(block_ids[0], owners, capacity, shift, phases)
    steps = partners(owners) + [(owners - 1, owners - 1)]

    def send(own):
        got = []
        for x, ks in zip(own, steps):
            moves = [(2 * c + h, 2 * (c ^ k) + h) for c in range(owners) for h, k in enumerate(ks)]
            got.append(lax.ppermute(x, ("ctx", "head"), moves))
        return got

    def swap(got):
        return [lax.ppermute(x, "head", [(0, 1), (1, 0)]) for x in got]

    q = queries.reshape(rows, lat)
    got = send(packed)
    if len(phases) == 1:
        (own,) = pack(lists, latent_cache.T, capacity, [], spread=phases[0])
        arrays = [*got, own, *swap(got)]
        state = attend(table, positions, q, biases[0], [], arrays, owners, capacity, "only", len(phases[0]))
        return state[0].reshape(q_rows, heads, KVL)
    *own, more = pack(lists, latent_cache.T, capacity, phases[1], spread=phases[0])
    got[-1], more = lax.optimization_barrier((got[-1], more))
    swapped = swap(got)
    *got, more, table = lax.optimization_barrier((*got, more, table))
    late = lax.all_to_all(more, "ctx", split_axis=0, concat_axis=0, tiled=True)
    arrays = [*got, *own, *swapped]
    carry, logs = attend(table, positions, q, biases[0], [], arrays, owners, capacity, "first", len(phases[0]))
    late, logs = lax.optimization_barrier((late, logs))
    arrays = [late, *swap([late])]
    state = attend(table, positions, q, biases[1], [carry, logs], arrays, owners, capacity, "last", len(phases[1]))
    return state[0].reshape(q_rows, heads, KVL)


def solution(mesh):
    return jax.shard_map(
        local,
        mesh=mesh,
        in_specs=(
            P(("groups", "ctx"), "head", None),
            P(("groups", "ctx"), None),
            P(("groups", "ctx")),
            P(("groups", "ctx"), None),
        ),
        out_specs=P(("groups", "ctx"), "head", None),
        check_vma=False,
    )
```

```python
import functools

import jax
import jax.numpy as jnp
from jax import lax
from jax.experimental import pallas as pl
from jax.experimental.pallas import tpu as pltpu
from jax.sharding import PartitionSpec as P

KVL = 512
BLOCK = 64
SEL = 32
PAIR = 2 * BLOCK
GROUP = 2 * PAIR
VMEM = 60 << 20
NEG = -1e30
SCALE = 1.4426950408889634 / 192.0**0.5
NT = (((1,), (1,)), ((), ()))
NN = (((1,), (0,)), ((), ()))


def log2(n):
    shift = n.bit_length() - 1
    assert 1 << shift == n
    return shift


def partners(owners):
    count = (owners - 2) // 2
    low, high = range(1, count + 1), range(count + 1, 2 * count + 1)
    return [(a, b) if i % 2 == 0 else (b, a) for i, (a, b) in enumerate(zip(low, high))]


def pack_kernel(capacity, chunks, spread, ids, cache, *refs):
    dests = ids.shape[0]
    pairs = partners(dests)
    outs, (table, rows, sem) = refs[:-3], refs[-3:]
    lat, tokens = rows.shape
    half = lat // 2
    shift = log2(tokens // BLOCK)
    head = lax.axis_index("head")
    me = lax.axis_index("ctx")
    copy = pltpu.make_async_copy(cache, rows, sem)
    copy.start()
    for k in range(dests):
        at = jnp.int32(k * (capacity + 1))
        for slot in range(capacity + 1):
            table[k * (capacity + 1) + slot] = 0
        for j in range(SEL):
            block = ids[k if spread else me ^ k, j]
            table[at] = block & ((1 << shift) - 1)
            at = at + (block >> shift == me).astype(jnp.int32)
        table[at] = 0

    def block_pair(k, chunk, start, size):
        first = k * (capacity + 1) + 2 * chunk
        a, b = table[first], table[first + 1]
        left = lax.broadcasted_iota(jnp.int32, (size, PAIR), 1) < BLOCK
        xa = rows[pl.ds(start, size), pl.ds(pl.multiple_of((a >> 1) * PAIR, PAIR), PAIR)]
        xb = rows[pl.ds(start, size), pl.ds(pl.multiple_of((b >> 1) * PAIR, PAIR), PAIR)]
        xa = jnp.where((a & 1) == 0, xa, pltpu.roll(xa, BLOCK, 1))
        xb = jnp.where((b & 1) == 1, xb, pltpu.roll(xb, BLOCK, 1))
        return jnp.where(left, xa, xb)

    copy.wait()
    if spread:
        for c, chunk in enumerate(spread):
            outs[0][c] = block_pair(me, chunk, 0, lat)
        for c, chunk in enumerate(chunks):
            for d in range(dests):
                outs[1][d, c] = block_pair(d, chunk, pl.multiple_of(head * half, 32), half)
        return
    for c, chunk in enumerate(chunks):
        for j, (a, b) in enumerate(pairs):
            outs[j][c] = block_pair(jnp.where(head == 0, a, b), chunk, 0, lat)
        outs[-1][c] = block_pair(dests - 1, chunk, pl.multiple_of(head * half, 32), half)


def pack(ids, cache_t, capacity, chunks, spread=None):
    dests = ids.shape[0]
    lat, tokens = cache_t.shape
    sizes = [lat] * len(partners(dests)) + [lat // 2]
    shapes = [(len(chunks), size, PAIR) for size in sizes]
    if spread:
        shapes = [(len(spread), lat, PAIR)] + ([(dests, len(chunks), lat // 2, PAIR)] if chunks else [])

    packed = pl.pallas_call(
        functools.partial(pack_kernel, capacity, chunks, spread),
        out_shape=[jax.ShapeDtypeStruct(s, jnp.bfloat16) for s in shapes],
        grid_spec=pltpu.PrefetchScalarGridSpec(
            num_scalar_prefetch=1,
            grid=(1,),
            in_specs=[pl.BlockSpec(memory_space=pl.ANY)],
            out_specs=[pl.BlockSpec(s, lambda i, *_, n=len(s): (0,) * n) for s in shapes],
            scratch_shapes=[
                pltpu.SMEM((dests * (capacity + 1),), jnp.int32),
                pltpu.VMEM((lat, tokens), jnp.bfloat16),
                pltpu.SemaphoreType.DMA,
            ],
        ),
        compiler_params=pltpu.CompilerParams(vmem_limit_bytes=VMEM),
        cost_estimate=pl.CostEstimate(flops=0, bytes_accessed=8 * lat * tokens, transcendentals=0),
        name="pack",
    )(ids, cache_t)
    return list(packed)


def pair_bias(bias, at, start_a, start_b):
    lane = lax.broadcasted_iota(jnp.int32, (8, PAIR), 1)
    start = jnp.where(lane < BLOCK, start_a, start_b)
    bias[:, pl.ds(at, PAIR)] = jnp.where(start >= 0, 0.0, NEG).astype(jnp.float32)


def pair_places(owners, phase, first):
    return {
        (c, o): i
        for i, (c, o) in enumerate((c, o) for c in range(phase) for o in range(owners) if o < owners - 1 or first and c == 0)
    }


def plan_kernel(owners, capacity, shift, phases, ids, table, *rest):
    biases, count = rest[:-1], rest[-1]
    for slot in range(owners * capacity):
        table[slot] = -1
    for o in range(owners):
        count[o] = 0
    for j in range(SEL):
        block = ids[j]
        owner = block >> shift
        rank = count[owner]
        table[owner * capacity + rank] = block * BLOCK
        count[owner] = rank + 1
    for p, (bias, phase) in enumerate(zip(biases, phases)):
        last = p > 0 and p == len(phases) - 1
        if last:
            bias[...] = jnp.full(bias.shape, NEG, bias.dtype)
            live = jnp.int32(0)
        for (c, o), i in pair_places(owners, len(phase), p == 0).items():
            slot = o * capacity + 2 * phase[c]
            a, b = table[slot], table[slot + 1]
            if last:
                used = a >= 0
                table[owners * capacity + c * owners + o] = jnp.where(used, live, -1)
                pair_bias(bias, pl.multiple_of(live * PAIR, PAIR), a, b)
                live = live + used.astype(jnp.int32)
            else:
                pair_bias(bias, i * PAIR, a, b)
        if last:
            for c in range(len(phase)):
                table[owners * capacity + c * owners + owners - 1] = -1
            table[owners * capacity + len(phase) * owners] = live


def plan(ids, owners, capacity, shift, phases):
    shapes = [(8, len(pair_places(owners, len(phase), p == 0)) * PAIR) for p, phase in enumerate(phases)]
    if len(phases) > 1:
        shapes[-1] = (8, shapes[-1][1] + PAIR)
    entries = owners * capacity + len(phases[-1]) * owners + 1
    return pl.pallas_call(
        functools.partial(plan_kernel, owners, capacity, shift, phases),
        out_shape=[jax.ShapeDtypeStruct((entries,), jnp.int32)]
        + [jax.ShapeDtypeStruct(s, jnp.float32) for s in shapes],
        grid_spec=pltpu.PrefetchScalarGridSpec(
            num_scalar_prefetch=1,
            grid=(1,),
            in_specs=[],
            out_specs=[pl.BlockSpec(memory_space=pltpu.SMEM)] + [pl.BlockSpec(s, lambda i, ids: (0, 0)) for s in shapes],
            scratch_shapes=[pltpu.SMEM((owners,), jnp.int32)],
        ),
        cost_estimate=pl.CostEstimate(flops=0, bytes_accessed=1 << 20, transcendentals=0),
        name="plan",
    )(ids)


class Arrived:
    def __init__(self, owners, arrays):
        pairs = partners(owners)
        count = len(pairs)
        head, me = lax.axis_index("head"), lax.axis_index("ctx")
        if len(arrays) == 2:
            _, self.chunks, half, _ = arrays[0].shape
            starts = [pl.multiple_of(h * half, 32) for h in (head, 1 - head)]
            self.parts = [
                (o, [(x.at[o], start, half) for x, start in zip(arrays, starts)]) for o in range(owners)
            ]
            return
        got, shared, own = arrays[:count], arrays[count], arrays[count + 1]
        swapped, shared_other = arrays[count + 2 : 2 * count + 2], arrays[2 * count + 2]
        self.chunks, lat, _ = own.shape
        half = lat // 2
        self.parts = [(me, [(own, 0, lat)])]
        for (a, b), x, y in zip(pairs, got, swapped):
            self.parts.append((me ^ jnp.where(head == 0, a, b), [(x, 0, lat)]))
            self.parts.append((me ^ jnp.where(head == 0, b, a), [(y, 0, lat)]))
        split = [(x, pl.multiple_of(h * half, 32), half) for x, h in ((shared, head), (shared_other, 1 - head))]
        self.parts.append((me ^ (owners - 1), split))

    def place(self, chunk, part, kt, at):
        for x, start, size in self.parts[part][1]:
            kt[pl.ds(start, size), pl.ds(pl.multiple_of(at, PAIR), PAIR)] = x[chunk]


class Half:
    def __init__(self, base, q, kt, bias, scores, weights, tops, sums, keys, diagonal=None):
        self.base, self.q, self.kt, self.bias = base, q, kt, bias
        self.scores, self.weights, self.tops, self.sums = scores, weights, tops, sums
        self.keys, self.diagonal = keys, diagonal
        self.groups = -(-keys // GROUP)
        self.size = scores.shape[0]

    def score(self, group):
        at = group * GROUP
        end = min(at + GROUP, self.keys)
        part = lax.dot_general(
            self.q[pl.ds(self.base, self.size), :], self.kt[:, at:end], NN, preferred_element_type=jnp.float32
        )
        part = part + self.bias[0:1, at:end]
        columns = [part[:, c : c + PAIR] for c in range(0, end - at, PAIR)]
        if self.diagonal is not None:
            where, key, pos, first = self.diagonal
            if at <= where < end:
                seen = jnp.concatenate(
                    [
                        jnp.broadcast_to(key, (BLOCK, PAIR)) <= pos[first + self.base // BLOCK + s]
                        for s in range(self.size // BLOCK)
                    ],
                    axis=0,
                )
                index = (where - at) // PAIR
                columns[index] = jnp.where(seen, columns[index], NEG)
        high = columns[0]
        for i, column in enumerate(columns):
            self.scores[:, at + i * PAIR : at + (i + 1) * PAIR] = column
            high = jnp.maximum(high, column) if i else high
        self.tops[...] = high if group == 0 else jnp.maximum(self.tops[...], high)

    def settle(self, old=None):
        top = jnp.max(self.tops[...], axis=1, keepdims=True) * SCALE
        top = jnp.broadcast_to(top, (self.size, PAIR))
        self.tops[...] = top if old is None else jnp.maximum(top, old)

    def weigh(self, slab):
        rows = pl.ds(slab * BLOCK, BLOCK)
        top = self.tops[rows, :]
        total = jnp.zeros((BLOCK, PAIR), jnp.float32)
        for at in range(0, self.keys, PAIR):
            part = jnp.exp2(self.scores[rows, at : at + PAIR] * SCALE - top)
            total = total + part
            self.weights[rows, at : at + PAIR] = part.astype(jnp.bfloat16)
        self.sums[rows, :] = total

    def total(self):
        return jnp.broadcast_to(jnp.sum(self.sums[...], axis=1, keepdims=True), (self.size, PAIR))

    def combine(self, column):
        return lax.dot_general(
            self.weights[:, 0 : self.keys],
            self.kt[column : column + GROUP, 0 : self.keys],
            NT,
            preferred_element_type=jnp.float32,
        )


def run_halves(a, b, before, after, combine):
    slabs = a.size // BLOCK
    for g in range(a.groups):
        a.score(g)
    before(a)
    for i in range(max(a.groups, slabs)):
        if i < b.groups:
            b.score(i)
        if i < slabs:
            a.weigh(i)
    before(b)
    after(a)
    for i, column in enumerate(range(0, KVL, GROUP)):
        combine(a, column)
        for s in range(i * slabs // 2, (i + 1) * slabs // 2):
            b.weigh(s)
    after(b)
    for column in range(0, KVL, GROUP):
        combine(b, column)


SCRATCH = 9


def attend_kernel(owners, capacity, kind, levels, table, pos, q, bias, *refs):
    start, end = kind in ("first", "only"), kind in ("last", "only")
    if not start:
        carry, logs, *refs = refs
    outs = refs[len(refs) - SCRATCH - (1 if end else 2) : len(refs) - SCRATCH]
    kt, *work = refs[len(refs) - SCRATCH :]
    arrived = Arrived(owners, refs[: len(refs) - SCRATCH - len(outs)])
    chunks = arrived.chunks
    step = pl.program_id(0)
    sub = work[0].shape[0]
    index = owners * capacity
    needed = table[index + chunks * owners] if kind == "last" else None

    @pl.when(step == 0)
    def _():
        for c in range(chunks):
            for part, (owner, _) in enumerate(arrived.parts):
                if kind == "last":
                    at = table[index + c * owners + owner]
                    pl.when(at >= 0)(functools.partial(arrived.place, c, part, kt, at * PAIR))
                elif start and c == 0:
                    arrived.place(c, part, kt, owner * PAIR)
                else:
                    at = (c * (owners - 1) + owner + int(start)) * PAIR
                    pl.when(owner < owners - 1)(functools.partial(arrived.place, c, part, kt, at))
        if kind == "last":
            fill = jnp.int32(levels[-1])
            for level in reversed(levels[:-1]):
                fill = jnp.where(needed <= level, level, fill)

            @pl.loop(needed, fill)
            def _(i):
                kt[:, pl.ds(pl.multiple_of(i * PAIR, PAIR), PAIR)] = jnp.zeros((kt.shape[0], PAIR), kt.dtype)

    def attend(keys):
        diagonal = None
        if start:
            key = table[(owners - 1) * capacity] + lax.broadcasted_iota(jnp.int32, (1, PAIR), 1)
            diagonal = ((owners - 1) * PAIR, key, pos, step * (2 * sub // BLOCK))
        a = Half(0, q, kt, bias, *work[0::2], keys, diagonal)
        b = Half(sub, q, kt, bias, *work[1::2], keys, diagonal)

        def before(part):
            part.settle(None if start else logs[pl.ds(part.base, sub), :])

        def after(part):
            rows = pl.ds(part.base, sub)
            total = part.total()
            if not start:
                kept = jnp.exp2(logs[rows, :] - part.tops[...])
                total = total + kept
            inverse = 1.0 / total
            part.sums[...] = inverse
            if not end:
                outs[1][rows, :] = part.tops[...] + jnp.log2(total)
            if not start:
                part.tops[...] = kept * inverse

        def combine(part, column):
            summed = part.combine(column)
            rows = pl.ds(part.base, sub)
            for at in range(0, GROUP, PAIR):
                cols = slice(column + at, column + at + PAIR)
                result = summed[:, at : at + PAIR] * part.sums[...]
                if not start:
                    result = result + carry[rows, cols] * part.tops[...]
                outs[0][rows, cols] = result.astype(outs[0].dtype)

        run_halves(a, b, before, after, combine)

    if kind != "last":
        attend(kt.shape[1])
        return
    below = -1
    for level in levels:
        pl.when(jnp.logical_and(needed > below, needed <= level))(functools.partial(attend, level * PAIR))
        below = level


def attend(table, pos, q, bias, state, arrays, owners, capacity, kind, chunks):
    rows, lat = q.shape
    pairs = len(pair_places(owners, chunks, kind in ("first", "only")))
    keys = pairs * PAIR
    levels = [n for n in (4, 5, 6, 8) if n < pairs] + [pairs]
    sub = 512
    step = 2 * sub
    out_shape = [jax.ShapeDtypeStruct((rows, KVL), jnp.float32), jax.ShapeDtypeStruct((rows, PAIR), jnp.float32)]
    if kind in ("last", "only"):
        out_shape = [jax.ShapeDtypeStruct((rows, KVL), jnp.bfloat16)]

    def whole(x):
        return pl.BlockSpec(x.shape, lambda i, *_: (0,) * x.ndim)

    def row_block(x):
        return pl.BlockSpec((step, x.shape[1]), lambda i, *_: (i, 0))

    return pl.pallas_call(
        functools.partial(attend_kernel, owners, capacity, kind, levels),
        out_shape=out_shape,
        grid_spec=pltpu.PrefetchScalarGridSpec(
            num_scalar_prefetch=2,
            grid=(rows // step,),
            in_specs=[row_block(q), whole(bias)] + [row_block(x) for x in state] + [whole(x) for x in arrays],
            out_specs=[row_block(x) for x in out_shape],
            scratch_shapes=[
                pltpu.VMEM((lat, keys), jnp.bfloat16),
                *[pltpu.VMEM((sub, keys), jnp.float32)] * 2,
                *[pltpu.VMEM((sub, keys), jnp.bfloat16)] * 2,
                *[pltpu.VMEM((sub, PAIR), jnp.float32)] * 4,
            ],
        ),
        compiler_params=pltpu.CompilerParams(vmem_limit_bytes=VMEM),
        cost_estimate=pl.CostEstimate(
            flops=2 * rows * keys * (lat + KVL), bytes_accessed=rows * (lat + 2 * KVL) * 2, transcendentals=rows * keys
        ),
        name="attend_" + kind,
    )(table, pos, q, bias, *state, *arrays)


def split_phases(chunks):
    cut = (chunks + 1) // 2
    return [phase for phase in (list(range(cut)), list(range(cut, chunks))) if phase]


def local(queries, latent_cache, positions, block_ids):
    owners = lax.axis_size("ctx")
    capacity = max(2, 2 * SEL // owners)
    shift = log2(latent_cache.shape[0] // BLOCK)
    q_rows, heads, lat = queries.shape
    rows = q_rows * heads
    lists = lax.all_to_all(
        jnp.broadcast_to(block_ids, (owners, SEL)), "ctx", split_axis=0, concat_axis=0, tiled=True
    )
    phases = split_phases(capacity // 2)
    packed = pack(lists, latent_cache.T, capacity, phases[0])
    table, *biases = plan(block_ids[0], owners, capacity, shift, phases)
    steps = partners(owners) + [(owners - 1, owners - 1)]

    def send(own):
        got = []
        for x, ks in zip(own, steps):
            moves = [(2 * c + h, 2 * (c ^ k) + h) for c in range(owners) for h, k in enumerate(ks)]
            got.append(lax.ppermute(x, ("ctx", "head"), moves))
        return got

    def swap(got):
        return [lax.ppermute(x, "head", [(0, 1), (1, 0)]) for x in got]

    q = queries.reshape(rows, lat)
    got = send(packed)
    if len(phases) == 1:
        (own,) = pack(lists, latent_cache.T, capacity, [], spread=phases[0])
        arrays = [*got, own, *swap(got)]
        state = attend(table, positions, q, biases[0], [], arrays, owners, capacity, "only", len(phases[0]))
        return state[0].reshape(q_rows, heads, KVL)
    *own, more = pack(lists, latent_cache.T, capacity, phases[1], spread=phases[0])
    got[-1], more = lax.optimization_barrier((got[-1], more))
    swapped = swap(got)
    *got, more, table = lax.optimization_barrier((*got, more, table))
    late = lax.all_to_all(more, "ctx", split_axis=0, concat_axis=0, tiled=True)
    arrays = [*got, *own, *swapped]
    carry, logs = attend(table, positions, q, biases[0], [], arrays, owners, capacity, "first", len(phases[0]))
    late, logs = lax.optimization_barrier((late, logs))
    arrays = [late, *swap([late])]
    state = attend(table, positions, q, biases[1], [carry, logs], arrays, owners, capacity, "last", len(phases[1]))
    return state[0].reshape(q_rows, heads, KVL)


def solution(mesh):
    return jax.shard_map(
        local,
        mesh=mesh,
        in_specs=(
            P(("groups", "ctx"), "head", None),
            P(("groups", "ctx"), None),
            P(("groups", "ctx")),
            P(("groups", "ctx"), None),
        ),
        out_specs=P(("groups", "ctx"), "head", None),
        check_vma=False,
    )
```
